32 devices in a mesh: ctx: 16 (over z, y, core), fsdp: 2 (over x).
Axes of the slice: x: 2, y: 2, z: 4, core: 2. Of those that a mesh axis runs over, the one named last changes fastest.
Arguments:
- tokens: bfloat16 [2, 2048, 768], P('fsdp', 'ctx'), may hold values from -6 to 6
- prev_logits: float32 [2, 2048, 12], P('fsdp', 'ctx'), may hold values from -3 to 3
- routes: int32 [2, 2048, 2], P('fsdp', 'ctx'), may hold values from 0 to 11, all different within a row
- order: int32 [2, 4096], P('fsdp', 'ctx'), may hold values from 0 to 255, as said below
- deal: int32 [32], replicated, may hold values from 0 to 31, each once
- w_qkv: bfloat16 [2, 768, 2304], P(None, ('ctx', 'fsdp')), may hold values from -0.21875 to 0.21875
- w_out: bfloat16 [2, 768, 768], P(None, ('ctx', 'fsdp')), may hold values from -0.625 to 0.625
- w_gate: bfloat16 [2, 8, 768, 2048], P(None, None, ('ctx', 'fsdp')), may hold values from -0.21875 to 0.21875
- w_up: bfloat16 [2, 8, 768, 2048], P(None, None, ('ctx', 'fsdp')), may hold values from -0.21875 to 0.21875
- w_down: bfloat16 [2, 8, 2048, 768], P(None, None, ('ctx', 'fsdp')), may hold values from -0.25 to 0.25
- norm_attn: bfloat16 [2, 768], P(None, ('ctx', 'fsdp')), may hold values from 0.5 to 1.5
- norm_moe: bfloat16 [2, 768], P(None, ('ctx', 'fsdp')), may hold values from 0.5 to 1.5
- w_router: bfloat16 [2, 768, 12], P(None, ('ctx', 'fsdp')), may hold values from -0.125 to 0.125
- w_const: bfloat16 [2, 768, 4], P(None, ('ctx', 'fsdp')), may hold values from -0.21875 to 0.21875
- const_vec: bfloat16 [2, 768, 2], P(None, ('ctx', 'fsdp')), may hold values from -5 to 5
- grad_out: bfloat16 [2, 2048, 768], P('fsdp', 'ctx'), may hold values from -6 to 6
Outputs:
- output_rows: bfloat16 [2, 2048, 768], P('fsdp', 'ctx')
- input_grad: float32 [2, 2048, 768], P('fsdp', 'ctx')
- qkv_grad: float32 [2, 768, 2304], P(None, ('ctx', 'fsdp'))
- out_grad: float32 [2, 768, 768], P(None, ('ctx', 'fsdp'))
- gate_grad: float32 [2, 8, 768, 2048], P(None, None, ('ctx', 'fsdp'))
- up_grad: float32 [2, 8, 768, 2048], P(None, None, ('ctx', 'fsdp'))
- down_grad: float32 [2, 8, 2048, 768], P(None, None, ('ctx', 'fsdp'))
- norm_attn_grad: float32 [2, 768], P(None, ('ctx', 'fsdp'))
- norm_moe_grad: float32 [2, 768], P(None, ('ctx', 'fsdp'))
- router_grad: float32 [2, 768, 12], P(None, ('ctx', 'fsdp'))
- const_gate_grad: float32 [2, 768, 4], P(None, ('ctx', 'fsdp'))
- const_vec_grad: float32 [2, 768, 2], P(None, ('ctx', 'fsdp'))
The draws below stay inside these ranges and needn't reach their ends.
Inputs may be any that keep to these rules, and one draw needn't show every extreme that they name: Each token names 2 different routes: 0 to 7 feed-forward experts, 8 the zero expert, 9 the copy expert, 10 and 11 the constant experts. `order`: each aligned block of 256 entries (one device's pairs) is a permutation of 0 to 255. `deal`: a permutation, the same for every group.
All inputs are finite; a program needn't handle non-finite values.
Results may differ from the reference program's by a relative error of at most 0.023.
Values may be sent and summed in bfloat16 or wider, within the bound.
No kernel may reach another device: no remote copies, remote signals or barrier semaphores. Data moves between devices by JAX's collectives and lax.ppermute only.
A program may use at most 576 MiB of HBM per device.

```python
import jax
import jax.numpy as jnp
from jax import lax

D = 768
HEADS = 12
HEAD_DIM = 64
FF = 2048
EXPERTS = 8
TOP = 2
LAYERS = 2
TOK_DEV = 128
ROUTED = 12
GROUPS = 2
GROUP = 2048
PROMPT = 1024
CONT = 512
NBLK = 32
CAP = 26
N_CTX = 16


def draw_order(key, part):
    key = jax.random.fold_in(key, 7)
    key_list = jax.random.split(key, GROUPS * N_CTX)

    def shuffle_one(single):
        return jax.random.permutation(single, TOP * TOK_DEV)
    shuffled = jax.vmap(shuffle_one)(key_list)
    return shuffled.reshape(GROUPS, GROUP * TOP).astype(jnp.int32)


def shard_levels(stream_key, shape, cuts, smallest, largest):
    factor_of = 1.0
    for position, parts in cuts:
        steps = jax.random.uniform(jax.random.fold_in(jax.random.fold_in(stream_key, 6), position), (parts,), jnp.float32, smallest / len(cuts), largest / len(cuts))
        factor_of = factor_of * jnp.repeat(jnp.exp(steps), shape[position] // parts).reshape((-1,) + (1,) * (len(shape) - 1 - position))
    return factor_of


def different_ones(rng, rows, count, top, lift):
    order = jax.random.permutation(jax.random.fold_in(rng, 1), count)
    boost = order
    for power in range(3):
        boost = boost * boost // count
    boost = boost * lift // count
    lots = jax.random.randint(jax.random.fold_in(rng, 2), (rows, count), 0, 4096) + boost
    sure = jax.random.permutation(jax.random.fold_in(rng, 3), rows)[jnp.arange(count) % rows]
    lots = jnp.where(jnp.arange(rows)[:, None] == sure[None, :], 1 << 14, lots)
    score = lots * count + jnp.arange(count)
    return lax.top_k(score.astype(jnp.int32), top)[1].astype(jnp.int32)


def bell_draw(own_key, dims, deviation, limit, shards=(), held_as=jnp.bfloat16):
    loudness = shard_levels(own_key, dims, shards, -0.22, 0.18) if shards else 1.0
    entries = jax.random.normal(own_key, dims, jnp.float32) * deviation * loudness
    return jnp.minimum(jnp.maximum(entries, -limit), limit).astype(held_as)


def setup_inputs(seed: int = 0) -> dict:
    streams_of = jax.random.split(jax.random.key(seed), 17)
    tokens = bell_draw(streams_of[0], (GROUPS, GROUP, D), 1.0, 6.0, ((0, 2), (1, 16)))
    prev_logits = bell_draw(streams_of[1], (GROUPS, GROUP, ROUTED), 0.5, 3.0, ((0, 2), (1, 16)), jnp.float32)
    routes = different_ones(streams_of[2], GROUPS * GROUP, ROUTED, TOP, 1365).reshape((GROUPS, GROUP, TOP))
    order = draw_order(jax.random.fold_in(streams_of[16], 71), 0)
    deal = jax.random.permutation(streams_of[4], NBLK).astype(jnp.int32)
    w_qkv = bell_draw(streams_of[5], (LAYERS, D, 3 * D), D ** -0.5, 0.21875, ((1, 32),))
    w_out = bell_draw(streams_of[6], (LAYERS, D, D), (D // 8) ** -0.5, 0.625, ((1, 32),))
    w_gate = bell_draw(streams_of[7], (LAYERS, EXPERTS, D, FF), D ** -0.5, 0.21875, ((2, 32),))
    w_up = bell_draw(streams_of[8], (LAYERS, EXPERTS, D, FF), D ** -0.5, 0.21875, ((2, 32),))
    w_down = bell_draw(streams_of[9], (LAYERS, EXPERTS, FF, D), (FF // 4) ** -0.5, 0.25, ((2, 32),))
    norm_attn = jnp.clip(1.0 + 0.1 * jax.random.normal(streams_of[10], (LAYERS, D), jnp.float32), 0.5, 1.5).astype(jnp.bfloat16)
    norm_moe = jnp.clip(1.0 + 0.1 * jax.random.normal(streams_of[11], (LAYERS, D), jnp.float32), 0.5, 1.5).astype(jnp.bfloat16)
    w_router = bell_draw(streams_of[12], (LAYERS, D, ROUTED), (3 * D) ** -0.5, 0.125, ((1, 32),))
    w_const = bell_draw(streams_of[13], (LAYERS, D, 4), D ** -0.5, 0.21875, ((1, 32),))
    const_vec = bell_draw(streams_of[14], (LAYERS, D, 2), 1.0, 5.0, ((1, 32),))
    grad_out = bell_draw(streams_of[15], (GROUPS, GROUP, D), 1.0, 6.0, ((0, 2), (1, 16)))
    return {"tokens": tokens, "prev_logits": prev_logits, "routes": routes, "order": order, "deal": deal, "w_qkv": w_qkv, "w_out": w_out, "w_gate": w_gate, "w_up": w_up, "w_down": w_down, "norm_attn": norm_attn, "norm_moe": norm_moe, "w_router": w_router, "w_const": w_const, "const_vec": const_vec, "grad_out": grad_out}


@jax.custom_vjp
def low(v):
    return lax.optimization_barrier(v.astype(jnp.bfloat16)).astype(jnp.float32)

@jax.custom_vjp
def low_back(v):
    return v

def low_keep(v):
    return (low(v), None)

def low_pass(kept, grad):
    return (grad,)

def back_keep(v):
    return (v, None)

def back_low(kept, grad):
    return (low(grad),)
low.defvjp(low_keep, low_pass)
low_back.defvjp(back_keep, back_low)
norm_eps = 1e-06
masked_score = -1e+30
highest = lax.Precision.HIGHEST

def rms_rows(values, gain):
    scale = lax.rsqrt(lax.optimization_barrier(jnp.mean(values * values, axis=-1, keepdims=True)) + norm_eps)
    return values * scale * gain

def rotate(heads_in, cosine_table, sine_table):
    half_dim = heads_in.shape[-1] // 2
    former = heads_in[..., :half_dim]
    latter = heads_in[..., half_dim:]
    return jnp.concatenate([former * cosine_table - latter * sine_table, latter * cosine_table + former * sine_table], axis=-1)

def visible(query_places, key_places):
    query_segment = jnp.where(query_places >= PROMPT, (query_places - PROMPT) // CONT, -1)
    key_segment = jnp.where(key_places >= PROMPT, (key_places - PROMPT) // CONT, -1)
    earlier = key_places[None, :] <= query_places[:, None]
    shared = (key_places[None, :] < PROMPT) | (key_segment[None, :] == query_segment[:, None])
    return earlier & shared

def keep_pairs(route_rows, rank_rows):
    flat_routes = route_rows.reshape(-1)
    onehot = (flat_routes[:, None] == jnp.arange(EXPERTS, dtype=jnp.int32)[None, :]).astype(jnp.int32)
    ranked = jnp.zeros_like(onehot).at[rank_rows].set(onehot)
    before = jnp.cumsum(ranked, axis=0, dtype=jnp.int32) - ranked
    slot_rank = lax.optimization_barrier(jnp.sum(before[rank_rows] * onehot, axis=1, dtype=jnp.int32))
    return (slot_rank, (flat_routes >= EXPERTS) | (slot_rank < CAP))

def attend(queries, key_heads, value_heads, places):
    span = 512 if GROUP % 512 == 0 else GROUP
    query_blocks = queries.reshape(GROUP // span, span, HEADS, HEAD_DIM)
    place_blocks = places.reshape(GROUP // span, span)

    def one_block(inputs):
        query_blk, place_blk = inputs
        scores = low_back(jnp.einsum('qhd,khd->hqk', query_blk, key_heads, precision=highest) * HEAD_DIM ** (-0.5))
        allowed = visible(place_blk, places)
        scores = jnp.where(allowed[None], scores, masked_score)
        weights = low(jax.nn.softmax(scores, axis=-1))
        return jnp.einsum('hqk,khd->qhd', weights, value_heads, precision=highest)
    result = lax.map(jax.checkpoint(one_block), (query_blocks, place_blocks))
    return result.reshape(GROUP, HEADS * HEAD_DIM)

def layer_rows(hidden, previous, weights_now, chosen, places, cosine_table, sine_table):
    wqkv, wout, wgate, wup, wdown, gain_attn, gain_moe, wrouter, wconst, cvec = weights_now
    normed = low(rms_rows(hidden, gain_attn))
    projected = low_back(jnp.dot(normed, wqkv, precision=highest))
    query_heads = low(rotate(projected[:, :D].reshape(GROUP, HEADS, HEAD_DIM), cosine_table, sine_table))
    key_heads = low(rotate(projected[:, D:2 * D].reshape(GROUP, HEADS, HEAD_DIM), cosine_table, sine_table))
    value_heads = low(projected[:, 2 * D:].reshape(GROUP, HEADS, HEAD_DIM))
    attended = low_back(low(attend(query_heads, key_heads, value_heads, places)))
    attn_out = low_back(jnp.dot(attended, wout, precision=highest))
    midway = hidden + attn_out
    mixed_rows = rms_rows(midway, gain_moe)
    mixed_low = low(mixed_rows)
    logits = jnp.dot(mixed_low, wrouter, precision=highest) + previous
    chances = jax.nn.softmax(logits, axis=-1)
    mixing = jax.nn.softmax(jnp.dot(mixed_low, wconst, precision=highest).reshape(GROUP, 2, 2), axis=-1)
    weight_of = chances * chosen
    mixture = weight_of[:, EXPERTS + 1:EXPERTS + 2] * mixed_rows
    for number in range(2):
        const_out = mixing[:, number, 0:1] * mixed_rows + mixing[:, number, 1:2] * cvec[:, number][None, :]
        mixture = mixture + weight_of[:, EXPERTS + 2 + number:EXPERTS + 3 + number] * const_out
    for expert in range(EXPERTS):
        gate_act = low_back(jnp.dot(mixed_low, wgate[expert], precision=highest))
        upward = low_back(jnp.dot(mixed_low, wup[expert], precision=highest))
        hidden_act = low(jax.nn.silu(gate_act) * upward)
        expert_out = low_back(jnp.dot(hidden_act, wdown[expert], precision=highest))
        mixture = mixture + weight_of[:, expert:expert + 1] * expert_out
    return (midway + mixture, logits)

def reference(tokens, prev_logits, routes, order, deal, w_qkv, w_out, w_gate, w_up, w_down, norm_attn, norm_moe, w_router, w_const, const_vec, grad_out):
    block_rows = TOK_DEV // 2
    rows_all = jnp.arange(GROUP, dtype=jnp.int32)
    places = deal[rows_all // block_rows].astype(jnp.int32) * block_rows + rows_all % block_rows
    within = jnp.where(places < PROMPT, places, PROMPT + (places - PROMPT) % CONT)
    frequency = 10000.0 ** (-jnp.arange(HEAD_DIM // 2, dtype=jnp.float32) / (HEAD_DIM // 2))
    angles = within.astype(jnp.float32)[:, None] * frequency[None, :]
    cosine_table = jnp.cos(angles)[:, None, :]
    sine_table = jnp.sin(angles)[:, None, :]
    chosen_all = []
    for group_at in range(GROUPS):
        route_rows = routes[group_at].reshape(N_CTX, TOK_DEV, TOP)
        rank_rows = order[group_at].reshape(N_CTX, TOK_DEV * TOP)
        slot_rank, retained = jax.vmap(keep_pairs)(route_rows, rank_rows)
        onehot = (routes[group_at][..., None] == jnp.arange(ROUTED, dtype=jnp.int32)).astype(jnp.float32)
        chosen_all.append(lax.optimization_barrier(jnp.sum(onehot * retained.reshape(GROUP, TOP, 1).astype(jnp.float32), axis=1)))
    previous_all = prev_logits.astype(jnp.float32)

    def forward(inputs, weight_list):
        results = []
        for group_at in range(GROUPS):
            hidden = inputs[group_at]
            previous = previous_all[group_at]
            for layer_at in range(LAYERS):
                weights_now = tuple((member[layer_at] for member in weight_list))
                hidden, previous = layer_rows(hidden, previous, weights_now, chosen_all[group_at], places, cosine_table, sine_table)
            results.append(hidden)
        return jnp.stack(results)
    weight_list = tuple((member.astype(jnp.float32) for member in (w_qkv, w_out, w_gate, w_up, w_down, norm_attn, norm_moe, w_router, w_const, const_vec)))
    output, backward = jax.vjp(forward, tokens.astype(jnp.float32), weight_list)
    input_grad, weight_grads = backward(grad_out.astype(jnp.float32))
    return (output.astype(jnp.bfloat16), input_grad, weight_grads[0], weight_grads[1], weight_grads[2], weight_grads[3], weight_grads[4], weight_grads[5], weight_grads[6], weight_grads[7], weight_grads[8], weight_grads[9])
```

```python
import functools

import jax
import jax.numpy as jnp
from jax import lax
from jax.experimental import pallas as pl
from jax.experimental.pallas import tpu as pltpu
from jax.sharding import Mesh
from jax.sharding import PartitionSpec as P

HEADS = 12
HEAD_DIM = 64
EXPERTS = 8
TOP = 2
LAYERS = 2
ROUTED = 12
CAP = 26
SLOTS = 32
LANES = 128
PAIRS = HEADS // 2

EX = "ex"
SUB = "sub"
FS = "fsdp"
CTX = (EX, SUB)
ALL = (EX, SUB, FS)

norm_eps = 1e-06
masked_score = -1e30
highest = lax.Precision.HIGHEST
f32 = jnp.float32
bf16 = jnp.bfloat16
VMEM_LIMIT = 56 * 1024 * 1024

SMALL_ROUTER = 2
SMALL_CONST = SMALL_ROUTER + ROUTED
SMALL_CVEC = SMALL_CONST + 4
SMALL_USED = SMALL_CVEC + 2


def dot_nn(a, b):
    return lax.dot_general(a, b, (((1,), (0,)), ((), ())), preferred_element_type=f32)


def dot_nt(a, b):
    return lax.dot_general(a, b, (((1,), (1,)), ((), ())), preferred_element_type=f32)


def dot_tn(a, b):
    return lax.dot_general(a, b, (((0,), (0,)), ((), ())), preferred_element_type=f32)


def kernel_params(steps):
    return pltpu.CompilerParams(
        dimension_semantics=("arbitrary",) * steps, vmem_limit_bytes=VMEM_LIMIT
    )


def turn_lanes(x, cosine, sine):
    lane = lax.broadcasted_iota(jnp.int32, x.shape, 1)
    ahead = pltpu.roll(x, LANES - HEAD_DIM // 2, 1)
    behind = pltpu.roll(x, HEAD_DIM // 2, 1)
    partner = jnp.where(lane % HEAD_DIM < HEAD_DIM // 2, ahead, behind)
    return x * cosine + partner * sine


def project_kernel(turned, a_ref, *refs):
    count = len(turned)
    w_refs = refs[:count]
    cos_ref, sin_ref = refs[count : count + 2]
    out_refs = refs[count + 2 :]
    a = a_ref[...]
    for w_ref, out_ref, turn in zip(w_refs, out_refs, turned):
        acc = dot_nn(a, w_ref[...])
        if not turn:
            out_ref[...] = acc.astype(bf16)
            continue
        for at in range(0, acc.shape[1], LANES):
            part = turn_lanes(acc[:, at : at + LANES], cos_ref[...], sin_ref[...])
            out_ref[:, at : at + LANES] = part.astype(bf16)


def project(rows, packed, columns, turned, cosine, sine):
    count, width = rows.shape
    tile = min(count, 256)
    w_specs = [
        pl.BlockSpec((width, width), functools.partial(lambda at, i: (0, at), at))
        for at in columns
    ]
    row_spec = pl.BlockSpec((tile, width), lambda i: (i, 0))
    table = pl.BlockSpec((tile, LANES), lambda i: (i, 0))
    return pl.pallas_call(
        functools.partial(project_kernel, turned),
        grid=(count // tile,),
        in_specs=[row_spec] + w_specs + [table, table],
        out_specs=[row_spec] * len(columns),
        out_shape=[jax.ShapeDtypeStruct((count, width), bf16)] * len(columns),
        compiler_params=kernel_params(1),
        cost_estimate=pl.CostEstimate(
            flops=2 * count * width * width * len(columns),
            bytes_accessed=2 * width * (count * (1 + len(columns)) + width * len(columns)),
            transcendentals=0,
        ),
    )(rows, *([packed] * len(columns)), cosine, sine)


def split_heads(x):
    wide = x.astype(f32)
    left = lax.broadcasted_iota(jnp.int32, wide.shape, 1) < HEAD_DIM
    zero = jnp.zeros_like(wide)
    return jnp.concatenate(
        [jnp.where(left, wide, zero), jnp.where(left, zero, wide)], axis=0
    ).astype(bf16)


def join_heads(x, rows):
    left = lax.broadcasted_iota(jnp.int32, (rows, LANES), 1) < HEAD_DIM
    return jnp.where(left, x[:rows], x[rows:])


def attend_kernel(
    prompt, q_ref, k_ref, v_ref, at_ref, start_ref, key_ref, o_ref, total_ref, bias_ref
):
    pair = pl.program_id(0)
    rows = q_ref.shape[0]

    @pl.when(pair == 0)
    def _():
        places, keys = at_ref[...], key_ref[...]
        seen = (keys <= places) & ((keys < prompt) | (keys >= start_ref[...]))
        bias_ref[...] = jnp.where(seen, 0.0, masked_score)
        total_ref[...] = jnp.zeros_like(total_ref)

    queries = split_heads(q_ref[...] * HEAD_DIM ** (-0.5))
    keys, values = k_ref[...], v_ref[...]
    lane = lax.broadcasted_iota(jnp.int32, (rows, LANES), 1)
    outs = []
    totals = total_ref[...]
    for side in range(2):
        scores = dot_nt(queries[side * rows : (side + 1) * rows], keys) + bias_ref[...]
        top = jnp.max(scores, axis=1, keepdims=True)
        expo = jnp.exp(scores - top)
        total = jnp.sum(expo, axis=1, keepdims=True)
        outs.append(dot_nn(expo.astype(bf16), values) / total)
        totals = jnp.where(lane == 2 * pair + side, top + jnp.log(total), totals)
    o_ref[...] = jnp.where(lane < HEAD_DIM, outs[0], outs[1])
    total_ref[...] = totals


def attend(queries, keys, values, places, starts, key_places, prompt):
    rows, width = queries.shape
    length = keys.shape[0]
    own = pl.BlockSpec((rows, LANES), lambda j: (0, j))
    every = pl.BlockSpec((length, LANES), lambda j: (0, j))
    column = pl.BlockSpec((rows, 1), lambda j: (0, 0))
    line = pl.BlockSpec((1, length), lambda j: (0, 0))
    return pl.pallas_call(
        functools.partial(attend_kernel, prompt),
        grid=(PAIRS,),
        in_specs=[own, every, every, column, column, line],
        out_specs=[own, pl.BlockSpec((rows, LANES), lambda j: (0, 0))],
        out_shape=[
            jax.ShapeDtypeStruct((rows, width), f32),
            jax.ShapeDtypeStruct((rows, LANES), f32),
        ],
        scratch_shapes=[pltpu.VMEM((rows, length), f32)],
        compiler_params=kernel_params(1),
        cost_estimate=pl.CostEstimate(
            flops=8 * rows * length * width,
            bytes_accessed=4 * length * width,
            transcendentals=rows * length * HEADS,
        ),
    )(queries, keys, values, places, starts, key_places)


def pick_column(table, at):
    lane = lax.broadcasted_iota(jnp.int32, table.shape, 1)
    return jnp.sum(jnp.where(lane == at, table, 0.0), axis=1, keepdims=True)


def query_kernel(
    prompt,
    q_ref,
    g_ref,
    k_ref,
    v_ref,
    total_ref,
    delta_ref,
    at_ref,
    start_ref,
    key_ref,
    cos_ref,
    sin_ref,
    out_ref,
    bias_ref,
):
    pair = pl.program_id(0)
    rows = q_ref.shape[0]

    @pl.when(pair == 0)
    def _():
        places, keys = at_ref[...], key_ref[...]
        seen = (keys <= places) & ((keys < prompt) | (keys >= start_ref[...]))
        bias_ref[...] = jnp.where(seen, 0.0, masked_score)

    scale = HEAD_DIM ** (-0.5)
    queries = split_heads(q_ref[...] * scale)
    grads = split_heads(g_ref[...])
    keys, values = k_ref[...], v_ref[...]
    lane = lax.broadcasted_iota(jnp.int32, (rows, LANES), 1)
    outs = []
    for side in range(2):
        part = slice(side * rows, (side + 1) * rows)
        total = pick_column(total_ref[...], 2 * pair + side)
        delta = pick_column(delta_ref[...], 2 * pair + side)
        scores = dot_nt(queries[part], keys) + bias_ref[...]
        probs = jnp.exp(scores - total)
        prob_grad = dot_nt(grads[part], values)
        score_grad = (probs * (prob_grad - delta)).astype(bf16)
        outs.append(dot_nn(score_grad, keys))
    out = jnp.where(lane < HEAD_DIM, outs[0], outs[1]) * scale
    out_ref[...] = turn_lanes(out, cos_ref[...], -sin_ref[...]).astype(bf16)


def query_back(queries, grads, keys, values, totals, delta, places, starts, key_places, cosine, sine, prompt):
    rows, width = queries.shape
    length = keys.shape[0]
    own = pl.BlockSpec((rows, LANES), lambda j: (0, j))
    every = pl.BlockSpec((length, LANES), lambda j: (0, j))
    same = pl.BlockSpec((rows, LANES), lambda j: (0, 0))
    column = pl.BlockSpec((rows, 1), lambda j: (0, 0))
    line = pl.BlockSpec((1, length), lambda j: (0, 0))
    return pl.pallas_call(
        functools.partial(query_kernel, prompt),
        grid=(PAIRS,),
        in_specs=[own, own, every, every, same, same, column, column, line, same, same],
        out_specs=own,
        out_shape=jax.ShapeDtypeStruct((rows, width), bf16),
        scratch_shapes=[pltpu.VMEM((rows, length), f32)],
        compiler_params=kernel_params(1),
        cost_estimate=pl.CostEstimate(
            flops=12 * rows * length * width,
            bytes_accessed=4 * length * width,
            transcendentals=rows * length * HEADS,
        ),
    )(queries, grads, keys, values, totals, delta, places, starts, key_places, cosine, sine)


def key_kernel(
    prompt,
    k_ref,
    v_ref,
    q_ref,
    g_ref,
    stat_ref,
    own_ref,
    at_ref,
    start_ref,
    cos_ref,
    sin_ref,
    dk_ref,
    dv_ref,
    bias_ref,
    lines_ref,
):
    pair = pl.program_id(0)
    rows = k_ref.shape[0]

    @pl.when(pair == 0)
    def _():
        keys, places = own_ref[...], at_ref[...]
        seen = (keys <= places) & ((keys < prompt) | (keys >= start_ref[...]))
        bias_ref[...] = jnp.where(seen, 0.0, masked_score)
        flat = stat_ref[...].astype(f32).T
        for head in range(HEADS):
            lines_ref[head] = flat[head : head + 1] + flat[16 + head : 17 + head]
            lines_ref[16 + head] = flat[32 + head : 33 + head] + flat[48 + head : 49 + head]

    scale = HEAD_DIM ** (-0.5)
    own_keys = split_heads(k_ref[...] * scale)
    own_values = split_heads(v_ref[...])
    queries, grads = q_ref[...], g_ref[...]
    lane = lax.broadcasted_iota(jnp.int32, (rows, LANES), 1)
    key_outs, value_outs = [], []
    for side in range(2):
        part = slice(side * rows, (side + 1) * rows)
        total = lines_ref[2 * pair + side]
        delta = lines_ref[16 + 2 * pair + side]
        scores = dot_nt(own_keys[part], queries) + bias_ref[...]
        probs = jnp.exp(scores - total)
        value_outs.append(dot_nn(probs.astype(bf16), grads))
        prob_grad = dot_nt(own_values[part], grads)
        score_grad = (probs * (prob_grad - delta)).astype(bf16)
        key_outs.append(dot_nn(score_grad, queries))
    left = lane < HEAD_DIM
    dk = jnp.where(left, key_outs[0], key_outs[1]) * scale
    dk_ref[...] = turn_lanes(dk, cos_ref[...], -sin_ref[...]).astype(bf16)
    dv_ref[...] = jnp.where(left, value_outs[0], value_outs[1]).astype(bf16)


def key_back(own_keys, own_values, queries, sent, own_places, places, starts, cosine, sine, prompt):
    rows, width = own_keys.shape
    length = queries.shape[0]
    own = pl.BlockSpec((rows, LANES), lambda j: (0, j))
    every = pl.BlockSpec((length, LANES), lambda j: (0, j))
    stats = pl.BlockSpec((length, LANES), lambda j: (0, PAIRS))
    same = pl.BlockSpec((rows, LANES), lambda j: (0, 0))
    column = pl.BlockSpec((rows, 1), lambda j: (0, 0))
    line = pl.BlockSpec((1, length), lambda j: (0, 0))
    return pl.pallas_call(
        functools.partial(key_kernel, prompt),
        grid=(PAIRS,),
        in_specs=[own, own, every, every, stats, column, line, line, same, same],
        out_specs=[own, own],
        out_shape=[jax.ShapeDtypeStruct((rows, width), bf16)] * 2,
        scratch_shapes=[
            pltpu.VMEM((rows, length), f32),
            pltpu.VMEM((32, 1, length), f32),
        ],
        compiler_params=kernel_params(1),
        cost_estimate=pl.CostEstimate(
            flops=16 * rows * length * width,
            bytes_accessed=4 * length * width,
            transcendentals=rows * length * HEADS,
        ),
    )(own_keys, own_values, queries, sent, sent, own_places, places, starts, cosine, sine)


def rms_rows(values, gain):
    scale = lax.rsqrt(jnp.mean(values * values, axis=-1, keepdims=True) + norm_eps)
    return values * scale * gain


def rms_back(values, gain, grad):
    mean = jnp.mean(values * values, axis=-1, keepdims=True) + norm_eps
    scale = lax.rsqrt(mean)
    inner = grad * gain
    along = jnp.mean(inner * values, axis=-1, keepdims=True)
    gain_grad = jnp.sum(grad * values * scale, axis=0)
    return scale * inner - values * (scale / mean * along), gain_grad


def high_low(x):
    top = x.astype(bf16)
    return top, (x - top.astype(f32)).astype(bf16)


def dispatch(x):
    return lax.all_to_all(x, EX, 0, 0, tiled=True)


def shards(
    tokens,
    prev_logits,
    routes,
    order,
    deal,
    w_qkv,
    w_out,
    w_gate,
    w_up,
    w_down,
    norm_attn,
    norm_moe,
    w_router,
    w_const,
    const_vec,
    grad_out,
):
    rows, width = tokens.shape[1], tokens.shape[2]
    subs = lax.axis_size(SUB)
    ctx_size = lax.axis_size(EX) * subs
    length = rows * ctx_size
    prompt = length // 2
    cont_len = prompt // (ctx_size // 8)
    block_rows = rows // 2
    own_rows = w_qkv.shape[1]
    me = lax.axis_index(CTX)

    pad = jnp.zeros((own_rows, LANES - SMALL_USED), bf16)

    def fetch(layer):
        mine = jnp.concatenate(
            [
                w_qkv[layer],
                w_out[layer],
                norm_attn[layer][:, None],
                norm_moe[layer][:, None],
                w_router[layer],
                w_const[layer],
                const_vec[layer],
                pad,
            ],
            axis=1,
        )
        packed = lax.all_gather(mine, ALL, axis=0, tiled=True)
        experts = []
        for member in (w_gate, w_up, w_down):
            moved = dispatch(member[layer])
            whole = lax.all_gather(moved, (SUB, FS), axis=1, tiled=True)
            experts.append(whole.reshape(-1, whole.shape[2]))
        return packed, experts

    fetched = [fetch(layer) for layer in range(LAYERS)]

    all_places = (
        deal[:, None] * block_rows + jnp.arange(block_rows, dtype=jnp.int32)[None, :]
    ).reshape(length)
    within = jnp.where(all_places < prompt, all_places, prompt + (all_places - prompt) % cont_len)
    all_starts = jnp.where(all_places < prompt, 0, all_places - (all_places - prompt) % cont_len)
    lane = jnp.arange(LANES, dtype=jnp.int32)
    half = HEAD_DIM // 2
    frequency = 10000.0 ** (-(lane % half).astype(f32) / half)
    angles = within.astype(f32)[:, None] * frequency[None, :]
    cosine = jnp.cos(angles)
    sine = jnp.sin(angles) * jnp.where(lane % HEAD_DIM < half, -1.0, 1.0)[None, :]

    def own_part(table):
        return lax.dynamic_slice_in_dim(table, me * rows, rows, 0)

    own_cos, own_sin = own_part(cosine), own_part(sine)
    own_places = own_part(all_places)[:, None]
    own_starts = own_part(all_starts)[:, None]
    place_line, start_line = all_places[None, :], all_starts[None, :]

    route_rows = routes[0]
    flat_routes = jnp.concatenate([route_rows[:, k] for k in range(TOP)])
    flat_order = jnp.concatenate([order[0].reshape(rows, TOP)[:, k] for k in range(TOP)])
    earlier = (flat_routes[None, :] == flat_routes[:, None]) & (
        flat_order[None, :] < flat_order[:, None]
    )
    slot = jnp.sum(earlier.astype(jnp.int32), axis=1)
    in_slot = (flat_routes < EXPERTS) & (slot < CAP)
    target = jnp.where(in_slot, flat_routes * SLOTS + slot, -1)
    slot_ids = jnp.arange(EXPERTS * SLOTS, dtype=jnp.int32)
    pair_slots = (target[:, None] == slot_ids[None, :]).astype(bf16)
    slot_pairs = (slot_ids[:, None] == target[None, :]).astype(bf16)
    slot_tokens = slot_pairs[:, :rows] + slot_pairs[:, rows:]
    token_slots = pair_slots[:rows] + pair_slots[rows:]
    route_ids = jnp.arange(ROUTED, dtype=jnp.int32)
    picks = [(route_rows[:, k : k + 1] == route_ids[None, :]).astype(f32) for k in range(TOP)]
    chosen = picks[0] + picks[1]
    head_of = (
        jnp.arange(width, dtype=jnp.int32)[:, None] // HEAD_DIM == lane[None, :]
    ).astype(f32)

    def unpack(packed):
        small = packed[:, 4 * width :]
        return small, small[:, 0].astype(f32), small[:, 1].astype(f32)

    hidden = tokens[0].astype(f32)
    previous = prev_logits[0]
    saved_all = []
    for layer in range(LAYERS):
        packed, (wgate, wup, wdown) = fetched[layer]
        small, gain_attn, gain_moe = unpack(packed)
        normed = rms_rows(hidden, gain_attn).astype(bf16)
        normed_all = lax.all_gather(normed, CTX, axis=0, tiled=True)
        (queries,) = project(normed, packed, (0,), (True,), own_cos, own_sin)
        keys, values = project(normed_all, packed, (1, 2), (True, False), cosine, sine)
        attended, totals = attend(
            queries, keys, values, own_places, own_starts, place_line, prompt
        )
        att_low = attended.astype(bf16)
        wout = packed[:, 3 * width : 4 * width]
        midway = hidden + dot_nn(att_low, wout)
        mixed = rms_rows(midway, gain_moe)
        mixed_low = mixed.astype(bf16)
        slot_in = dot_nn(slot_tokens, mixed_low).astype(bf16)
        expert_in = dispatch(slot_in.reshape(EXPERTS, SLOTS, width)).reshape(-1, width)
        thin = dot_nn(mixed_low, small)
        logits = thin[:, SMALL_ROUTER:SMALL_CONST] + previous
        chances = jax.nn.softmax(logits, axis=-1)
        mixing = jax.nn.softmax(thin[:, SMALL_CONST:SMALL_CVEC].reshape(rows, 2, 2), axis=-1)
        gate_act = dot_nn(expert_in, wgate)
        upward = dot_nn(expert_in, wup)
        inner = (jax.nn.silu(gate_act) * upward).astype(bf16)
        expert_out = dot_nn(inner, wdown).astype(bf16)
        back = dispatch(expert_out.reshape(EXPERTS, SLOTS, width)).reshape(-1, width)
        pair_out = dot_nn(pair_slots, back)
        weight = chances * chosen
        picked = [jnp.sum(chances * picks[k], axis=1, keepdims=True) for k in range(TOP)]
        alpha = (
            weight[:, 9:10]
            + weight[:, 10:11] * mixing[:, 0, 0:1]
            + weight[:, 11:12] * mixing[:, 1, 0:1]
        )
        betas = [weight[:, 10 + c : 11 + c] * mixing[:, c, 1:2] for c in range(2)]
        cvecs = [small[:, SMALL_CVEC + c].astype(f32) for c in range(2)]
        output = (
            midway
            + picked[0] * pair_out[:rows]
            + picked[1] * pair_out[rows:]
            + alpha * mixed
            + betas[0] * cvecs[0][None, :]
            + betas[1] * cvecs[1][None, :]
        )
        saved_all.append(
            (
                hidden,
                normed,
                normed_all,
                queries,
                keys,
                values,
                attended,
                totals,
                att_low,
                midway,
                mixed,
                mixed_low,
                chances,
                mixing,
                expert_in,
                gate_act,
                upward,
                inner,
                pair_out,
                weight,
                picked,
                alpha,
                betas,
                cvecs,
            )
        )
        hidden = output
        previous = logits
    output_rows = hidden.astype(bf16)[None]

    grad = grad_out[0].astype(f32)
    logit_next = jnp.zeros((rows, ROUTED), f32)
    results = [None] * LAYERS
    for layer in reversed(range(LAYERS)):
        (
            hidden,
            normed,
            normed_all,
            queries,
            keys,
            values,
            attended,
            totals,
            att_low,
            midway,
            mixed,
            mixed_low,
            chances,
            mixing,
            expert_in,
            gate_act,
            upward,
            inner,
            pair_out,
            weight,
            picked,
            alpha,
            betas,
            cvecs,
        ) = saved_all[layer]
        packed, (wgate, wup, wdown) = fetched[layer]
        small, gain_attn, gain_moe = unpack(packed)
        pair_grad = jnp.concatenate([picked[k] * grad for k in range(TOP)], axis=0).astype(bf16)
        slot_grad = dot_nn(slot_pairs, pair_grad).astype(bf16)
        out_grad = dispatch(slot_grad.reshape(EXPERTS, SLOTS, width)).reshape(-1, width)
        inner_grad = dot_nt(out_grad, wdown)
        sigma = jax.nn.sigmoid(gate_act)
        gated = gate_act * sigma
        up_grad = (inner_grad * gated).astype(bf16)
        gate_grad = (inner_grad * upward * (sigma + gated * (1.0 - sigma))).astype(bf16)
        in_grad = (dot_nt(gate_grad, wgate) + dot_nt(up_grad, wup)).astype(bf16)
        in_back = dispatch(in_grad.reshape(EXPERTS, SLOTS, width)).reshape(-1, width)
        expert_grads = (
            dot_tn(expert_in, gate_grad),
            dot_tn(expert_in, up_grad),
            dot_tn(inner, out_grad),
        )
        returned = []
        for member in expert_grads:
            cut = member.astype(bf16).reshape(EXPERTS, subs * 2, -1, member.shape[1])
            part = lax.psum_scatter(cut, (SUB, FS), scatter_dimension=1, tiled=True)
            returned.append(dispatch(part.reshape(EXPERTS, -1, member.shape[1])).astype(f32))

        picked_grad = [
            jnp.sum(grad * pair_out[k * rows : (k + 1) * rows], axis=1, keepdims=True)
            for k in range(TOP)
        ]
        along = jnp.sum(grad * mixed, axis=1, keepdims=True)
        across = [jnp.sum(grad * cvecs[c][None, :], axis=1, keepdims=True) for c in range(2)]
        chance_grad = picks[0] * picked_grad[0] + picks[1] * picked_grad[1]
        side = jnp.concatenate(
            [
                jnp.zeros((rows, EXPERTS + 1), f32),
                along,
                mixing[:, 0, 0:1] * along + mixing[:, 0, 1:2] * across[0],
                mixing[:, 1, 0:1] * along + mixing[:, 1, 1:2] * across[1],
            ],
            axis=1,
        )
        chance_grad = chance_grad + side * chosen
        logit_grad = (
            chances * (chance_grad - jnp.sum(chances * chance_grad, axis=1, keepdims=True))
            + logit_next
        )
        mix_cols = []
        for c in range(2):
            first = weight[:, 10 + c : 11 + c] * along
            second = weight[:, 10 + c : 11 + c] * across[c]
            m0, m1 = mixing[:, c, 0:1], mixing[:, c, 1:2]
            mean = m0 * first + m1 * second
            mix_cols += [m0 * (first - mean), m1 * (second - mean)]
        thin_grad = jnp.concatenate(
            [jnp.zeros((rows, SMALL_ROUTER), f32), logit_grad]
            + mix_cols
            + [jnp.zeros((rows, LANES - SMALL_CVEC), f32)],
            axis=1,
        )
        low_grad = (
            alpha * grad
            + lax.dot_general(
                thin_grad,
                small.astype(f32),
                (((1,), (1,)), ((), ())),
                precision=highest,
                preferred_element_type=f32,
            )
            + dot_nn(token_slots, in_back)
        )
        mid_part, gain_moe_grad = rms_back(midway, gain_moe, low_grad)
        mid_grad = grad + mid_part
        mid_low = mid_grad.astype(bf16)
        wout = packed[:, 3 * width : 4 * width]
        att_grad = dot_nt(mid_low, wout).astype(bf16)
        delta = jnp.dot(att_grad.astype(f32) * attended, head_of, precision=highest)
        pieces = []
        for stat in (totals, delta):
            pieces += [part[:, :16] for part in high_low(stat)]
        sent = jnp.concatenate(
            [att_grad] + pieces + [jnp.zeros((rows, LANES - 64), bf16)], axis=1
        )
        sent_all = lax.all_gather(sent, CTX, axis=0, tiled=True)
        (all_queries,) = project(normed_all, packed, (0,), (True,), cosine, sine)
        query_grad = query_back(
            queries,
            att_grad,
            keys,
            values,
            totals,
            delta,
            own_places,
            own_starts,
            place_line,
            own_cos,
            own_sin,
            prompt,
        )
        key_grad, value_grad = key_back(
            own_part(keys),
            own_part(values),
            all_queries,
            sent_all,
            own_places,
            place_line,
            start_line,
            own_cos,
            own_sin,
            prompt,
        )
        proj_grad = jnp.concatenate([query_grad, key_grad, value_grad], axis=1)
        normed_grad = dot_nt(proj_grad, packed[:, : 3 * width])
        hidden_part, gain_attn_grad = rms_back(hidden, gain_attn, normed_grad)
        thin_w = jnp.dot(mixed_low.astype(f32).T, thin_grad, precision=highest)
        cvec_grads = [jnp.sum(betas[c] * grad, axis=0)[:, None] for c in range(2)]
        packed_grad = jnp.concatenate(
            [
                dot_tn(normed, proj_grad),
                dot_tn(att_low, mid_low),
                gain_attn_grad[:, None],
                gain_moe_grad[:, None],
                thin_w[:, SMALL_ROUTER:SMALL_CVEC],
                cvec_grads[0],
                cvec_grads[1],
                jnp.zeros((width, LANES - SMALL_USED), f32),
            ],
            axis=1,
        ).astype(bf16)
        owned = lax.psum_scatter(packed_grad, ALL, scatter_dimension=0, tiled=True).astype(f32)
        results[layer] = (
            owned[:, : 3 * width],
            owned[:, 3 * width : 4 * width],
            returned[0],
            returned[1],
            returned[2],
            owned[:, 4 * width],
            owned[:, 4 * width + 1],
            owned[:, 4 * width + SMALL_ROUTER : 4 * width + SMALL_CONST],
            owned[:, 4 * width + SMALL_CONST : 4 * width + SMALL_CVEC],
            owned[:, 4 * width + SMALL_CVEC : 4 * width + SMALL_USED],
        )
        grad = mid_grad + hidden_part
        logit_next = logit_grad
    stacked = tuple(
        jnp.stack([results[layer][member] for layer in range(LAYERS)]) for member in range(10)
    )
    return (output_rows, grad[None]) + stacked


def solution(mesh):
    devices = mesh.devices
    finer = Mesh(devices.reshape(EXPERTS, devices.shape[0] // EXPERTS, devices.shape[1]), ALL)
    token_spec = P(FS, CTX, None)
    row_spec = P(None, ALL, None)
    expert_spec = P(None, None, ALL, None)
    gain_spec = P(None, ALL)
    return jax.shard_map(
        shards,
        mesh=finer,
        in_specs=(
            token_spec,
            token_spec,
            token_spec,
            P(FS, CTX),
            P(),
            row_spec,
            row_spec,
            expert_spec,
            expert_spec,
            expert_spec,
            gain_spec,
            gain_spec,
            row_spec,
            row_spec,
            row_spec,
            token_spec,
        ),
        out_specs=(
            token_spec,
            token_spec,
            row_spec,
            row_spec,
            expert_spec,
            expert_spec,
            expert_spec,
            gain_spec,
            gain_spec,
            row_spec,
            row_spec,
            row_spec,
        ),
        check_vma=False,
    )
```

```python
import functools

import jax
import jax.numpy as jnp
from jax import lax
from jax.experimental import pallas as pl
from jax.experimental.pallas import tpu as pltpu
from jax.sharding import Mesh
from jax.sharding import PartitionSpec as P

HEADS = 12
HEAD_DIM = 64
EXPERTS = 8
TOP = 2
LAYERS = 2
ROUTED = 12
CAP = 26
SLOTS = 32
LANES = 128
PAIRS = HEADS // 2

FS = "fsdp"


def ctx_axes(size):
    return tuple(f"ctx{at}" for at in range(size.bit_length() - 1))


norm_eps = 1e-06
masked_score = -1e30
highest = lax.Precision.HIGHEST
f32 = jnp.float32
bf16 = jnp.bfloat16
VMEM_LIMIT = 56 * 1024 * 1024

AT_CONST = 16
AT_CVEC = 24
AT_ATTN = 32
AT_MOE = 33


def dot_nn(a, b):
    return lax.dot_general(a, b, (((1,), (0,)), ((), ())), preferred_element_type=f32)


def dot_nt(a, b):
    return lax.dot_general(a, b, (((1,), (1,)), ((), ())), preferred_element_type=f32)


def dot_tn(a, b):
    return lax.dot_general(a, b, (((0,), (0,)), ((), ())), preferred_element_type=f32)


def kernel_params(steps):
    return pltpu.CompilerParams(
        dimension_semantics=("arbitrary",) * steps, vmem_limit_bytes=VMEM_LIMIT
    )


def turn_lanes(x, cosine, sine):
    lane = lax.broadcasted_iota(jnp.int32, x.shape, 1)
    ahead = pltpu.roll(x, LANES - HEAD_DIM // 2, 1)
    behind = pltpu.roll(x, HEAD_DIM // 2, 1)
    partner = jnp.where(lane % HEAD_DIM < HEAD_DIM // 2, ahead, behind)
    return x * cosine + partner * sine


def project_kernel(turned, a_ref, *refs):
    count = len(turned)
    w_refs = refs[:count]
    cos_ref, sin_ref = refs[count : count + 2]
    out_refs = refs[count + 2 :]
    a = a_ref[...]
    for w_ref, out_ref, turn in zip(w_refs, out_refs, turned):
        acc = dot_nn(a, w_ref[...])
        if not turn:
            out_ref[...] = acc.astype(bf16)
            continue
        for at in range(0, acc.shape[1], LANES):
            part = turn_lanes(acc[:, at : at + LANES], cos_ref[...], sin_ref[...])
            out_ref[:, at : at + LANES] = part.astype(bf16)


def project(rows, packed, columns, turned, cosine, sine):
    count, width = rows.shape
    tile = min(count, 512)
    w_specs = [
        pl.BlockSpec((width, width), functools.partial(lambda at, i: (0, at), at))
        for at in columns
    ]
    row_spec = pl.BlockSpec((tile, width), lambda i: (i, 0))
    table = pl.BlockSpec((tile, LANES), lambda i: (i, 0))
    return pl.pallas_call(
        functools.partial(project_kernel, turned),
        grid=(count // tile,),
        in_specs=[row_spec] + w_specs + [table, table],
        out_specs=[row_spec] * len(columns),
        out_shape=[jax.ShapeDtypeStruct((count, width), bf16)] * len(columns),
        compiler_params=kernel_params(1),
        cost_estimate=pl.CostEstimate(
            flops=2 * count * width * width * len(columns),
            bytes_accessed=2 * width * (count * (1 + len(columns)) + width * len(columns)),
            transcendentals=0,
        ),
    )(rows, *([packed] * len(columns)), cosine, sine)


def split_heads(x):
    wide = x.astype(f32)
    left = lax.broadcasted_iota(jnp.int32, wide.shape, 1) < HEAD_DIM
    zero = jnp.zeros_like(wide)
    return jnp.concatenate(
        [jnp.where(left, wide, zero), jnp.where(left, zero, wide)], axis=0
    ).astype(bf16)


def join_heads(x, rows):
    left = lax.broadcasted_iota(jnp.int32, (rows, LANES), 1) < HEAD_DIM
    return jnp.where(left, x[:rows], x[rows:])


def attend_kernel(
    prompt, q_ref, k_ref, v_ref, at_ref, start_ref, key_ref, o_ref, total_ref, bias_ref
):
    pair = pl.program_id(0)
    rows = q_ref.shape[0]

    @pl.when(pair == 0)
    def _():
        places, keys = at_ref[...], key_ref[...]
        seen = (keys <= places) & ((keys < prompt) | (keys >= start_ref[...]))
        bias_ref[...] = jnp.where(seen, 0.0, masked_score)
        total_ref[...] = jnp.zeros_like(total_ref)

    queries = split_heads(q_ref[...] * HEAD_DIM ** (-0.5))
    keys, values = k_ref[...], v_ref[...]
    lane = lax.broadcasted_iota(jnp.int32, (rows, LANES), 1)
    outs = []
    totals = total_ref[...]
    for side in range(2):
        scores = dot_nt(queries[side * rows : (side + 1) * rows], keys) + bias_ref[...]
        top = jnp.max(scores, axis=1, keepdims=True)
        expo = jnp.exp(scores - top)
        total = jnp.sum(expo, axis=1, keepdims=True)
        outs.append(dot_nn(expo.astype(bf16), values) / total)
        totals = jnp.where(lane == 2 * pair + side, top + jnp.log(total), totals)
    o_ref[...] = jnp.where(lane < HEAD_DIM, outs[0], outs[1])
    total_ref[...] = totals


def attend(queries, keys, values, places, starts, key_places, prompt):
    rows, width = places.shape[0], queries.shape[1]
    length = keys.shape[0]
    own = pl.BlockSpec((rows, LANES), lambda j: (0, j))
    every = pl.BlockSpec((length, LANES), lambda j: (0, j))
    column = pl.BlockSpec((rows, 1), lambda j: (0, 0))
    line = pl.BlockSpec((1, length), lambda j: (0, 0))
    return pl.pallas_call(
        functools.partial(attend_kernel, prompt),
        grid=(PAIRS,),
        in_specs=[own, every, every, column, column, line],
        out_specs=[own, pl.BlockSpec((rows, LANES), lambda j: (0, 0))],
        out_shape=[
            jax.ShapeDtypeStruct((rows, width), f32),
            jax.ShapeDtypeStruct((rows, LANES), f32),
        ],
        scratch_shapes=[pltpu.VMEM((rows, length), f32)],
        compiler_params=kernel_params(1),
        cost_estimate=pl.CostEstimate(
            flops=8 * rows * length * width,
            bytes_accessed=4 * length * width,
            transcendentals=rows * length * HEADS,
        ),
    )(queries, keys, values, places, starts, key_places)


def pick_column(table, at):
    lane = lax.broadcasted_iota(jnp.int32, table.shape, 1)
    return jnp.sum(jnp.where(lane == at, table, 0.0), axis=1, keepdims=True)


def query_kernel(
    prompt,
    start,
    q_ref,
    g_ref,
    k_ref,
    v_ref,
    total_ref,
    delta_ref,
    at_ref,
    start_ref,
    key_ref,
    cos_ref,
    sin_ref,
    out_ref,
    bias_ref,
):
    pair = pl.program_id(0) + start
    rows = q_ref.shape[0]

    @pl.when(pair == start)
    def _():
        places, keys = at_ref[...], key_ref[...]
        seen = (keys <= places) & ((keys < prompt) | (keys >= start_ref[...]))
        bias_ref[...] = jnp.where(seen, 0.0, masked_score)

    scale = HEAD_DIM ** (-0.5)
    queries = split_heads(q_ref[...] * scale)
    grads = split_heads(g_ref[...])
    keys, values = k_ref[...], v_ref[...]
    lane = lax.broadcasted_iota(jnp.int32, (rows, LANES), 1)
    outs = []
    for side in range(2):
        part = slice(side * rows, (side + 1) * rows)
        total = pick_column(total_ref[...], 2 * pair + side)
        delta = pick_column(delta_ref[...], 2 * pair + side)
        scores = dot_nt(queries[part], keys) + bias_ref[...]
        probs = jnp.exp(scores - total)
        prob_grad = dot_nt(grads[part], values)
        score_grad = (probs * (prob_grad - delta)).astype(bf16)
        outs.append(dot_nn(score_grad, keys))
    out = jnp.where(lane < HEAD_DIM, outs[0], outs[1]) * scale
    out_ref[...] = turn_lanes(out, cos_ref[...], -sin_ref[...]).astype(bf16)


def query_back(
    start, count, queries, grads, keys, values, totals, delta, places, starts, key_places, cosine, sine, prompt
):
    rows = places.shape[0]
    length = keys.shape[0]
    own = pl.BlockSpec((rows, LANES), lambda j: (0, j + start))
    every = pl.BlockSpec((length, LANES), lambda j: (0, j + start))
    same = pl.BlockSpec((rows, LANES), lambda j: (0, 0))
    column = pl.BlockSpec((rows, 1), lambda j: (0, 0))
    line = pl.BlockSpec((1, length), lambda j: (0, 0))
    width = count * LANES
    return pl.pallas_call(
        functools.partial(query_kernel, prompt, start),
        grid=(count,),
        in_specs=[own, own, every, every, same, same, column, column, line, same, same],
        out_specs=pl.BlockSpec((rows, LANES), lambda j: (0, j)),
        out_shape=jax.ShapeDtypeStruct((rows, width), bf16),
        scratch_shapes=[pltpu.VMEM((rows, length), f32)],
        compiler_params=kernel_params(1),
        cost_estimate=pl.CostEstimate(
            flops=12 * rows * length * width,
            bytes_accessed=4 * length * width,
            transcendentals=rows * length * HEADS,
        ),
    )(queries, grads, keys, values, totals, delta, places, starts, key_places, cosine, sine)


def key_kernel(
    prompt,
    k_ref,
    v_ref,
    q_ref,
    g_ref,
    stat_ref,
    own_ref,
    at_ref,
    start_ref,
    cos_ref,
    sin_ref,
    dk_ref,
    dv_ref,
    bias_ref,
    lines_ref,
):
    pair = pl.program_id(0)
    rows = k_ref.shape[0]

    @pl.when(pair == 0)
    def _():
        keys, places = own_ref[...], at_ref[...]
        seen = (keys <= places) & ((keys < prompt) | (keys >= start_ref[...]))
        bias_ref[...] = jnp.where(seen, 0.0, masked_score)
        flat = stat_ref[...].astype(f32).T
        for head in range(HEADS):
            lines_ref[head] = flat[head : head + 1] + flat[16 + head : 17 + head]
            lines_ref[16 + head] = flat[32 + head : 33 + head] + flat[48 + head : 49 + head]

    scale = HEAD_DIM ** (-0.5)
    own_keys = split_heads(k_ref[...] * scale)
    own_values = split_heads(v_ref[...])
    queries, grads = q_ref[...], g_ref[...]
    lane = lax.broadcasted_iota(jnp.int32, (rows, LANES), 1)
    key_outs, value_outs = [], []
    for side in range(2):
        part = slice(side * rows, (side + 1) * rows)
        total = lines_ref[2 * pair + side]
        delta = lines_ref[16 + 2 * pair + side]
        scores = dot_nt(own_keys[part], queries) + bias_ref[...]
        probs = jnp.exp(scores - total)
        value_outs.append(dot_nn(probs.astype(bf16), grads))
        prob_grad = dot_nt(own_values[part], grads)
        score_grad = (probs * (prob_grad - delta)).astype(bf16)
        key_outs.append(dot_nn(score_grad, queries))
    left = lane < HEAD_DIM
    dk = jnp.where(left, key_outs[0], key_outs[1]) * scale
    dk_ref[...] = turn_lanes(dk, cos_ref[...], -sin_ref[...]).astype(bf16)
    dv_ref[...] = jnp.where(left, value_outs[0], value_outs[1]).astype(bf16)


def key_back(own_keys, own_values, queries, sent, own_places, places, starts, cosine, sine, prompt):
    rows = own_places.shape[0]
    length, width = queries.shape
    own = pl.BlockSpec((rows, LANES), lambda j: (0, j))
    every = pl.BlockSpec((length, LANES), lambda j: (0, j))
    stats = pl.BlockSpec((length, LANES), lambda j: (0, PAIRS))
    same = pl.BlockSpec((rows, LANES), lambda j: (0, 0))
    column = pl.BlockSpec((rows, 1), lambda j: (0, 0))
    line = pl.BlockSpec((1, length), lambda j: (0, 0))
    return pl.pallas_call(
        functools.partial(key_kernel, prompt),
        grid=(PAIRS,),
        in_specs=[own, own, every, every, stats, column, line, line, same, same],
        out_specs=[own, own],
        out_shape=[jax.ShapeDtypeStruct((rows, width), bf16)] * 2,
        scratch_shapes=[
            pltpu.VMEM((rows, length), f32),
            pltpu.VMEM((32, 1, length), f32),
        ],
        compiler_params=kernel_params(1),
        cost_estimate=pl.CostEstimate(
            flops=16 * rows * length * width,
            bytes_accessed=4 * length * width,
            transcendentals=rows * length * HEADS,
        ),
    )(own_keys, own_values, queries, sent, sent, own_places, places, starts, cosine, sine)


def cross(x, flag_ref):
    tall = x.shape[0]
    far = jnp.full((tall, LANES), flag_ref[0, 0], jnp.int32) > 0
    near = jnp.full((tall, LANES), flag_ref[0, 1], jnp.int32) > 0
    left, right = x[:, :LANES], x[:, LANES:]
    left = jnp.where(near, pltpu.roll(left, HEAD_DIM, 1), left)
    right = jnp.where(near, pltpu.roll(right, HEAD_DIM, 1), right)
    return jnp.concatenate(
        [jnp.where(far, right, left), jnp.where(far, left, right)], axis=1
    )


def stack_rows(refs):
    return jnp.concatenate([ref[...] for ref in refs], axis=0)


def expert_kernel(flag_ref, x_ref, *refs):
    gates, ups, downs = refs[:4], refs[4:8], refs[8:12]
    gate_ref, up_ref, out_ref, acc_ref = refs[12:]
    step = pl.program_id(0)
    x = x_ref[...]
    gate = dot_nn(x, stack_rows(gates))
    up = dot_nn(x, stack_rows(ups))
    gate_ref[...] = gate
    up_ref[...] = up
    inner = cross(gate * jax.nn.sigmoid(gate) * up, flag_ref).astype(bf16)
    out = dot_nn(inner, stack_rows(downs))

    @pl.when(step == 0)
    def _():
        acc_ref[...] = out

    @pl.when(step > 0)
    def _():
        acc_ref[...] += out

    @pl.when(step == pl.num_programs(0) - 1)
    def _():
        out_ref[...] = acc_ref[...].astype(bf16)


def expert_specs(width, hidden):
    tile = hidden // EXPERTS
    tall = pl.BlockSpec((width // 4, tile), lambda j: (0, j))
    flat = pl.BlockSpec((tile // 4, width), lambda j: (j, 0))
    return tile, [tall] * 8 + [flat] * 4


def run_expert(flags, x, gates, ups, downs):
    rows, width = x.shape
    hidden = gates[0].shape[1]
    tile, specs = expert_specs(width, hidden)
    whole = pl.BlockSpec((rows, width), lambda j: (0, 0))
    column = pl.BlockSpec((rows, tile), lambda j: (0, j))
    return pl.pallas_call(
        expert_kernel,
        grid=(EXPERTS,),
        in_specs=[pl.BlockSpec(memory_space=pltpu.SMEM), whole] + specs,
        out_specs=[column, column, whole],
        out_shape=[
            jax.ShapeDtypeStruct((rows, hidden), f32),
            jax.ShapeDtypeStruct((rows, hidden), f32),
            jax.ShapeDtypeStruct((rows, width), bf16),
        ],
        scratch_shapes=[pltpu.VMEM((rows, width), f32)],
        compiler_params=kernel_params(1),
        cost_estimate=pl.CostEstimate(
            flops=6 * rows * width * hidden,
            bytes_accessed=6 * width * hidden + 8 * rows * hidden,
            transcendentals=rows * hidden,
        ),
    )(flags, x, *gates, *ups, *downs)


def expert_back_kernel(both, flag_ref, x_ref, grad_ref, order_ref, *refs):
    if not both:
        gate_ref, up_ref = refs[:2]
        refs = refs[2:]
    gates, ups, downs = refs[:4], refs[4:8], refs[8:12]
    outs, back_ref = refs[12:18], refs[18]
    acc_ref, turned_ref = refs[19:21]
    step = pl.program_id(0)
    last = step == pl.num_programs(0) - 1
    width = x_ref.shape[1]

    @pl.when(step == 0)
    def _():
        turned_ref[...] = x_ref[...].astype(f32).T.astype(bf16)

    grad = grad_ref[...]
    gate_w, up_w, down_w = stack_rows(gates), stack_rows(ups), stack_rows(downs)
    if both:
        x = x_ref[...]
        gate, up = dot_nn(x, gate_w), dot_nn(x, up_w)
    else:
        gate, up = gate_ref[...], up_ref[...]
    sigma = jax.nn.sigmoid(gate)
    gated = gate * sigma
    inner = cross(gated * up, flag_ref)
    inner_grad = cross(dot_nt(grad, down_w), flag_ref)
    up_low = (inner_grad * gated).astype(bf16)
    gate_low = (inner_grad * up * (sigma + gated * (1.0 - sigma))).astype(bf16)
    parts = [dot_nt(gate_low, gate_w) + dot_nt(up_low, up_w)]
    if both:
        parts.append(dot_nn(inner.astype(bf16), down_w))
    part = jnp.concatenate(parts, axis=1) if both else parts[0]

    @pl.when(step == 0)
    def _():
        acc_ref[...] = part

    @pl.when(step > 0)
    def _():
        acc_ref[...] += part

    @pl.when(last)
    def _():
        in_low = acc_ref[:, :width].astype(bf16)
        back_ref[:, :width] = dot_nt(in_low, order_ref[...]).astype(bf16)
        if both:
            back_ref[:, width:] = acc_ref[:, width:].astype(bf16)

    turned = turned_ref[...]
    members = (
        dot_nn(turned, gate_low).astype(bf16),
        dot_nn(turned, up_low).astype(bf16),
        dot_nn(inner.T.astype(bf16), grad).astype(bf16),
    )
    for at, member in enumerate(members):
        half = member.shape[0] // 2
        outs[2 * at][...] = member[:half]
        outs[2 * at + 1][...] = member[half:]


def run_expert_back(flags, received, order, gate, up, gates, ups, downs):
    both = gate is None
    if both:
        rows, width = received[0].shape[0], received[0].shape[1] // 2
    else:
        rows, width = received[0].shape
    hidden = gates[0].shape[1]
    tile, specs = expert_specs(width, hidden)
    first = pl.BlockSpec((rows, width), lambda j: (0, 0))
    beside = pl.BlockSpec((rows, width), lambda j: (0, 1)) if both else first
    table = pl.BlockSpec((width, width), lambda j: (0, 0))
    column = pl.BlockSpec((rows, tile), lambda j: (0, j))
    tall = pl.BlockSpec((width // 2, tile), lambda j: (0, j))
    flat = pl.BlockSpec((None, tile // 2, width), lambda j: (j, 0, 0))
    tall_shape = jax.ShapeDtypeStruct((width // 2, hidden), bf16)
    flat_shape = jax.ShapeDtypeStruct((EXPERTS, tile // 2, width), bf16)
    wide = 2 * width if both else width
    *halves, back = pl.pallas_call(
        functools.partial(expert_back_kernel, both),
        grid=(EXPERTS,),
        in_specs=[pl.BlockSpec(memory_space=pltpu.SMEM), first, beside, table]
        + ([] if both else [column, column])
        + specs,
        out_specs=[tall] * 4 + [flat] * 2 + [pl.BlockSpec((rows, wide), lambda j: (0, 0))],
        out_shape=[tall_shape] * 4
        + [flat_shape] * 2
        + [jax.ShapeDtypeStruct((rows, wide), bf16)],
        scratch_shapes=[pltpu.VMEM((rows, wide), f32), pltpu.VMEM((width, rows), bf16)],
        compiler_params=kernel_params(1),
        cost_estimate=pl.CostEstimate(
            flops=(18 if both else 12) * rows * width * hidden,
            bytes_accessed=12 * width * hidden + 8 * rows * hidden,
            transcendentals=rows * hidden,
        ),
    )(flags, *received, order, *([] if both else [gate, up]), *gates, *ups, *downs)
    return halves, back


def product_kernel(x_ref, g_ref, *refs):
    thin_ref = refs[0] if len(refs) == 3 else None
    kept_ref, given_ref = refs[-2:]
    turned = x_ref[...].astype(f32).T.astype(bf16)
    half = turned.shape[0] // 2
    wide = g_ref.shape[1]
    span = turned.shape[0]
    for at in range(0, wide, span):
        part = dot_nn(turned, g_ref[:, at : at + span]).astype(bf16)
        kept_ref[:, at : at + span] = part[:half]
        given_ref[:, at : at + span] = part[half:]
    if thin_ref is not None:
        kept_ref[:, wide:] = thin_ref[:half]
        given_ref[:, wide:] = thin_ref[half:]


def weight_product(x, grad, thin=None):
    rows, width = x.shape
    wide = grad.shape[1] + (0 if thin is None else thin.shape[1])
    shape = jax.ShapeDtypeStruct((width // 2, wide), bf16)
    vmem = pl.BlockSpec(memory_space=pltpu.VMEM)
    return pl.pallas_call(
        product_kernel,
        in_specs=[vmem] * (2 if thin is None else 3),
        out_specs=[vmem] * 2,
        out_shape=[shape] * 2,
        compiler_params=pltpu.CompilerParams(vmem_limit_bytes=VMEM_LIMIT),
        cost_estimate=pl.CostEstimate(
            flops=2 * rows * width * wide,
            bytes_accessed=2 * (width * wide + rows * (width + wide)),
            transcendentals=0,
        ),
    )(x, grad, *([] if thin is None else [thin]))


def lanes_of(rows):
    return lax.broadcasted_iota(jnp.int32, (rows, LANES), 1)


def two_part_nn(a, b):
    top = a.astype(bf16)
    return dot_nn(top, b) + dot_nn((a - top.astype(f32)).astype(bf16), b)


def two_part_nt(a, b):
    top = a.astype(bf16)
    return dot_nt(top, b) + dot_nt((a - top.astype(f32)).astype(bf16), b)


def root_scale(x):
    return lax.rsqrt(jnp.mean(x * x, axis=1, keepdims=True) + norm_eps)


def line_of(small_ref, at):
    return small_ref[...].astype(f32).T[at : at + 1]


def norm_kernel(x_ref, small_ref, out_ref, line_ref):
    @pl.when(pl.program_id(0) == 0)
    def _():
        line_ref[...] = line_of(small_ref, AT_ATTN)

    x = x_ref[...].astype(f32)
    out_ref[...] = (x * root_scale(x) * line_ref[...]).astype(bf16)


def norm_rows(x, packed):
    count, width = x.shape
    tile = min(count, 512)
    spec = pl.BlockSpec((tile, width), lambda i: (i, 0))
    return pl.pallas_call(
        norm_kernel,
        grid=(count // tile,),
        in_specs=[spec, pl.BlockSpec((width, LANES), lambda i: (0, 3 * width // LANES))],
        out_specs=spec,
        out_shape=jax.ShapeDtypeStruct((count, width), bf16),
        scratch_shapes=[pltpu.VMEM((1, width), f32)],
        compiler_params=kernel_params(1),
        cost_estimate=pl.CostEstimate(
            flops=8 * count * width, bytes_accessed=4 * count * width, transcendentals=0
        ),
    )(x, packed)


def pair_partner(x):
    lane = lanes_of(x.shape[0])
    return jnp.where(lane % 2 == 0, pltpu.roll(x, LANES - 1, 1), pltpu.roll(x, 1, 1))


def side_weights(chances, mixes, chosen):
    weight = chances * chosen
    last = [pick_column(weight, 9 + at) for at in range(3)]
    mix = [pick_column(mixes, AT_CONST + at) for at in range(4)]
    alpha = last[0] + last[1] * mix[0] + last[2] * mix[2]
    return last, mix, alpha, (last[1] * mix[1], last[2] * mix[3])


def slots_of_grad(grad, chances, picks, slot_pairs):
    parts = [jnp.sum(chances * pick, axis=1, keepdims=True) * grad for pick in picks]
    return dot_nn(slot_pairs, jnp.concatenate(parts, axis=0).astype(bf16)).astype(bf16)


def to_expert_kernel(
    final,
    att_ref,
    hidden_ref,
    wout_ref,
    small_ref,
    previous_ref,
    slot_tokens_ref,
    order_ref,
    *refs,
):
    if final:
        grad_ref, first_ref, second_ref, slot_pairs_ref = refs[:4]
        refs = refs[4:]
    mid_ref, logit_ref, chance_ref, mix_ref, message_ref = refs
    mid = hidden_ref[...] + dot_nn(att_ref[...].astype(bf16), wout_ref[...])
    mid_ref[...] = mid
    low = (mid * root_scale(mid) * line_of(small_ref, AT_MOE)).astype(bf16)
    thin = dot_nn(low, small_ref[...])
    lane = lanes_of(mid.shape[0])
    logits = jnp.where(lane < ROUTED, thin + previous_ref[...], 0.0)
    logit_ref[...] = logits
    top = jnp.max(jnp.where(lane < ROUTED, logits, masked_score), axis=1, keepdims=True)
    expo = jnp.where(lane < ROUTED, jnp.exp(logits - top), 0.0)
    chances = expo / jnp.sum(expo, axis=1, keepdims=True)
    chance_ref[...] = chances
    inside = (lane >= AT_CONST) & (lane < AT_CONST + 4)
    apart = jnp.where(inside, thin - pair_partner(thin), 0.0)
    mix_ref[...] = jnp.where(inside, jax.nn.sigmoid(apart), 0.0)
    width = mid.shape[1]
    moved = dot_nn(low, order_ref[...]).astype(bf16)
    message_ref[:, :width] = dot_nn(slot_tokens_ref[...], moved).astype(bf16)
    if final:
        message_ref[:, width:] = slots_of_grad(
            grad_ref[...].astype(f32),
            chances,
            (first_ref[...], second_ref[...]),
            slot_pairs_ref[...],
        )


def from_expert_kernel(
    final, mid_ref, chance_ref, mix_ref, first_ref, second_ref, small_ref, pair_slots_ref, back_ref, *refs
):
    if final:
        (out_ref,) = refs
    else:
        next_ref, out_ref, normed_ref = refs
    mid = mid_ref[...]
    rows, width = mid.shape
    picks = (first_ref[...], second_ref[...])
    chances = chance_ref[...]
    _, _, alpha, betas = side_weights(chances, mix_ref[...], picks[0] + picks[1])
    lines = small_ref[...].astype(f32).T
    out = mid + alpha * (mid * root_scale(mid) * lines[AT_MOE : AT_MOE + 1])
    out += betas[0] * lines[AT_CVEC : AT_CVEC + 1] + betas[1] * lines[AT_CVEC + 1 : AT_CVEC + 2]
    pairs = dot_nn(pair_slots_ref[...], back_ref[...])
    for at in range(TOP):
        picked = jnp.sum(chances * picks[at], axis=1, keepdims=True)
        out += picked * pairs[at * rows : (at + 1) * rows]
    out_ref[...] = out.astype(out_ref.dtype)
    if not final:
        normed_ref[...] = (out * root_scale(out) * line_of(next_ref, AT_ATTN)).astype(bf16)


def rms_back_rows(values, gain, grad):
    scale = root_scale(values)
    inner = grad * gain
    along = jnp.mean(inner * values, axis=1, keepdims=True)
    gain_grad = jnp.sum(grad * values * scale, axis=0, keepdims=True)
    return scale * inner - values * (scale * scale * scale * along), gain_grad


def to_attention_kernel(
    grad_ref,
    mid_ref,
    chance_ref,
    mix_ref,
    first_ref,
    second_ref,
    small_ref,
    pair_slots_ref,
    token_slots_ref,
    back_ref,
    in_back_ref,
    next_ref,
    wout_ref,
    att_ref,
    total_ref,
    head_ref,
    mid_grad_ref,
    mid_low_ref,
    sent_ref,
    delta_ref,
    thin_grad_ref,
    thin_w_ref,
    line_grad_ref,
):
    grad, mid = grad_ref[...].astype(f32), mid_ref[...]
    rows, width = mid.shape
    picks = (first_ref[...], second_ref[...])
    chosen = picks[0] + picks[1]
    chances, mixes = chance_ref[...], mix_ref[...]
    last, mix, alpha, betas = side_weights(chances, mixes, chosen)
    lines = small_ref[...].astype(f32).T
    gain = lines[AT_MOE : AT_MOE + 1]
    cvecs = [lines[AT_CVEC + c : AT_CVEC + 1 + c] for c in range(2)]
    mixed = mid * root_scale(mid) * gain
    pairs = dot_nn(pair_slots_ref[...], back_ref[...])
    along = jnp.sum(grad * mixed, axis=1, keepdims=True)
    across = [jnp.sum(grad * cvecs[c], axis=1, keepdims=True) for c in range(2)]
    lane = lanes_of(rows)
    chance_grad = jnp.where(lane == 9, along, 0.0)
    for c in range(2):
        both = mix[2 * c] * along + mix[2 * c + 1] * across[c]
        chance_grad = jnp.where(lane == 10 + c, both, chance_grad)
    chance_grad *= chosen
    for at in range(TOP):
        part = jnp.sum(grad * pairs[at * rows : (at + 1) * rows], axis=1, keepdims=True)
        chance_grad += picks[at] * part
    logit_grad = chances * (
        chance_grad - jnp.sum(chances * chance_grad, axis=1, keepdims=True)
    ) + jnp.where(lane < ROUTED, next_ref[...], 0.0)
    mix_grad = jnp.zeros_like(mixes)
    for c in range(2):
        mix_grad = jnp.where(lane == AT_CONST + 2 * c, last[1 + c] * along, mix_grad)
        mix_grad = jnp.where(lane == AT_CONST + 2 * c + 1, last[1 + c] * across[c], mix_grad)
    product = mixes * mix_grad
    thin_grad = logit_grad + mixes * (mix_grad - (product + pair_partner(product)))
    thin_grad_ref[...] = thin_grad
    low_grad = (
        alpha * grad
        + two_part_nt(thin_grad, small_ref[...])
        + dot_nn(token_slots_ref[...], in_back_ref[...])
    )
    mid_part, gain_grad = rms_back_rows(mid, gain, low_grad)
    mid_grad = grad + mid_part
    mid_grad_ref[...] = mid_grad
    mid_low = mid_grad.astype(bf16)
    mid_low_ref[...] = mid_low
    att_grad = dot_nt(mid_low, wout_ref[...]).astype(bf16)
    delta = two_part_nn(att_grad.astype(f32) * att_ref[...], head_ref[...])
    delta_ref[...] = delta
    sent_ref[:, :width] = att_grad
    stats = jnp.zeros((rows, LANES), f32)
    for at, stat in enumerate((total_ref[...], delta)):
        top = stat.astype(bf16).astype(f32)
        for part, piece in enumerate((top, stat - top)):
            place = 32 * at + 16 * part
            stats += pltpu.roll(piece, place, 1) if place else piece
    sent_ref[:, width:] = stats.astype(bf16)
    turned = mixed.T.astype(bf16)
    thin_w_ref[...] = two_part_tn(turned, thin_grad)
    line_grad_ref[...] = jnp.concatenate(
        [gain_grad]
        + [jnp.sum(betas[c] * grad, axis=0, keepdims=True) for c in range(2)]
        + [jnp.zeros((5, width), f32)],
        axis=0,
    )


def two_part_tn(turned, x):
    top = x.astype(bf16)
    return dot_nn(turned, top) + dot_nn(turned, (x - top.astype(f32)).astype(bf16))


def from_attention_kernel(final, q_ref, k_ref, v_ref, wq_ref, wk_ref, wv_ref, hidden_ref, small_ref, mid_grad_ref, *refs):
    if final:
        grad_ref, line_grad_ref = refs
    else:
        chance_ref, first_ref, second_ref, slot_pairs_ref, grad_ref, line_grad_ref, message_ref = refs
    normed_grad = dot_nt(q_ref[...], wq_ref[...])
    normed_grad += dot_nt(k_ref[...], wk_ref[...])
    normed_grad += dot_nt(v_ref[...], wv_ref[...])
    part, gain_grad = rms_back_rows(
        hidden_ref[...], line_of(small_ref, AT_ATTN), normed_grad
    )
    grad = mid_grad_ref[...] + part
    grad_ref[...] = grad
    line_grad_ref[...] = jnp.concatenate(
        [gain_grad, jnp.zeros((7, gain_grad.shape[1]), f32)], axis=0
    )
    if not final:
        message_ref[...] = slots_of_grad(
            grad, chance_ref[...], (first_ref[...], second_ref[...]), slot_pairs_ref[...]
        )


class Block:
    def __init__(self, array, wide, at):
        self.array, self.wide, self.at = array, wide, at


def run_fused(kernel, args, outs, flops):
    arrays, specs = [], []
    for arg in args:
        if isinstance(arg, Block):
            arrays.append(arg.array)
            specs.append(
                pl.BlockSpec(
                    (arg.array.shape[0], arg.wide),
                    functools.partial(lambda at, i: (0, at), arg.at),
                )
            )
        else:
            arrays.append(arg)
            specs.append(pl.BlockSpec(arg.shape, lambda i: (0, 0)))
    return pl.pallas_call(
        kernel,
        grid=(1,),
        in_specs=specs,
        out_specs=[pl.BlockSpec(shape, lambda i: (0, 0)) for shape, _ in outs],
        out_shape=[jax.ShapeDtypeStruct(shape, dtype) for shape, dtype in outs],
        compiler_params=kernel_params(1),
        cost_estimate=pl.CostEstimate(flops=flops, bytes_accessed=1 << 22, transcendentals=0),
    )(*arrays)


def after(x, *things):
    return lax.optimization_barrier((x,) + things)[0]


def swap(x, axis):
    return lax.ppermute(x, axis, [(0, 1), (1, 0)])


def fold(x, axis, at):
    given = lax.dynamic_index_in_dim(x, 1 - at, 1, keepdims=False)
    kept = lax.dynamic_index_in_dim(x, at, 1, keepdims=False)
    return (kept.astype(f32) + swap(given, axis).astype(f32)).astype(bf16)


def gather_rows(x, axes, fillers=()):
    far, near, core = axes[:-2], axes[-2], axes[-1]
    count = 2 ** len(far)
    found = [x]
    for step in range(1, count):
        pairs = [(at, (at + step) % count) for at in range(count)]
        found.append(lax.ppermute(x, far, pairs))
    blocks, filled = [], []
    for step, block in enumerate(found):
        beside = swap(block, near)
        if step < len(fillers):
            filled.append(fillers[step](beside if step == 0 else block))
        pair = jnp.concatenate([block, beside], axis=0)
        blocks += [pair, swap(pair, core)]
    rows = jnp.concatenate(blocks, axis=0)
    return (rows, filled) if fillers else rows


def gathered_order(axes):
    count = 2 ** (len(axes) - 2)
    me = lax.axis_index(axes)
    far, near, core = me // 4, me // 2 % 2, me % 2
    order = []
    for step in range(count):
        for other_core in range(2):
            for other_near in range(2):
                order.append(
                    (far - step) % count * 4 + (near ^ other_near) * 2 + (core ^ other_core)
                )
    return jnp.stack(order).astype(jnp.int32)


def shards(
    axes,
    tokens,
    prev_logits,
    routes,
    order,
    deal,
    w_qkv,
    w_out,
    w_gate,
    w_up,
    w_down,
    norm_attn,
    norm_moe,
    w_router,
    w_const,
    const_vec,
    grad_out,
):
    rows, width = tokens.shape[1], tokens.shape[2]
    ex_axes, sub_axes = axes[:3], axes[3:]
    every_axis = axes + (FS,)
    subs = 2 ** len(sub_axes)
    ctx_size = EXPERTS * subs
    length = rows * ctx_size
    prompt = length // 2
    cont_len = prompt // (ctx_size // 8)
    block_rows = rows // 2
    own_rows = w_qkv.shape[1]
    fs_at = lax.axis_index(FS)
    sub_at = lax.axis_index(sub_axes)

    ex_at = lax.axis_index(ex_axes)

    def deal_out(x):
        return lax.all_to_all(x, ex_axes, 0, 0, tiled=True)

    def dispatch(x):
        blocks = [x[:SLOTS]]
        for step in range(1, EXPERTS):
            block = x[step * SLOTS : (step + 1) * SLOTS]
            pairs = [(at, at ^ step) for at in range(EXPERTS)]
            blocks.append(lax.ppermute(block, ex_axes, pairs))
        return jnp.concatenate(blocks, axis=0)

    def blank(count):
        return jnp.zeros((own_rows, count), bf16)

    def fetch_packed(layer, *wait):
        mine = jnp.concatenate(
            [
                w_qkv[layer],
                w_router[layer],
                blank(AT_CONST - ROUTED),
                w_const[layer],
                blank(AT_CVEC - AT_CONST - 4),
                const_vec[layer],
                blank(AT_ATTN - AT_CVEC - 2),
                norm_attn[layer][:, None],
                norm_moe[layer][:, None],
                blank(LANES - AT_MOE - 1),
            ],
            axis=1,
        )
        return lax.all_gather(after(mine, *wait), every_axis, axis=0, tiled=True)

    by_chunks = subs == 2
    flags = jnp.stack([sub_at, fs_at]).astype(jnp.int32)[None, :]

    def move_in(member, *wait):
        moved = deal_out(after(member, *wait))
        return moved.reshape(-1, moved.shape[2]) if by_chunks else moved

    def spread(moved, *wait):
        moved = after(moved, *wait)
        if not by_chunks:
            whole = lax.all_gather(moved, sub_axes + (FS,), axis=1, tiled=True)
            return (whole.reshape(-1, whole.shape[2]),)
        across = swap(moved, FS)
        return (moved, across)

    def share(parts, *wait):
        if not by_chunks:
            return parts[0]
        moved, across = after(parts[0], *wait), parts[1]
        return (moved, across, swap(moved, sub_axes[0]), swap(across, sub_axes[0]))

    if not by_chunks:
        to_chunks = jnp.eye(width, dtype=bf16)
    else:
        place = jnp.arange(width, dtype=jnp.int32)
        chunk, inside = place // (width // 4), place % (width // 4)
        source = (
            inside // own_rows * 4 + (chunk ^ (sub_at * 2 + fs_at)).astype(jnp.int32)
        ) * own_rows + inside % own_rows
        to_chunks = (place[:, None] == source[None, :]).astype(bf16)

    tokens_all = gather_rows(tokens[0], axes)
    def fetch_out(layer, *wait):
        return lax.all_gather(after(w_out[layer], *wait), every_axis, axis=0, tiled=True)

    all_packed = [fetch_packed(0)]
    all_out = [fetch_out(0)]
    gate_moved = move_in(w_gate[0])
    up_moved = move_in(w_up[0], gate_moved)
    gate_parts = spread(gate_moved)
    down_moved = move_in(w_down[0], up_moved, *gate_parts, tokens_all)
    up_parts = spread(up_moved)
    all_experts = []

    block_order = gathered_order(axes)
    deal_pairs = deal.reshape(ctx_size, 2)
    own_blocks = jnp.sum(
        jnp.where(
            (block_order[:, None] == jnp.arange(ctx_size, dtype=jnp.int32)[None, :])[:, :, None],
            deal_pairs[None],
            0,
        ),
        axis=1,
    ).reshape(2 * ctx_size)
    all_places = (
        own_blocks[:, None] * block_rows + jnp.arange(block_rows, dtype=jnp.int32)[None, :]
    ).reshape(length)
    within = jnp.where(all_places < prompt, all_places, prompt + (all_places - prompt) % cont_len)
    all_starts = jnp.where(all_places < prompt, 0, all_places - (all_places - prompt) % cont_len)
    lane = jnp.arange(LANES, dtype=jnp.int32)
    half = HEAD_DIM // 2
    frequency = 10000.0 ** (-(lane % half).astype(f32) / half)
    angles = within.astype(f32)[:, None] * frequency[None, :]
    cosine = jnp.cos(angles)
    sine = jnp.sin(angles) * jnp.where(lane % HEAD_DIM < half, -1.0, 1.0)[None, :]
    own_cos, own_sin = cosine, sine
    own_places, own_starts = all_places[:rows, None], all_starts[:rows, None]
    place_line, start_line = all_places[None, :], all_starts[None, :]

    first_things = [tokens_all, *gate_parts, up_moved, cosine, sine]

    route_rows = routes[0]
    flat_routes = jnp.concatenate([route_rows[:, k] for k in range(TOP)])
    flat_order = jnp.concatenate([order[0].reshape(rows, TOP)[:, k] for k in range(TOP)])
    earlier = (flat_routes[None, :] == flat_routes[:, None]) & (
        flat_order[None, :] < flat_order[:, None]
    )
    slot = jnp.sum(earlier.astype(jnp.int32), axis=1)
    in_slot = (flat_routes < EXPERTS) & (slot < CAP)
    target = jnp.where(in_slot, (flat_routes ^ ex_at) * SLOTS + slot, -1)
    slot_ids = jnp.arange(EXPERTS * SLOTS, dtype=jnp.int32)
    pair_slots = (target[:, None] == slot_ids[None, :]).astype(bf16)
    slot_pairs = (slot_ids[:, None] == target[None, :]).astype(bf16)
    slot_tokens = slot_pairs[:, :rows] + slot_pairs[:, rows:]
    token_slots = pair_slots[:rows] + pair_slots[rows:]
    picks = [(route_rows[:, k : k + 1] == lane[None, :]).astype(f32) for k in range(TOP)]
    head_of = (jnp.arange(width, dtype=jnp.int32)[:, None] // HEAD_DIM == lane[None, :]).astype(
        bf16
    )

    table = (rows, LANES)
    full = (rows, width)
    core_axis = sub_axes[0]

    def join_cores(kept, given, *wait):
        part = kept.astype(f32) + swap(after(given, *wait), core_axis).astype(f32)
        if part.ndim == 3:
            half = part.shape[1] // 2
            return part[:, :half].astype(bf16), part[:, half:].astype(bf16)
        half = part.shape[0] // 2
        return part[:half].astype(bf16), part[half:].astype(bf16)

    def join_groups(pieces, *wait):
        kept, given = pieces
        part = (kept.astype(f32) + swap(after(given, *wait), FS).astype(f32)).astype(bf16)
        return part.reshape(EXPERTS, -1, part.shape[-1])

    def reduce_rows(part):
        part = part.reshape(-1, part.shape[2])
        return lax.psum_scatter(part, ex_axes, scatter_dimension=0, tiled=True)

    def scatter_whole(member):
        cut = member.astype(bf16).reshape(EXPERTS, subs * 2, -1, member.shape[1])
        part = lax.psum_scatter(cut, sub_axes + (FS,), scatter_dimension=1, tiled=True)
        return part.reshape((EXPERTS,) + part.shape[2:])

    def expert_plain_back(x, out_grad, gate_act, upward, weights):
        wgate, wup, wdown = weights
        sigma = jax.nn.sigmoid(gate_act)
        gated = gate_act * sigma
        inner = (gated * upward).astype(bf16)
        inner_grad = dot_nt(out_grad, wdown)
        up_grad = (inner_grad * gated).astype(bf16)
        gate_grad = (inner_grad * upward * (sigma + gated * (1.0 - sigma))).astype(bf16)
        in_grad = (dot_nt(gate_grad, wgate) + dot_nt(up_grad, wup)).astype(bf16)
        products = (dot_tn(x, gate_grad), dot_tn(x, up_grad), dot_tn(inner, out_grad))
        return [scatter_whole(member) for member in products], in_grad

    def expert_plain(x, weights):
        wgate, wup, wdown = weights
        gate_act, upward = dot_nn(x, wgate), dot_nn(x, wup)
        inner = (jax.nn.silu(gate_act) * upward).astype(bf16)
        return gate_act, upward, dot_nn(inner, wdown).astype(bf16)

    hidden = tokens[0].astype(f32)
    previous = jnp.pad(prev_logits[0], ((0, 0), (0, LANES - ROUTED)))
    grad = grad_out[0]
    all_packed[0] = after(all_packed[0], *first_things, slot_tokens, previous)
    saved_all = []
    for layer in range(LAYERS):
        final = layer == LAYERS - 1
        packed = all_packed[layer]
        if layer == 0:
            normed_all = norm_rows(tokens_all, packed)
            normed = normed_all[:rows]
        else:
            up_moved = move_in(w_up[layer], normed)
            normed_all = gather_rows(normed, axes)
            normed_all = after(normed_all, *gate_parts, up_moved)
            down_moved = move_in(w_down[layer], normed_all)
            up_parts = spread(up_moved, normed_all)
        normed_used = normed
        all_queries, keys, values = project(
            normed_all, packed, (0, 1, 2), (True, True, False), cosine, sine
        )
        queries = all_queries
        if layer == 0:
            all_packed.append(fetch_packed(1, keys))
            all_out.append(fetch_out(1, keys))
        attended, totals = attend(
            queries, keys, values, own_places, own_starts, place_line, prompt
        )
        if final:
            attended = after(attended, down_moved, *up_parts)
        down_parts = spread(down_moved)
        small = Block(packed, LANES, 3 * width // LANES)
        wout = all_out[layer]
        midway, logits, chances, mixing, slot_in = run_fused(
            functools.partial(to_expert_kernel, final),
            [attended, hidden, wout, small, previous, slot_tokens, to_chunks]
            + ([grad, picks[0], picks[1], slot_pairs] if final else []),
            [
                (full, f32),
                (table, f32),
                (table, f32),
                (table, f32),
                ((EXPERTS * SLOTS, (2 if final else 1) * width), bf16),
            ],
            6 * rows * width * width,
        )
        if layer == 0:
            slot_in = after(slot_in, down_moved, *up_parts)
        expert_in = dispatch(slot_in)
        weights = [share(parts, slot_in) for parts in (gate_parts, up_parts, down_parts)]
        if not final:
            next_gate = move_in(w_gate[layer + 1], expert_in)
        gate_act = upward = halves = None
        if by_chunks and final:
            halves, expert_out = run_expert_back(
                flags, (expert_in, expert_in), to_chunks, None, None, *weights
            )
        elif by_chunks:
            gate_act, upward, expert_out = run_expert(flags, expert_in, *weights)
        elif final:
            half_in, half_grad = expert_in[:, :width], expert_in[:, width:]
            gate_act, upward, expert_out = expert_plain(half_in, weights)
            halves, in_grad = expert_plain_back(half_in, half_grad, gate_act, upward, weights)
            expert_out = jnp.concatenate([in_grad, expert_out], axis=1)
        else:
            gate_act, upward, expert_out = expert_plain(expert_in, weights)
        if not final:
            expert_out = after(expert_out, next_gate)
            gate_parts = spread(next_gate, expert_out)
        back = dispatch(expert_out)
        in_back = None
        if final:
            in_back, back = back[:, :width], back[:, width:]
        if final:
            (output_rows,) = run_fused(
                functools.partial(from_expert_kernel, True),
                [midway, chances, mixing, picks[0], picks[1], small, pair_slots, back],
                [(full, bf16)],
                2 * rows * width * EXPERTS * SLOTS,
            )
        else:
            all_packed[layer + 1] = after(all_packed[layer + 1], expert_out)
            output, normed = run_fused(
                functools.partial(from_expert_kernel, False),
                [midway, chances, mixing, picks[0], picks[1], small, pair_slots, back]
                + [Block(all_packed[layer + 1], LANES, 3 * width // LANES)],
                [(full, f32), (full, bf16)],
                2 * rows * width * EXPERTS * SLOTS,
            )
        saved_all.append(
            (
                hidden,
                normed_used,
                normed_all,
                all_queries,
                queries,
                keys,
                values,
                attended,
                totals,
                midway,
                chances,
                mixing,
                expert_in,
                gate_act,
                upward,
                halves,
                in_back,
                weights,
                back,
            )
        )
        if not final:
            hidden = output
        previous = logits

    logit_next = jnp.zeros(table, f32)
    results = [None] * LAYERS
    moved_grads = [[None] * 3 for _ in range(LAYERS)]
    out_folded = [None] * LAYERS
    for layer in reversed(range(LAYERS)):
        final = layer == LAYERS - 1
        (
            hidden,
            normed,
            normed_all,
            all_queries,
            queries,
            keys,
            values,
            attended,
            totals,
            midway,
            chances,
            mixing,
            expert_in,
            gate_act,
            upward,
            halves,
            in_back,
            weights,
            back,
        ) = saved_all[layer]
        packed = all_packed[layer]
        small = Block(packed, LANES, 3 * width // LANES)
        wout = all_out[layer]
        if not final:
            if by_chunks:
                slot_grad = after(slot_grad, moved_grads[1][1])
            out_grad = dispatch(slot_grad)
            if by_chunks:
                out_grad = after(out_grad, *qkv_joined)
                moved_grads[1][2] = deal_out(after(folded[1][2], out_grad))
                halves, in_grad = run_expert_back(
                    flags, (expert_in, out_grad), to_chunks, gate_act, upward, *weights
                )
                in_grad = after(in_grad, moved_grads[1][2])
            else:
                halves, in_grad = expert_plain_back(
                    expert_in, out_grad, gate_act, upward, weights
                )
            in_back = dispatch(in_grad)
            if by_chunks:
                in_back = after(in_back, qkv_folded, out_folded[1])
                owned = reduce_rows(
                    jnp.concatenate([out_folded[1], after(qkv_folded, in_back)], axis=2)
                )
        if final:
            folded = [None] * LAYERS
        if by_chunks:
            joined = [join_cores(halves[2 * at], halves[2 * at + 1]) for at in range(3)]
            in_back = after(in_back, *joined[0])
            folded[layer] = [join_groups(joined[at]) for at in range(3)]
        mid_grad, mid_low, sent, delta, logit_next, thin_w, line_grads = run_fused(
            to_attention_kernel,
            [grad, midway, chances, mixing, picks[0], picks[1], small, pair_slots]
            + [token_slots, back, in_back, logit_next, wout, attended, totals, head_of],
            [
                (full, f32),
                (full, bf16),
                ((rows, width + LANES), bf16),
                (table, f32),
                (table, f32),
                ((width, LANES), f32),
                ((8, width), f32),
            ],
            6 * rows * width * width,
        )
        def some_queries(start, dependence):
            return query_back(
                start,
                2,
                after(queries, dependence),
                sent,
                keys,
                values,
                totals,
                delta,
                own_places,
                own_starts,
                place_line,
                own_cos,
                own_sin,
                prompt,
            )

        sent_all, query_grads = gather_rows(
            sent, axes, [functools.partial(some_queries, start) for start in range(0, PAIRS, 2)]
        )
        late_low = after(mid_low, sent)
        if by_chunks:
            att_rel = dot_nn(attended.astype(bf16), to_chunks).astype(bf16)
            out_joined = join_cores(*weight_product(att_rel, late_low))
        else:
            out_w_grad = dot_tn(attended.astype(bf16), late_low).astype(bf16)
        query_grad = jnp.concatenate(query_grads, axis=1)
        if by_chunks:
            sent_all = after(sent_all, folded[layer][0], query_grad)
            moved_grads[layer][0] = deal_out(after(folded[layer][0], sent_all))
        key_grad, value_grad = key_back(
            keys,
            values,
            all_queries,
            sent_all,
            own_places,
            place_line,
            start_line,
            own_cos,
            own_sin,
            prompt,
        )
        if by_chunks and final:
            key_grad = after(key_grad, moved_grads[layer][0], folded[layer][1])
            moved_grads[layer][1] = deal_out(after(folded[layer][1], key_grad))
        proj_grad = jnp.concatenate([query_grad, key_grad, value_grad], axis=1)
        before = []
        if layer > 0:
            before = [saved_all[layer - 1][10], picks[0], picks[1], slot_pairs]
        grad, gain_grads, *slot_grad = run_fused(
            functools.partial(from_attention_kernel, layer == 0),
            [query_grad, key_grad, value_grad]
            + [Block(packed, width, at) for at in range(3)]
            + [hidden, small, mid_grad]
            + before,
            [(full, f32), ((8, width), f32)]
            + ([((EXPERTS * SLOTS, width), bf16)] if layer > 0 else []),
            6 * rows * width * width,
        )
        slot_grad = slot_grad[0] if slot_grad else None
        some = jnp.concatenate([gain_grads[:1], line_grads[:3]], axis=0)
        wanted = jnp.array([AT_ATTN, AT_MOE, AT_CVEC, AT_CVEC + 1], dtype=jnp.int32)
        spread_out = (wanted[:, None] == lane[None, :]).astype(f32)
        thin_part = thin_w + jnp.dot(some.T, spread_out, precision=highest)
        if by_chunks:
            out_folded[layer] = join_groups(out_joined)
        if by_chunks and final:
            thin_low = dot_tn(to_chunks, thin_part.astype(bf16)).astype(bf16)
            normed_rel = dot_nn(normed, to_chunks).astype(bf16)
            qkv_joined = join_cores(*weight_product(normed_rel, after(proj_grad, grad), thin_low))
            qkv_folded = join_groups(qkv_joined)
            continue
        share_of = 3 * width // ctx_size
        columns = proj_grad.reshape(rows, ctx_size, share_of).transpose(1, 0, 2)
        if by_chunks:
            columns = after(columns, moved_grads[0][0])
        columns = lax.all_to_all(columns, axes, 0, 0, tiled=True)
        if by_chunks:
            moved_grads[0][1] = deal_out(after(folded[0][1], columns))
        columns = jnp.take(columns, block_order, axis=0).reshape(length, share_of)
        part = jnp.concatenate([dot_tn(columns, normed_all).T, thin_part], axis=1).astype(bf16)
        part = fold(part.reshape(ctx_size, 2, own_rows, share_of + LANES), FS, fs_at)
        if by_chunks:
            part = after(part, moved_grads[0][1])
        part = lax.all_to_all(part, axes, 0, 0, tiled=True)
        if by_chunks:
            last = jnp.concatenate([folded[0][2], out_folded[0]], axis=1)
            last = deal_out(after(last, part))
            tall = folded[0][2].shape[1]
            moved_grads[0][2], last_out = last[:, :tall], last[:, tall:]
        part = part.astype(f32)
        qkv_owned = part[:, :, :share_of].transpose(1, 0, 2).reshape(own_rows, 3 * width)
        thin_owned = jnp.sum(part[:, :, share_of:], axis=0)
        if by_chunks:
            out_owned = jnp.sum(last_out.astype(f32), axis=0)
        else:
            moved_grads[layer] = [deal_out(part) for part in halves]
            out_owned = lax.psum_scatter(
                out_w_grad, every_axis, scatter_dimension=0, tiled=True
            ).astype(f32)
        results[layer] = (qkv_owned, out_owned, thin_owned)
    if by_chunks:
        owned = owned.astype(f32)
        results[1] = (owned[:, width : 4 * width], owned[:, :width], owned[:, 4 * width :])

    def stack(parts):
        return jnp.stack(parts)

    thin_all = [results[layer][2] for layer in range(LAYERS)]
    return (
        output_rows[None],
        grad[None],
        stack([results[layer][0] for layer in range(LAYERS)]),
        stack([results[layer][1] for layer in range(LAYERS)]),
        stack([moved_grads[layer][0].astype(f32) for layer in range(LAYERS)]),
        stack([moved_grads[layer][1].astype(f32) for layer in range(LAYERS)]),
        stack([moved_grads[layer][2].astype(f32) for layer in range(LAYERS)]),
        stack([thin[:, AT_ATTN] for thin in thin_all]),
        stack([thin[:, AT_MOE] for thin in thin_all]),
        stack([thin[:, :ROUTED] for thin in thin_all]),
        stack([thin[:, AT_CONST : AT_CONST + 4] for thin in thin_all]),
        stack([thin[:, AT_CVEC : AT_CVEC + 2] for thin in thin_all]),
    )


def solution(mesh):
    devices = mesh.devices
    axes = ctx_axes(devices.shape[0])
    every_axis = axes + (FS,)
    finer = Mesh(devices.reshape((2,) * len(axes) + (devices.shape[1],)), every_axis)
    token_spec = P(FS, axes, None)
    row_spec = P(None, every_axis, None)
    expert_spec = P(None, None, every_axis, None)
    gain_spec = P(None, every_axis)
    return jax.shard_map(
        functools.partial(shards, axes),
        mesh=finer,
        in_specs=(
            token_spec,
            token_spec,
            token_spec,
            P(FS, axes),
            P(),
            row_spec,
            row_spec,
            expert_spec,
            expert_spec,
            expert_spec,
            gain_spec,
            gain_spec,
            row_spec,
            row_spec,
            row_spec,
            token_spec,
        ),
        out_specs=(
            token_spec,
            token_spec,
            row_spec,
            row_spec,
            expert_spec,
            expert_spec,
            expert_spec,
            gain_spec,
            gain_spec,
            row_spec,
            row_spec,
            row_spec,
        ),
        check_vma=False,
    )
```

```python
import functools

import jax
import jax.numpy as jnp
from jax import lax
from jax.experimental import pallas as pl
from jax.experimental.pallas import tpu as pltpu
from jax.sharding import Mesh
from jax.sharding import PartitionSpec as P

HEADS = 12
HEAD_DIM = 64
EXPERTS = 8
TOP = 2
LAYERS = 2
ROUTED = 12
CAP = 26
SLOTS = 32
LANES = 128
PAIRS = HEADS // 2

FS = "fsdp"


def ctx_axes(size):
    return tuple(f"ctx{at}" for at in range(size.bit_length() - 1))


norm_eps = 1e-06
masked_score = -1e30
highest = lax.Precision.HIGHEST
f32 = jnp.float32
bf16 = jnp.bfloat16
VMEM_LIMIT = 56 * 1024 * 1024
SPLIT = 3

AT_CONST = 16
AT_CVEC = 24
AT_ATTN = 32
AT_MOE = 33


def dot_nn(a, b):
    return lax.dot_general(a, b, (((1,), (0,)), ((), ())), preferred_element_type=f32)


def dot_nt(a, b):
    return lax.dot_general(a, b, (((1,), (1,)), ((), ())), preferred_element_type=f32)


def dot_tn(a, b):
    return lax.dot_general(a, b, (((0,), (0,)), ((), ())), preferred_element_type=f32)


def kernel_params(steps):
    return pltpu.CompilerParams(
        dimension_semantics=("arbitrary",) * steps, vmem_limit_bytes=VMEM_LIMIT
    )


def turn_lanes(x, cosine, sine):
    lane = lax.broadcasted_iota(jnp.int32, x.shape, 1)
    ahead = pltpu.roll(x, LANES - HEAD_DIM // 2, 1)
    behind = pltpu.roll(x, HEAD_DIM // 2, 1)
    partner = jnp.where(lane % HEAD_DIM < HEAD_DIM // 2, ahead, behind)
    return x * cosine + partner * sine


def once(shape, index):
    return pl.BlockSpec(shape, index, pipeline_mode=pl.Buffered(1))


def project_kernel(turned, count, fresh, *refs):
    w_ref, small_ref, cos_ref, sin_ref, out_ref = refs[count : count + 5]
    sources = [(ref, 0, ref.shape[0]) for ref in refs[:count]]
    if fresh:
        low_ref = refs[count + 5]

        @pl.when(pl.program_id(0) == 0)
        def _():
            line = line_of(small_ref, AT_ATTN)
            start = 0
            for ref, _, tall in sources:
                x = ref[...].astype(f32)
                low_ref[start : start + tall] = (x * root_scale(x) * line).astype(bf16)
                start += tall

        sources = [(low_ref, 0, low_ref.shape[0])]
    weights = w_ref[...]

    def walk(turn):
        start = 0
        for a_ref, _, whole in sources:
            for low in range(0, whole, 256):
                tall = min(256, whole - low)
                acc = dot_nn(a_ref[low : low + tall], weights)
                place = slice(start + low, start + low + tall)
                for at in range(0, acc.shape[1], LANES):
                    part = acc[:, at : at + LANES]
                    if turn:
                        part = turn_lanes(part, cos_ref[place], sin_ref[place])
                    out_ref[place, at : at + LANES] = part.astype(bf16)
            start += whole

    @pl.when(pl.program_id(0) < turned)
    def _():
        walk(True)

    @pl.when(pl.program_id(0) >= turned)
    def _():
        walk(False)


def project(blocks, packed, cosine, sine, fresh=False):
    width = blocks[0].shape[1]
    count = sum(block.shape[0] for block in blocks)
    tile = width // SPLIT
    table = once((count, LANES), lambda i: (0, 0))
    return pl.pallas_call(
        functools.partial(project_kernel, 2 * SPLIT, len(blocks), fresh),
        grid=(3 * SPLIT,),
        in_specs=[once(block.shape, lambda i: (0, 0)) for block in blocks]
        + [pl.BlockSpec((width, tile), lambda i: (0, i))]
        + [once((width, LANES), lambda i: (0, 4 * width // LANES)), table, table],
        out_specs=pl.BlockSpec((count, tile), lambda i: (0, i)),
        out_shape=jax.ShapeDtypeStruct((count, 3 * width), bf16),
        scratch_shapes=[pltpu.VMEM((count, width), bf16)] if fresh else [],
        compiler_params=kernel_params(1),
        cost_estimate=pl.CostEstimate(
            flops=6 * count * width * width,
            bytes_accessed=2 * width * (4 * count + 3 * width),
            transcendentals=0,
        ),
    )(*blocks, packed, packed, cosine, sine)


def split_heads(x):
    wide = x.astype(f32)
    left = lax.broadcasted_iota(jnp.int32, wide.shape, 1) < HEAD_DIM
    zero = jnp.zeros_like(wide)
    return jnp.concatenate(
        [jnp.where(left, wide, zero), jnp.where(left, zero, wide)], axis=0
    ).astype(bf16)


def join_heads(x, rows):
    left = lax.broadcasted_iota(jnp.int32, (rows, LANES), 1) < HEAD_DIM
    return jnp.where(left, x[:rows], x[rows:])


def attend_kernel(
    prompt, q_ref, k_ref, v_ref, at_ref, start_ref, key_ref, o_ref, total_ref, bias_ref
):
    pair = pl.program_id(0)
    rows = q_ref.shape[0]

    @pl.when(pair == 0)
    def _():
        places, keys = at_ref[...], key_ref[...]
        seen = (keys <= places) & ((keys < prompt) | (keys >= start_ref[...]))
        bias_ref[...] = jnp.where(seen, 0.0, masked_score)
        total_ref[...] = jnp.zeros_like(total_ref)

    queries = split_heads(q_ref[...] * HEAD_DIM ** (-0.5))
    keys, values = k_ref[...], v_ref[...]
    lane = lax.broadcasted_iota(jnp.int32, (rows, LANES), 1)
    outs = []
    totals = total_ref[...]
    for side in range(2):
        scores = dot_nt(queries[side * rows : (side + 1) * rows], keys) + bias_ref[...]
        top = jnp.max(scores, axis=1, keepdims=True)
        expo = jnp.exp(scores - top)
        total = jnp.sum(expo, axis=1, keepdims=True)
        outs.append(dot_nn(expo.astype(bf16), values) / total)
        totals = jnp.where(lane == 2 * pair + side, top + jnp.log(total), totals)
    o_ref[...] = jnp.where(lane < HEAD_DIM, outs[0], outs[1])
    total_ref[...] = totals


def attend(projected, places, starts, key_places, prompt):
    rows = places.shape[0]
    length, width = projected.shape[0], projected.shape[1] // 3
    own = pl.BlockSpec((rows, LANES), lambda j: (0, j))
    keys = pl.BlockSpec((length, LANES), lambda j: (0, PAIRS + j))
    values = pl.BlockSpec((length, LANES), lambda j: (0, 2 * PAIRS + j))
    column = pl.BlockSpec((rows, 1), lambda j: (0, 0))
    line = pl.BlockSpec((1, length), lambda j: (0, 0))
    return pl.pallas_call(
        functools.partial(attend_kernel, prompt),
        grid=(PAIRS,),
        in_specs=[own, keys, values, column, column, line],
        out_specs=[own, pl.BlockSpec((rows, LANES), lambda j: (0, 0))],
        out_shape=[
            jax.ShapeDtypeStruct((rows, width), f32),
            jax.ShapeDtypeStruct((rows, LANES), f32),
        ],
        scratch_shapes=[pltpu.VMEM((rows, length), f32)],
        compiler_params=kernel_params(1),
        cost_estimate=pl.CostEstimate(
            flops=8 * rows * length * width,
            bytes_accessed=4 * length * width,
            transcendentals=rows * length * HEADS,
        ),
    )(projected, projected, projected, places, starts, key_places)


def pick_column(table, at):
    lane = lax.broadcasted_iota(jnp.int32, table.shape, 1)
    return jnp.sum(jnp.where(lane == at, table, 0.0), axis=1, keepdims=True)


def query_kernel(
    prompt,
    start,
    q_ref,
    g_ref,
    k_ref,
    v_ref,
    total_ref,
    delta_ref,
    at_ref,
    start_ref,
    key_ref,
    cos_ref,
    sin_ref,
    out_ref,
    bias_ref,
):
    pair = pl.program_id(0) + start
    rows = q_ref.shape[0]

    @pl.when(pair == start)
    def _():
        places, keys = at_ref[...], key_ref[...]
        seen = (keys <= places) & ((keys < prompt) | (keys >= start_ref[...]))
        bias_ref[...] = jnp.where(seen, 0.0, masked_score)

    scale = HEAD_DIM ** (-0.5)
    queries = split_heads(q_ref[...] * scale)
    grads = split_heads(g_ref[...])
    keys, values = k_ref[...], v_ref[...]
    lane = lax.broadcasted_iota(jnp.int32, (rows, LANES), 1)
    outs = []
    for side in range(2):
        part = slice(side * rows, (side + 1) * rows)
        total = pick_column(total_ref[...], 2 * pair + side)
        delta = pick_column(delta_ref[...], 2 * pair + side)
        scores = dot_nt(queries[part], keys) + bias_ref[...]
        probs = jnp.exp(scores - total)
        prob_grad = dot_nt(grads[part], values)
        score_grad = (probs * (prob_grad - delta)).astype(bf16)
        outs.append(dot_nn(score_grad, keys))
    out = jnp.where(lane < HEAD_DIM, outs[0], outs[1]) * scale
    out_ref[...] = turn_lanes(out, cos_ref[...], -sin_ref[...]).astype(bf16)


def query_back(
    start, count, projected, grads, totals, delta, places, starts, key_places, cosine, sine, prompt
):
    rows = places.shape[0]
    length = projected.shape[0]
    own = pl.BlockSpec((rows, LANES), lambda j: (0, j + start))
    keys = pl.BlockSpec((length, LANES), lambda j: (0, PAIRS + j + start))
    values = pl.BlockSpec((length, LANES), lambda j: (0, 2 * PAIRS + j + start))
    same = pl.BlockSpec((rows, LANES), lambda j: (0, 0))
    column = pl.BlockSpec((rows, 1), lambda j: (0, 0))
    line = pl.BlockSpec((1, length), lambda j: (0, 0))
    width = count * LANES
    return pl.pallas_call(
        functools.partial(query_kernel, prompt, start),
        grid=(count,),
        in_specs=[own, own, keys, values, same, same, column, column, line, same, same],
        out_specs=pl.BlockSpec((rows, LANES), lambda j: (0, j)),
        out_shape=jax.ShapeDtypeStruct((rows, width), bf16),
        scratch_shapes=[pltpu.VMEM((rows, length), f32)],
        compiler_params=kernel_params(1),
        cost_estimate=pl.CostEstimate(
            flops=12 * rows * length * width,
            bytes_accessed=4 * length * width,
            transcendentals=rows * length * HEADS,
        ),
    )(
        projected,
        grads,
        projected,
        projected,
        totals,
        delta,
        places,
        starts,
        key_places,
        cosine,
        sine,
    )


def key_kernel(prompt, count, k_ref, v_ref, q_ref, *refs):
    grad_refs, stat_refs = refs[:count], refs[count : 2 * count]
    own_ref, at_ref, start_ref, cos_ref, sin_ref = refs[2 * count : 2 * count + 5]
    dk_ref, dv_ref, bias_ref, lines_ref = refs[2 * count + 5 :]
    pair = pl.program_id(0)
    rows = k_ref.shape[0]

    @pl.when(pair == 0)
    def _():
        keys, places = own_ref[...], at_ref[...]
        seen = (keys <= places) & ((keys < prompt) | (keys >= start_ref[...]))
        bias_ref[...] = jnp.where(seen, 0.0, masked_score)
        flat = stack_rows(stat_refs).astype(f32).T
        for head in range(HEADS):
            lines_ref[head] = flat[head : head + 1] + flat[16 + head : 17 + head]
            lines_ref[16 + head] = flat[32 + head : 33 + head] + flat[48 + head : 49 + head]

    scale = HEAD_DIM ** (-0.5)
    own_keys = split_heads(k_ref[...] * scale)
    own_values = split_heads(v_ref[...])
    queries, grads = q_ref[...], stack_rows(grad_refs)
    lane = lax.broadcasted_iota(jnp.int32, (rows, LANES), 1)
    key_outs, value_outs = [], []
    for side in range(2):
        part = slice(side * rows, (side + 1) * rows)
        total = lines_ref[2 * pair + side]
        delta = lines_ref[16 + 2 * pair + side]
        scores = dot_nt(own_keys[part], queries) + bias_ref[...]
        probs = jnp.exp(scores - total)
        value_outs.append(dot_nn(probs.astype(bf16), grads))
        prob_grad = dot_nt(own_values[part], grads)
        score_grad = (probs * (prob_grad - delta)).astype(bf16)
        key_outs.append(dot_nn(score_grad, queries))
    left = lane < HEAD_DIM
    dk = jnp.where(left, key_outs[0], key_outs[1]) * scale
    dk_ref[...] = turn_lanes(dk, cos_ref[...], -sin_ref[...]).astype(bf16)
    dv_ref[...] = jnp.where(left, value_outs[0], value_outs[1]).astype(bf16)


def key_back(projected, sent, own_places, places, starts, cosine, sine, prompt):
    rows = own_places.shape[0]
    length, width = projected.shape[0], projected.shape[1] // 3
    out = pl.BlockSpec((rows, LANES), lambda j: (0, j))
    keys = pl.BlockSpec((rows, LANES), lambda j: (0, PAIRS + j))
    values = pl.BlockSpec((rows, LANES), lambda j: (0, 2 * PAIRS + j))
    every = pl.BlockSpec((length, LANES), lambda j: (0, j))
    same = pl.BlockSpec((rows, LANES), lambda j: (0, 0))
    column = pl.BlockSpec((rows, 1), lambda j: (0, 0))
    line = pl.BlockSpec((1, length), lambda j: (0, 0))
    return pl.pallas_call(
        functools.partial(key_kernel, prompt, len(sent)),
        grid=(PAIRS,),
        in_specs=[keys, values, every]
        + [pl.BlockSpec((block.shape[0], LANES), lambda j: (0, j)) for block in sent]
        + [pl.BlockSpec((block.shape[0], LANES), lambda j: (0, PAIRS)) for block in sent]
        + [column, line, line, same, same],
        out_specs=[out, out],
        out_shape=[jax.ShapeDtypeStruct((rows, width), bf16)] * 2,
        scratch_shapes=[
            pltpu.VMEM((rows, length), f32),
            pltpu.VMEM((32, 1, length), f32),
        ],
        compiler_params=kernel_params(1),
        cost_estimate=pl.CostEstimate(
            flops=16 * rows * length * width,
            bytes_accessed=4 * length * width,
            transcendentals=rows * length * HEADS,
        ),
    )(projected, projected, projected, *sent, *sent, own_places, places, starts, cosine, sine)


def cross(x, flag_ref):
    tall = x.shape[0]
    far = jnp.full((tall, LANES), flag_ref[0, 0], jnp.int32) > 0
    near = jnp.full((tall, LANES), flag_ref[0, 1], jnp.int32) > 0
    left, right = x[:, :LANES], x[:, LANES:]
    left = jnp.where(near, pltpu.roll(left, HEAD_DIM, 1), left)
    right = jnp.where(near, pltpu.roll(right, HEAD_DIM, 1), right)
    return jnp.concatenate(
        [jnp.where(far, right, left), jnp.where(far, left, right)], axis=1
    )


def stack_rows(refs):
    return jnp.concatenate([ref[...] for ref in refs], axis=0)


def expert_kernel(flag_ref, x_ref, *refs):
    gates, ups, downs = refs[:4], refs[4:8], refs[8:12]
    gate_ref, up_ref, out_ref, acc_ref = refs[12:]
    step = pl.program_id(0)
    x = x_ref[...]
    gate = dot_nn(x, stack_rows(gates))
    up = dot_nn(x, stack_rows(ups))
    gate_ref[...] = gate
    up_ref[...] = up
    inner = cross(gate * jax.nn.sigmoid(gate) * up, flag_ref).astype(bf16)
    out = dot_nn(inner, stack_rows(downs))

    @pl.when(step == 0)
    def _():
        acc_ref[...] = out

    @pl.when(step > 0)
    def _():
        acc_ref[...] += out

    @pl.when(step == pl.num_programs(0) - 1)
    def _():
        out_ref[...] = acc_ref[...].astype(bf16)


def expert_specs(width, hidden):
    tile = hidden // EXPERTS
    tall = pl.BlockSpec((width // 4, tile), lambda j: (0, j))
    flat = pl.BlockSpec((tile // 4, width), lambda j: (j, 0))
    return tile, [tall] * 8 + [flat] * 4


def run_expert(flags, x, gates, ups, downs):
    rows, width = x.shape
    hidden = gates[0].shape[1]
    tile, specs = expert_specs(width, hidden)
    whole = pl.BlockSpec((rows, width), lambda j: (0, 0))
    column = pl.BlockSpec((rows, tile), lambda j: (0, j))
    return pl.pallas_call(
        expert_kernel,
        grid=(EXPERTS,),
        in_specs=[pl.BlockSpec(memory_space=pltpu.SMEM), whole] + specs,
        out_specs=[column, column, whole],
        out_shape=[
            jax.ShapeDtypeStruct((rows, hidden), f32),
            jax.ShapeDtypeStruct((rows, hidden), f32),
            jax.ShapeDtypeStruct((rows, width), bf16),
        ],
        scratch_shapes=[pltpu.VMEM((rows, width), f32)],
        compiler_params=kernel_params(1),
        cost_estimate=pl.CostEstimate(
            flops=6 * rows * width * hidden,
            bytes_accessed=6 * width * hidden + 8 * rows * hidden,
            transcendentals=rows * hidden,
        ),
    )(flags, x, *gates, *ups, *downs)


def expert_back_kernel(both, flag_ref, x_ref, grad_ref, order_ref, *refs):
    if not both:
        gate_ref, up_ref = refs[:2]
        refs = refs[2:]
    gates, ups, downs = refs[:4], refs[4:8], refs[8:12]
    outs, back_ref = refs[12:18], refs[18]
    acc_ref, turned_ref = refs[19:21]
    step = pl.program_id(0)
    last = step == pl.num_programs(0) - 1
    width = x_ref.shape[1]

    @pl.when(step == 0)
    def _():
        turned_ref[...] = x_ref[...].astype(f32).T.astype(bf16)

    grad = grad_ref[...]
    gate_w, up_w, down_w = stack_rows(gates), stack_rows(ups), stack_rows(downs)
    if both:
        x = x_ref[...]
        gate, up = dot_nn(x, gate_w), dot_nn(x, up_w)
    else:
        gate, up = gate_ref[...], up_ref[...]
    sigma = jax.nn.sigmoid(gate)
    gated = gate * sigma
    inner = cross(gated * up, flag_ref)
    inner_grad = cross(dot_nt(grad, down_w), flag_ref)
    up_low = (inner_grad * gated).astype(bf16)
    gate_low = (inner_grad * up * (sigma + gated * (1.0 - sigma))).astype(bf16)
    parts = [dot_nt(gate_low, gate_w) + dot_nt(up_low, up_w)]
    if both:
        parts.append(dot_nn(inner.astype(bf16), down_w))
    part = jnp.concatenate(parts, axis=1) if both else parts[0]

    @pl.when(step == 0)
    def _():
        acc_ref[...] = part

    @pl.when(step > 0)
    def _():
        acc_ref[...] += part

    @pl.when(last)
    def _():
        in_low = acc_ref[:, :width].astype(bf16)
        back_ref[:, :width] = dot_nt(in_low, order_ref[...]).astype(bf16)
        if both:
            back_ref[:, width:] = acc_ref[:, width:].astype(bf16)

    turned = turned_ref[...]
    members = (
        dot_nn(turned, gate_low).astype(bf16),
        dot_nn(turned, up_low).astype(bf16),
        dot_nn(inner.T.astype(bf16), grad).astype(bf16),
    )
    for at, member in enumerate(members):
        half = member.shape[0] // 2
        outs[2 * at][...] = member[:half]
        outs[2 * at + 1][...] = member[half:]


def run_expert_back(flags, received, order, gate, up, gates, ups, downs):
    both = gate is None
    if both:
        rows, width = received[0].shape[0], received[0].shape[1] // 2
    else:
        rows, width = received[0].shape
    hidden = gates[0].shape[1]
    tile, specs = expert_specs(width, hidden)
    first = pl.BlockSpec((rows, width), lambda j: (0, 0))
    beside = pl.BlockSpec((rows, width), lambda j: (0, 1)) if both else first
    table = pl.BlockSpec((width, width), lambda j: (0, 0))
    column = pl.BlockSpec((rows, tile), lambda j: (0, j))
    tall = pl.BlockSpec((width // 2, tile), lambda j: (0, j))
    flat = pl.BlockSpec((None, tile // 2, width), lambda j: (j, 0, 0))
    tall_shape = jax.ShapeDtypeStruct((width // 2, hidden), bf16)
    flat_shape = jax.ShapeDtypeStruct((EXPERTS, tile // 2, width), bf16)
    wide = 2 * width if both else width
    *halves, back = pl.pallas_call(
        functools.partial(expert_back_kernel, both),
        grid=(EXPERTS,),
        in_specs=[pl.BlockSpec(memory_space=pltpu.SMEM), first, beside, table]
        + ([] if both else [column, column])
        + specs,
        out_specs=[tall] * 4 + [flat] * 2 + [pl.BlockSpec((rows, wide), lambda j: (0, 0))],
        out_shape=[tall_shape] * 4
        + [flat_shape] * 2
        + [jax.ShapeDtypeStruct((rows, wide), bf16)],
        scratch_shapes=[pltpu.VMEM((rows, wide), f32), pltpu.VMEM((width, rows), bf16)],
        compiler_params=kernel_params(1),
        cost_estimate=pl.CostEstimate(
            flops=(18 if both else 12) * rows * width * hidden,
            bytes_accessed=12 * width * hidden + 8 * rows * hidden,
            transcendentals=rows * hidden,
        ),
    )(flags, *received, order, *([] if both else [gate, up]), *gates, *ups, *downs)
    return halves, back


def product_kernel(x_ref, g_ref, *refs):
    thin_ref = refs[0] if len(refs) == 3 else None
    kept_ref, given_ref = refs[-2:]
    turned = x_ref[...].astype(f32).T.astype(bf16)
    half = turned.shape[0] // 2
    wide = g_ref.shape[1]
    span = turned.shape[0]
    for at in range(0, wide, span):
        part = dot_nn(turned, g_ref[:, at : at + span]).astype(bf16)
        kept_ref[:, at : at + span] = part[:half]
        given_ref[:, at : at + span] = part[half:]
    if thin_ref is not None:
        kept_ref[:, wide:] = thin_ref[:half]
        given_ref[:, wide:] = thin_ref[half:]


def weight_product(x, grad, thin=None):
    rows, width = x.shape
    wide = grad.shape[1] + (0 if thin is None else thin.shape[1])
    shape = jax.ShapeDtypeStruct((width // 2, wide), bf16)
    vmem = pl.BlockSpec(memory_space=pltpu.VMEM)
    return pl.pallas_call(
        product_kernel,
        in_specs=[vmem] * (2 if thin is None else 3),
        out_specs=[vmem] * 2,
        out_shape=[shape] * 2,
        compiler_params=pltpu.CompilerParams(vmem_limit_bytes=VMEM_LIMIT),
        cost_estimate=pl.CostEstimate(
            flops=2 * rows * width * wide,
            bytes_accessed=2 * (width * wide + rows * (width + wide)),
            transcendentals=0,
        ),
    )(x, grad, *([] if thin is None else [thin]))


def lanes_of(rows):
    return lax.broadcasted_iota(jnp.int32, (rows, LANES), 1)


def two_part_nn(a, b):
    top = a.astype(bf16)
    return dot_nn(top, b) + dot_nn((a - top.astype(f32)).astype(bf16), b)


def two_part_nt(a, b):
    top = a.astype(bf16)
    return dot_nt(top, b) + dot_nt((a - top.astype(f32)).astype(bf16), b)


def root_scale(x):
    return lax.rsqrt(jnp.mean(x * x, axis=1, keepdims=True) + norm_eps)


def line_of(small_ref, at):
    return small_ref[...].astype(f32).T[at : at + 1]


def norm_kernel(*refs):
    small_ref, out_ref = refs[-2:]
    line = line_of(small_ref, AT_ATTN)
    start = 0
    for x_ref in refs[:-2]:
        tall = x_ref.shape[0]
        x = x_ref[...].astype(f32)
        out_ref[start : start + tall] = (x * root_scale(x) * line).astype(bf16)
        start += tall


def norm_rows(blocks, packed):
    width = blocks[0].shape[1]
    count = sum(block.shape[0] for block in blocks)
    return pl.pallas_call(
        norm_kernel,
        grid=(1,),
        in_specs=[once(block.shape, lambda i: (0, 0)) for block in blocks]
        + [pl.BlockSpec((width, LANES), lambda i: (0, 4 * width // LANES))],
        out_specs=once((count, width), lambda i: (0, 0)),
        out_shape=jax.ShapeDtypeStruct((count, width), bf16),
        compiler_params=kernel_params(1),
        cost_estimate=pl.CostEstimate(
            flops=8 * count * width, bytes_accessed=4 * count * width, transcendentals=0
        ),
    )(*blocks, packed)


def pair_partner(x):
    lane = lanes_of(x.shape[0])
    return jnp.where(lane % 2 == 0, pltpu.roll(x, LANES - 1, 1), pltpu.roll(x, 1, 1))


def side_weights(chances, mixes, chosen):
    weight = chances * chosen
    last = [pick_column(weight, 9 + at) for at in range(3)]
    mix = [pick_column(mixes, AT_CONST + at) for at in range(4)]
    alpha = last[0] + last[1] * mix[0] + last[2] * mix[2]
    return last, mix, alpha, (last[1] * mix[1], last[2] * mix[3])


def slots_of_grad(grad, chances, picks, slot_pairs):
    parts = [jnp.sum(chances * pick, axis=1, keepdims=True) * grad for pick in picks]
    return dot_nn(slot_pairs, jnp.concatenate(parts, axis=0).astype(bf16)).astype(bf16)


def to_expert_kernel(
    final,
    att_ref,
    hidden_ref,
    wout_ref,
    small_ref,
    previous_ref,
    slot_tokens_ref,
    order_ref,
    *refs,
):
    if final:
        grad_ref, first_ref, second_ref, slot_pairs_ref = refs[:4]
        refs = refs[4:]
    mid_ref, logit_ref, chance_ref, mix_ref, message_ref = refs
    mid = hidden_ref[...] + dot_nn(att_ref[...].astype(bf16), wout_ref[...])
    mid_ref[...] = mid
    low = (mid * root_scale(mid) * line_of(small_ref, AT_MOE)).astype(bf16)
    thin = dot_nn(low, small_ref[...])
    lane = lanes_of(mid.shape[0])
    logits = jnp.where(lane < ROUTED, thin + previous_ref[...], 0.0)
    logit_ref[...] = logits
    top = jnp.max(jnp.where(lane < ROUTED, logits, masked_score), axis=1, keepdims=True)
    expo = jnp.where(lane < ROUTED, jnp.exp(logits - top), 0.0)
    chances = expo / jnp.sum(expo, axis=1, keepdims=True)
    chance_ref[...] = chances
    inside = (lane >= AT_CONST) & (lane < AT_CONST + 4)
    apart = jnp.where(inside, thin - pair_partner(thin), 0.0)
    mix_ref[...] = jnp.where(inside, jax.nn.sigmoid(apart), 0.0)
    width = mid.shape[1]
    moved = dot_nn(low, order_ref[...]).astype(bf16)
    message_ref[:, :width] = dot_nn(slot_tokens_ref[...], moved).astype(bf16)
    if final:
        message_ref[:, width:] = slots_of_grad(
            grad_ref[...].astype(f32),
            chances,
            (first_ref[...], second_ref[...]),
            slot_pairs_ref[...],
        )


def from_expert_kernel(
    final, mid_ref, chance_ref, mix_ref, first_ref, second_ref, small_ref, pair_slots_ref, back_ref, *refs
):
    if final:
        (out_ref,) = refs
    else:
        next_ref, out_ref, normed_ref = refs
    mid = mid_ref[...]
    rows, width = mid.shape
    picks = (first_ref[...], second_ref[...])
    chances = chance_ref[...]
    _, _, alpha, betas = side_weights(chances, mix_ref[...], picks[0] + picks[1])
    lines = small_ref[...].astype(f32).T
    out = mid + alpha * (mid * root_scale(mid) * lines[AT_MOE : AT_MOE + 1])
    out += betas[0] * lines[AT_CVEC : AT_CVEC + 1] + betas[1] * lines[AT_CVEC + 1 : AT_CVEC + 2]
    pairs = dot_nn(pair_slots_ref[...], back_ref[...])
    for at in range(TOP):
        picked = jnp.sum(chances * picks[at], axis=1, keepdims=True)
        out += picked * pairs[at * rows : (at + 1) * rows]
    out_ref[...] = out.astype(out_ref.dtype)
    if not final:
        normed_ref[...] = (out * root_scale(out) * line_of(next_ref, AT_ATTN)).astype(bf16)


def rms_back_rows(values, gain, grad):
    scale = root_scale(values)
    inner = grad * gain
    along = jnp.mean(inner * values, axis=1, keepdims=True)
    gain_grad = jnp.sum(grad * values * scale, axis=0, keepdims=True)
    return scale * inner - values * (scale * scale * scale * along), gain_grad


def to_attention_kernel(
    grad_ref,
    mid_ref,
    chance_ref,
    mix_ref,
    first_ref,
    second_ref,
    small_ref,
    pair_slots_ref,
    token_slots_ref,
    back_ref,
    in_back_ref,
    next_ref,
    wout_ref,
    att_ref,
    total_ref,
    head_ref,
    mid_grad_ref,
    mid_low_ref,
    sent_ref,
    delta_ref,
    thin_grad_ref,
    thin_w_ref,
    line_grad_ref,
):
    grad, mid = grad_ref[...].astype(f32), mid_ref[...]
    rows, width = mid.shape
    picks = (first_ref[...], second_ref[...])
    chosen = picks[0] + picks[1]
    chances, mixes = chance_ref[...], mix_ref[...]
    last, mix, alpha, betas = side_weights(chances, mixes, chosen)
    lines = small_ref[...].astype(f32).T
    gain = lines[AT_MOE : AT_MOE + 1]
    cvecs = [lines[AT_CVEC + c : AT_CVEC + 1 + c] for c in range(2)]
    mixed = mid * root_scale(mid) * gain
    pairs = dot_nn(pair_slots_ref[...], back_ref[...])
    along = jnp.sum(grad * mixed, axis=1, keepdims=True)
    across = [jnp.sum(grad * cvecs[c], axis=1, keepdims=True) for c in range(2)]
    lane = lanes_of(rows)
    chance_grad = jnp.where(lane == 9, along, 0.0)
    for c in range(2):
        both = mix[2 * c] * along + mix[2 * c + 1] * across[c]
        chance_grad = jnp.where(lane == 10 + c, both, chance_grad)
    chance_grad *= chosen
    for at in range(TOP):
        part = jnp.sum(grad * pairs[at * rows : (at + 1) * rows], axis=1, keepdims=True)
        chance_grad += picks[at] * part
    logit_grad = chances * (
        chance_grad - jnp.sum(chances * chance_grad, axis=1, keepdims=True)
    ) + jnp.where(lane < ROUTED, next_ref[...], 0.0)
    mix_grad = jnp.zeros_like(mixes)
    for c in range(2):
        mix_grad = jnp.where(lane == AT_CONST + 2 * c, last[1 + c] * along, mix_grad)
        mix_grad = jnp.where(lane == AT_CONST + 2 * c + 1, last[1 + c] * across[c], mix_grad)
    product = mixes * mix_grad
    thin_grad = logit_grad + mixes * (mix_grad - (product + pair_partner(product)))
    thin_grad_ref[...] = thin_grad
    low_grad = (
        alpha * grad
        + two_part_nt(thin_grad, small_ref[...])
        + dot_nn(token_slots_ref[...], in_back_ref[...])
    )
    mid_part, gain_grad = rms_back_rows(mid, gain, low_grad)
    mid_grad = grad + mid_part
    mid_grad_ref[...] = mid_grad
    mid_low = mid_grad.astype(bf16)
    mid_low_ref[...] = mid_low
    att_grad = dot_nt(mid_low, wout_ref[...]).astype(bf16)
    delta = two_part_nn(att_grad.astype(f32) * att_ref[...], head_ref[...])
    delta_ref[...] = delta
    sent_ref[:, :width] = att_grad
    stats = jnp.zeros((rows, LANES), f32)
    for at, stat in enumerate((total_ref[...], delta)):
        top = stat.astype(bf16).astype(f32)
        for part, piece in enumerate((top, stat - top)):
            place = 32 * at + 16 * part
            stats += pltpu.roll(piece, place, 1) if place else piece
    sent_ref[:, width:] = stats.astype(bf16)
    turned = mixed.T.astype(bf16)
    thin_w_ref[...] = two_part_tn(turned, thin_grad)
    line_grad_ref[...] = jnp.concatenate(
        [gain_grad]
        + [jnp.sum(betas[c] * grad, axis=0, keepdims=True) for c in range(2)]
        + [jnp.zeros((5, width), f32)],
        axis=0,
    )


def two_part_tn(turned, x):
    top = x.astype(bf16)
    return dot_nn(turned, top) + dot_nn(turned, (x - top.astype(f32)).astype(bf16))


def from_attention_kernel(final, *refs):
    q_refs, (k_ref, v_ref, wq_ref, wk_ref, wv_ref) = refs[:3], refs[3:8]
    hidden_ref, small_ref, mid_grad_ref = refs[8:11]
    refs = refs[11:]
    if final:
        grad_ref, line_grad_ref = refs
    else:
        chance_ref, first_ref, second_ref, slot_pairs_ref, grad_ref, line_grad_ref, message_ref = refs
    queries = jnp.concatenate([ref[...] for ref in q_refs], axis=1)
    normed_grad = dot_nt(queries, wq_ref[...])
    normed_grad += dot_nt(k_ref[...], wk_ref[...])
    normed_grad += dot_nt(v_ref[...], wv_ref[...])
    part, gain_grad = rms_back_rows(
        hidden_ref[...], line_of(small_ref, AT_ATTN), normed_grad
    )
    grad = mid_grad_ref[...] + part
    grad_ref[...] = grad
    line_grad_ref[...] = jnp.concatenate(
        [gain_grad, jnp.zeros((7, gain_grad.shape[1]), f32)], axis=0
    )
    if not final:
        message_ref[...] = slots_of_grad(
            grad, chance_ref[...], (first_ref[...], second_ref[...]), slot_pairs_ref[...]
        )


class Block:
    def __init__(self, array, wide, at):
        self.array, self.wide, self.at = array, wide, at


def run_fused(kernel, args, outs, flops):
    arrays, specs = [], []
    for arg in args:
        if isinstance(arg, Block):
            arrays.append(arg.array)
            specs.append(
                pl.BlockSpec(
                    (arg.array.shape[0], arg.wide),
                    functools.partial(lambda at, i: (0, at), arg.at),
                )
            )
        else:
            arrays.append(arg)
            specs.append(pl.BlockSpec(arg.shape, lambda i: (0, 0)))
    return pl.pallas_call(
        kernel,
        grid=(1,),
        in_specs=specs,
        out_specs=[pl.BlockSpec(shape, lambda i: (0, 0)) for shape, _ in outs],
        out_shape=[jax.ShapeDtypeStruct(shape, dtype) for shape, dtype in outs],
        compiler_params=kernel_params(1),
        cost_estimate=pl.CostEstimate(flops=flops, bytes_accessed=1 << 22, transcendentals=0),
    )(*arrays)


def after(x, *things):
    return lax.optimization_barrier((x,) + things)[0]


TABLE = {
    "a_g0": ("", ""),
    "a_u0": ("", "packed0"),
    "a_d0": ("packed0", "proj0"),
    "x_g0": ("", "packed0"),
    "x_u0": ("packed0", "proj0"),
    "x_d0": ("proj0", "ein0"),
    "c_g0": ("packed0", ""),
    "c_u0": ("proj0", ""),
    "c_d0": ("", ""),
    "k_1": ("proj0", ""),
    "a_g1": ("proj0", "msg0"),
    "a_u1": ("ein0", "eout0"),
    "a_d1": ("ag1", "att1"),
    "x_g1": ("eout0", "ag1"),
    "x_u1": ("ag1", ""),
    "x_d1": ("att1", ""),
    "c_g1": ("msg1", ""),
    "c_u1": ("msg1", ""),
    "c_d1": ("msg1", ""),
    "cj_g1": ("", ""),
    "cj_u1": ("", ""),
    "cj_d1": ("", ""),
    "xj_g1": ("", "sall1"),
    "xj_u1": ("", ""),
    "xj_d1": ("", ""),
    "p_o1": ("slot0", ""),
    "xj_o1": ("", ""),
    "r_g1": ("sall1", "key1"),
    "p_q1": ("og0", ""),
    "xj_q1": ("", "key0"),
    "r_u1": ("og0", "ig0"),
    "r_d1": ("sall0", "cols0"),
    "cj_g0": ("", ""),
    "cj_u0": ("", ""),
    "cj_d0": ("", ""),
    "xj_g0": ("", ""),
    "xj_u0": ("", ""),
    "xj_d0": ("", ""),
    "p_o0": ("sall0", ""),
    "xj_o0": ("", ""),
    "rs": ("key0", "part"),
    "r_u0": ("cols", "part0"),
    "r_d0": ("part", ""),
}


class Plan:
    def __init__(self, table):
        self.table, self.make, self.found, self.passed = table, {}, {}, {"": True}

    def add(self, name, build):
        self.make[name] = build
        if self.table[name][0] in self.passed:
            self.get(name)

    def get(self, name):
        if name not in self.found:
            self.found[name] = self.make[name](lambda x: x)
        return self.found[name]

    def point(self, at, value):
        done = []
        for name, (_, end) in self.table.items():
            if end == at and name in self.make:
                done += jax.tree.leaves(self.get(name))
        if done:
            value = after(value, *done)
        self.passed[at] = True
        for name, (start, _) in self.table.items():
            if start == at and name in self.make and name not in self.found:
                self.found[name] = self.make[name](lambda x: after(x, value))
        return value


def swap(x, axis):
    return lax.ppermute(x, axis, [(0, 1), (1, 0)])


def fold(x, axis, at):
    given = lax.dynamic_index_in_dim(x, 1 - at, 1, keepdims=False)
    kept = lax.dynamic_index_in_dim(x, at, 1, keepdims=False)
    return (kept.astype(f32) + swap(given, axis).astype(f32)).astype(bf16)


def gather_rows(x, axes, fillers=()):
    far, near, core = axes[:-2], axes[-2], axes[-1]
    count = 2 ** len(far)
    found = [x]
    for step in range(1, count):
        pairs = [(at, (at + step) % count) for at in range(count)]
        found.append(lax.ppermute(x, far, pairs))
    blocks, filled = [], []
    for step, block in enumerate(found):
        if 0 < step <= len(fillers):
            filled.append(fillers[step - 1](block if step > 1 else blocks[0]))
            block = after(block, filled[-1])
        pair = jnp.concatenate([block, swap(block, near)], axis=0)
        blocks += [pair, swap(pair, core)]
    return (blocks, filled) if fillers else blocks


def gathered_order(axes):
    count = 2 ** (len(axes) - 2)
    me = lax.axis_index(axes)
    far, near, core = me // 4, me // 2 % 2, me % 2
    order = []
    for step in range(count):
        for other_core in range(2):
            for other_near in range(2):
                order.append(
                    (far - step) % count * 4 + (near ^ other_near) * 2 + (core ^ other_core)
                )
    return jnp.stack(order).astype(jnp.int32)


def shards(
    axes,
    tokens,
    prev_logits,
    routes,
    order,
    deal,
    w_qkv,
    w_out,
    w_gate,
    w_up,
    w_down,
    norm_attn,
    norm_moe,
    w_router,
    w_const,
    const_vec,
    grad_out,
):
    rows, width = tokens.shape[1], tokens.shape[2]
    ex_axes, sub_axes = axes[:3], axes[3:]
    every_axis = axes + (FS,)
    subs = 2 ** len(sub_axes)
    ctx_size = EXPERTS * subs
    length = rows * ctx_size
    prompt = length // 2
    cont_len = prompt // (ctx_size // 8)
    block_rows = rows // 2
    own_rows = w_qkv.shape[1]
    fs_at = lax.axis_index(FS)
    sub_at = lax.axis_index(sub_axes)


    def deal_out(x):
        return lax.all_to_all(x, ex_axes, 0, 0, tiled=True)

    def dispatch(x):
        return deal_out(x.reshape(EXPERTS, SLOTS, -1)).reshape(x.shape)

    def blank(count):
        return jnp.zeros((own_rows, count), bf16)

    def fetch_packed(layer, tie):
        mine = jnp.concatenate(
            [
                w_qkv[layer],
                w_out[layer],
                w_router[layer],
                blank(AT_CONST - ROUTED),
                w_const[layer],
                blank(AT_CVEC - AT_CONST - 4),
                const_vec[layer],
                blank(AT_ATTN - AT_CVEC - 2),
                norm_attn[layer][:, None],
                norm_moe[layer][:, None],
                blank(LANES - AT_MOE - 1),
            ],
            axis=1,
        )
        return lax.all_gather(tie(mine), every_axis, axis=0, tiled=True)

    by_chunks = subs == 2
    flags = jnp.stack([sub_at, fs_at]).astype(jnp.int32)[None, :]

    plan = Plan(TABLE)

    def add_weight(name, member):
        plan.add(
            "a_" + name,
            lambda tie: deal_out(tie(member)).reshape(-1, member.shape[-1]),
        )
        plan.add("x_" + name, lambda tie: swap(tie(plan.get("a_" + name)), FS))
        plan.add(
            "c_" + name,
            lambda tie: (
                swap(tie(plan.get("a_" + name)), sub_axes[0]),
                swap(plan.get("x_" + name), sub_axes[0]),
            ),
        )

    def weights_of(layer):
        found = []
        for name, member in zip("gud", (w_gate, w_up, w_down)):
            if by_chunks:
                parts = [plan.get(part + name + str(layer)) for part in ("a_", "x_", "c_")]
                found.append((parts[0], parts[1]) + parts[2])
            else:
                moved = deal_out(member[layer])
                whole = lax.all_gather(moved, sub_axes + (FS,), axis=1, tiled=True)
                found.append(whole.reshape(-1, whole.shape[2]))
        return found

    if not by_chunks:
        to_chunks = jnp.eye(width, dtype=bf16)
    else:
        place = jnp.arange(width, dtype=jnp.int32)
        chunk, inside = place // (width // 4), place % (width // 4)
        source = (
            inside // own_rows * 4 + (chunk ^ (sub_at * 2 + fs_at)).astype(jnp.int32)
        ) * own_rows + inside % own_rows
        to_chunks = (place[:, None] == source[None, :]).astype(bf16)

    tokens_all = gather_rows(tokens[0], axes)
    all_packed = [fetch_packed(0, lambda x: x)]
    block_order = gathered_order(axes)
    deal_pairs = deal.reshape(ctx_size, 2)
    own_blocks = jnp.sum(
        jnp.where(
            (block_order[:, None] == jnp.arange(ctx_size, dtype=jnp.int32)[None, :])[:, :, None],
            deal_pairs[None],
            0,
        ),
        axis=1,
    ).reshape(2 * ctx_size)
    all_places = (
        own_blocks[:, None] * block_rows + jnp.arange(block_rows, dtype=jnp.int32)[None, :]
    ).reshape(length)
    within = jnp.where(all_places < prompt, all_places, prompt + (all_places - prompt) % cont_len)
    all_starts = jnp.where(all_places < prompt, 0, all_places - (all_places - prompt) % cont_len)
    lane = jnp.arange(LANES, dtype=jnp.int32)
    half = HEAD_DIM // 2
    frequency = 10000.0 ** (-(lane % half).astype(f32) / half)
    angles = within.astype(f32)[:, None] * frequency[None, :]
    cosine = jnp.cos(angles)
    sine = jnp.sin(angles) * jnp.where(lane % HEAD_DIM < half, -1.0, 1.0)[None, :]
    own_cos, own_sin = cosine, sine
    own_places, own_starts = all_places[:rows, None], all_starts[:rows, None]
    place_line, start_line = all_places[None, :], all_starts[None, :]

    if by_chunks:
        for layer in range(LAYERS):
            for name, member in zip("gud", (w_gate, w_up, w_down)):
                member = member[layer]
                if (name, layer) == ("u", 0):
                    member = after(member, cosine, sine)
                add_weight(name + str(layer), member)
    first_things = [*tokens_all, cosine, sine]

    route_rows = routes[0]
    flat_routes = jnp.concatenate([route_rows[:, k] for k in range(TOP)])
    flat_order = jnp.concatenate([order[0].reshape(rows, TOP)[:, k] for k in range(TOP)])
    earlier = (flat_routes[None, :] == flat_routes[:, None]) & (
        flat_order[None, :] < flat_order[:, None]
    )
    slot = jnp.sum(earlier.astype(jnp.int32), axis=1)
    in_slot = (flat_routes < EXPERTS) & (slot < CAP)
    target = jnp.where(in_slot, flat_routes * SLOTS + slot, -1)
    slot_ids = jnp.arange(EXPERTS * SLOTS, dtype=jnp.int32)
    pair_slots = (target[:, None] == slot_ids[None, :]).astype(bf16)
    slot_pairs = (slot_ids[:, None] == target[None, :]).astype(bf16)
    slot_tokens = slot_pairs[:, :rows] + slot_pairs[:, rows:]
    token_slots = pair_slots[:rows] + pair_slots[rows:]
    picks = [(route_rows[:, k : k + 1] == lane[None, :]).astype(f32) for k in range(TOP)]
    head_of = (jnp.arange(width, dtype=jnp.int32)[:, None] // HEAD_DIM == lane[None, :]).astype(
        bf16
    )

    table = (rows, LANES)
    full = (rows, width)
    core_axis = sub_axes[0]

    def join_cores(kept, given, *wait):
        part = kept.astype(f32) + swap(after(given, *wait), core_axis).astype(f32)
        if part.ndim == 3:
            half = part.shape[1] // 2
            return part[:, :half].astype(bf16), part[:, half:].astype(bf16)
        half = part.shape[0] // 2
        return part[:half].astype(bf16), part[half:].astype(bf16)

    def join_groups(pieces, *wait):
        kept, given = pieces
        part = (kept.astype(f32) + swap(after(given, *wait), FS).astype(f32)).astype(bf16)
        return part.reshape(EXPERTS, -1, part.shape[-1])

    def reduce_rows(part):
        part = part.reshape(-1, part.shape[2])
        return lax.psum_scatter(part, ex_axes, scatter_dimension=0, tiled=True)

    def add_grads(layer, halves):
        for at, name in enumerate("gud"):
            name += str(layer)
            kept, given = halves[2 * at], halves[2 * at + 1]
            plan.add(
                "cj_" + name,
                lambda tie, kept=kept, given=given: join_cores(kept, tie(given)),
            )
            plan.add(
                "xj_" + name,
                lambda tie, name=name: join_groups(
                    (plan.get("cj_" + name)[0], tie(plan.get("cj_" + name)[1]))
                ),
            )
            if name == "u0":
                plan.add(
                    "r_u0",
                    lambda tie: deal_out(
                        tie(jnp.concatenate([plan.get("xj_g0"), plan.get("xj_u0")], axis=2))
                    ),
                )
            if name not in ("g0", "u0", "d0"):
                plan.add(
                    "r_" + name, lambda tie, name=name: deal_out(tie(plan.get("xj_" + name)))
                )

    def add_out(layer, attended, mid_low):
        name = "o" + str(layer)

        def product(tie):
            att_rel = dot_nn(attended.astype(bf16), to_chunks).astype(bf16)
            return join_cores(*weight_product(att_rel, tie(mid_low)))

        plan.add("p_" + name, product)
        plan.add(
            "xj_" + name,
            lambda tie: join_groups((plan.get("p_" + name)[0], tie(plan.get("p_" + name)[1]))),
        )
        if layer == 0:
            plan.add(
                "r_d0",
                lambda tie: deal_out(
                    tie(jnp.concatenate([plan.get("xj_d0"), plan.get("xj_o0")], axis=1))
                ),
            )

    def add_qkv(thin_part, normed, proj_grad):
        def product(tie):
            thin_low = dot_tn(to_chunks, thin_part.astype(bf16)).astype(bf16)
            normed_rel = dot_nn(normed, to_chunks).astype(bf16)
            return join_cores(*weight_product(normed_rel, tie(proj_grad), thin_low))

        plan.add("p_q1", product)
        plan.add(
            "xj_q1",
            lambda tie: join_groups((plan.get("p_q1")[0], tie(plan.get("p_q1")[1]))),
        )
        plan.add(
            "rs",
            lambda tie: reduce_rows(
                jnp.concatenate([plan.get("xj_o1"), tie(plan.get("xj_q1"))], axis=2)
            ),
        )

    def scatter_whole(member):
        cut = member.astype(bf16).reshape(EXPERTS, subs * 2, -1, member.shape[1])
        part = lax.psum_scatter(cut, sub_axes + (FS,), scatter_dimension=1, tiled=True)
        return part.reshape((EXPERTS,) + part.shape[2:])

    def expert_plain_back(x, out_grad, gate_act, upward, weights):
        wgate, wup, wdown = weights
        sigma = jax.nn.sigmoid(gate_act)
        gated = gate_act * sigma
        inner = (gated * upward).astype(bf16)
        inner_grad = dot_nt(out_grad, wdown)
        up_grad = (inner_grad * gated).astype(bf16)
        gate_grad = (inner_grad * upward * (sigma + gated * (1.0 - sigma))).astype(bf16)
        in_grad = (dot_nt(gate_grad, wgate) + dot_nt(up_grad, wup)).astype(bf16)
        products = (dot_tn(x, gate_grad), dot_tn(x, up_grad), dot_tn(inner, out_grad))
        return [scatter_whole(member) for member in products], in_grad

    def expert_plain(x, weights):
        wgate, wup, wdown = weights
        gate_act, upward = dot_nn(x, wgate), dot_nn(x, wup)
        inner = (jax.nn.silu(gate_act) * upward).astype(bf16)
        return gate_act, upward, dot_nn(inner, wdown).astype(bf16)

    hidden = tokens[0].astype(f32)
    previous = jnp.pad(prev_logits[0], ((0, 0), (0, LANES - ROUTED)))
    grad = grad_out[0]
    all_packed[0] = after(all_packed[0], *first_things, slot_tokens, previous)
    all_packed[0] = plan.point("packed0", all_packed[0])
    plan.add("k_1", lambda tie: fetch_packed(1, tie))
    saved_all = []
    for layer in range(LAYERS):
        final = layer == LAYERS - 1
        packed = all_packed[layer]
        if layer == 0:
            blocks = tokens_all
            normed_all = norm_rows(tokens_all, packed)
        else:
            normed = plan.point("norm1", normed)
            blocks = gather_rows(normed, axes)
            blocks[-1] = plan.point("ag1", blocks[-1])
            normed_all = None if by_chunks else jnp.concatenate(blocks, axis=0)
        projected = project(blocks, packed, cosine, sine, layer == 0)
        projected = plan.point("proj" + str(layer), projected)
        attended, totals = attend(projected, own_places, own_starts, place_line, prompt)
        attended = plan.point("att" + str(layer), attended)
        if layer == 0:
            all_packed.append(plan.get("k_1"))
        small = Block(packed, LANES, 4 * width // LANES)
        wout = Block(packed, width, 3)
        midway, logits, chances, mixing, slot_in = run_fused(
            functools.partial(to_expert_kernel, final),
            [attended, hidden, wout, small, previous, slot_tokens, to_chunks]
            + ([grad, picks[0], picks[1], slot_pairs] if final else []),
            [
                (full, f32),
                (table, f32),
                (table, f32),
                (table, f32),
                ((EXPERTS * SLOTS, (2 if final else 1) * width), bf16),
            ],
            6 * rows * width * width,
        )
        slot_in = plan.point("msg" + str(layer), slot_in)
        expert_in = dispatch(slot_in)
        expert_in = plan.point("ein" + str(layer), expert_in)
        weights = weights_of(layer)
        gate_act = upward = halves = None
        if by_chunks and final:
            halves, expert_out = run_expert_back(
                flags, (expert_in, expert_in), to_chunks, None, None, *weights
            )
        elif by_chunks:
            gate_act, upward, expert_out = run_expert(flags, expert_in, *weights)
        elif final:
            half_in, half_grad = expert_in[:, :width], expert_in[:, width:]
            gate_act, upward, expert_out = expert_plain(half_in, weights)
            halves, in_grad = expert_plain_back(half_in, half_grad, gate_act, upward, weights)
            expert_out = jnp.concatenate([in_grad, expert_out], axis=1)
        else:
            gate_act, upward, expert_out = expert_plain(expert_in, weights)
        if by_chunks and final:
            add_grads(1, halves)
        expert_out = plan.point("eout" + str(layer), expert_out)
        back = dispatch(expert_out)
        in_back = None
        if final:
            in_back, back = back[:, :width], back[:, width:]
        if not final:
            all_packed[1] = after(all_packed[1], expert_out)
            output, normed = run_fused(
                functools.partial(from_expert_kernel, False),
                [midway, chances, mixing, picks[0], picks[1], small, pair_slots, back]
                + [Block(all_packed[layer + 1], LANES, 4 * width // LANES)],
                [(full, f32), (full, bf16)],
                2 * rows * width * EXPERTS * SLOTS,
            )
        normed_own = None if layer == 0 else blocks[0][:rows]
        saved_all.append(
            (
                hidden,
                normed_own,
                normed_all,
                projected,
                attended,
                totals,
                midway,
                chances,
                mixing,
                expert_in,
                gate_act,
                upward,
                halves,
                in_back,
                weights,
                back,
            )
        )
        if not final:
            hidden = output
        previous = logits

    logit_next = jnp.zeros(table, f32)
    results = [None] * LAYERS
    moved_grads = [[None] * 3 for _ in range(LAYERS)]
    out_folded = [None] * LAYERS
    for layer in reversed(range(LAYERS)):
        final = layer == LAYERS - 1
        (
            hidden,
            normed,
            normed_all,
            projected,
            attended,
            totals,
            midway,
            chances,
            mixing,
            expert_in,
            gate_act,
            upward,
            halves,
            in_back,
            weights,
            back,
        ) = saved_all[layer]
        packed = all_packed[layer]
        small = Block(packed, LANES, 4 * width // LANES)
        wout = Block(packed, width, 3)
        if not final:
            slot_grad = plan.point("slot0", slot_grad)
            out_grad = dispatch(slot_grad)
            out_grad = plan.point("og0", out_grad)
            if by_chunks:
                halves, in_grad = run_expert_back(
                    flags, (expert_in, out_grad), to_chunks, gate_act, upward, *weights
                )
            else:
                halves, in_grad = expert_plain_back(
                    expert_in, out_grad, gate_act, upward, weights
                )
            if by_chunks:
                add_grads(0, halves)
            in_grad = plan.point("ig0", in_grad)
            in_back = dispatch(in_grad)
            in_back = plan.point("ib0", in_back)

        mid_grad, mid_low, sent, delta, logit_next, thin_w, line_grads = run_fused(
            to_attention_kernel,
            [grad, midway, chances, mixing, picks[0], picks[1], small, pair_slots]
            + [token_slots, back, in_back, logit_next, wout, attended, totals, head_of],
            [
                (full, f32),
                (full, bf16),
                ((rows, width + LANES), bf16),
                (table, f32),
                (table, f32),
                ((width, LANES), f32),
                ((8, width), f32),
            ],
            6 * rows * width * width,
        )
        def some_queries(start, dependence):
            return query_back(
                start,
                2,
                after(projected, dependence),
                sent,
                totals,
                delta,
                own_places,
                own_starts,
                place_line,
                own_cos,
                own_sin,
                prompt,
            )

        sent = plan.point("sent" + str(layer), sent)
        if final:
            (output_rows,) = run_fused(
                functools.partial(from_expert_kernel, True),
                [midway, chances, mixing, picks[0], picks[1], small, pair_slots]
                + [after(back, sent)],
                [(full, bf16)],
                2 * rows * width * EXPERTS * SLOTS,
            )
        sent_all, query_grads = gather_rows(
            sent, axes, [functools.partial(some_queries, start) for start in range(0, PAIRS, 2)]
        )
        if by_chunks:
            add_out(layer, attended, mid_low)
        else:
            out_w_grad = dot_tn(attended.astype(bf16), mid_low).astype(bf16)
        sent_all[-1] = plan.point("sall" + str(layer), sent_all[-1])
        key_grad, value_grad = key_back(
            projected,
            sent_all,
            own_places,
            place_line,
            start_line,
            own_cos,
            own_sin,
            prompt,
        )
        key_grad = plan.point("key" + str(layer), key_grad)
        proj_grad = jnp.concatenate([*query_grads, key_grad, value_grad], axis=1)
        before = []
        if layer > 0:
            before = [saved_all[layer - 1][7], picks[0], picks[1], slot_pairs]
        grad, gain_grads, *slot_grad = run_fused(
            functools.partial(from_attention_kernel, layer == 0),
            [*query_grads, key_grad, value_grad]
            + [Block(packed, width, at) for at in range(3)]
            + [hidden, small, mid_grad]
            + before,
            [(full, f32), ((8, width), f32)]
            + ([((EXPERTS * SLOTS, width), bf16)] if layer > 0 else []),
            6 * rows * width * width,
        )
        slot_grad = slot_grad[0] if slot_grad else None
        some = jnp.concatenate([gain_grads[:1], line_grads[:3]], axis=0)
        wanted = jnp.array([AT_ATTN, AT_MOE, AT_CVEC, AT_CVEC + 1], dtype=jnp.int32)
        spread_out = (wanted[:, None] == lane[None, :]).astype(f32)
        thin_part = thin_w + jnp.dot(some.T, spread_out, precision=highest)
        if by_chunks and final:
            add_qkv(thin_part, normed, proj_grad)
            continue
        share_of = 3 * width // ctx_size
        columns = proj_grad.reshape(rows, ctx_size, share_of).transpose(1, 0, 2)
        columns = plan.point("cols0", columns)
        columns = lax.all_to_all(columns, axes, 0, 0, tiled=True)
        columns = plan.point("cols", columns)
        columns = jnp.take(columns, block_order, axis=0).reshape(length, share_of)
        part = jnp.concatenate([dot_tn(columns, normed_all).T, thin_part], axis=1).astype(bf16)
        part = fold(part.reshape(ctx_size, 2, own_rows, share_of + LANES), FS, fs_at)
        part = plan.point("part0", part)
        part = lax.all_to_all(part, axes, 0, 0, tiled=True)
        part = plan.point("part", part)
        if by_chunks:
            last = plan.get("r_d0")
            tall = plan.get("xj_d0").shape[1]
            both = plan.get("r_u0")
            wide = both.shape[2] // 2
            moved_grads[0] = [both[:, :, :wide], both[:, :, wide:], last[:, :tall]]
            moved_grads[1] = [plan.get("r_" + name + "1") for name in "gud"]
            last_out = last[:, tall:]
        part = part.astype(f32)
        qkv_owned = part[:, :, :share_of].transpose(1, 0, 2).reshape(own_rows, 3 * width)
        thin_owned = jnp.sum(part[:, :, share_of:], axis=0)
        if by_chunks:
            out_owned = jnp.sum(last_out.astype(f32), axis=0)
        else:
            moved_grads[layer] = [deal_out(part) for part in halves]
            out_owned = lax.psum_scatter(
                out_w_grad, every_axis, scatter_dimension=0, tiled=True
            ).astype(f32)
        results[layer] = (qkv_owned, out_owned, thin_owned)
    if by_chunks:
        owned = after(plan.get("rs"), last).astype(f32)
        results[1] = (owned[:, width : 4 * width], owned[:, :width], owned[:, 4 * width :])

    def stack(parts):
        return jnp.stack(parts)

    thin_all = [results[layer][2] for layer in range(LAYERS)]
    return (
        output_rows[None],
        grad[None],
        stack([results[layer][0] for layer in range(LAYERS)]),
        stack([results[layer][1] for layer in range(LAYERS)]),
        stack([moved_grads[layer][0].astype(f32) for layer in range(LAYERS)]),
        stack([moved_grads[layer][1].astype(f32) for layer in range(LAYERS)]),
        stack([moved_grads[layer][2].astype(f32) for layer in range(LAYERS)]),
        stack([thin[:, AT_ATTN] for thin in thin_all]),
        stack([thin[:, AT_MOE] for thin in thin_all]),
        stack([thin[:, :ROUTED] for thin in thin_all]),
        stack([thin[:, AT_CONST : AT_CONST + 4] for thin in thin_all]),
        stack([thin[:, AT_CVEC : AT_CVEC + 2] for thin in thin_all]),
    )


def solution(mesh):
    devices = mesh.devices
    axes = ctx_axes(devices.shape[0])
    every_axis = axes + (FS,)
    finer = Mesh(devices.reshape((2,) * len(axes) + (devices.shape[1],)), every_axis)
    token_spec = P(FS, axes, None)
    row_spec = P(None, every_axis, None)
    expert_spec = P(None, None, every_axis, None)
    gain_spec = P(None, every_axis)
    return jax.shard_map(
        functools.partial(shards, axes),
        mesh=finer,
        in_specs=(
            token_spec,
            token_spec,
            token_spec,
            P(FS, axes),
            P(),
            row_spec,
            row_spec,
            expert_spec,
            expert_spec,
            expert_spec,
            gain_spec,
            gain_spec,
            row_spec,
            row_spec,
            row_spec,
            token_spec,
        ),
        out_specs=(
            token_spec,
            token_spec,
            row_spec,
            row_spec,
            expert_spec,
            expert_spec,
            expert_spec,
            gain_spec,
            gain_spec,
            row_spec,
            row_spec,
            row_spec,
        ),
        check_vma=False,
    )
```

```python
import functools

import jax
import jax.numpy as jnp
from jax import lax
from jax.experimental import pallas as pl
from jax.experimental.pallas import tpu as pltpu
from jax.sharding import Mesh
from jax.sharding import PartitionSpec as P

HEADS = 12
HEAD_DIM = 64
EXPERTS = 8
TOP = 2
LAYERS = 2
ROUTED = 12
CAP = 26
SLOTS = 32
LANES = 128
PAIRS = HEADS // 2

FS = "fsdp"


def ctx_axes(size):
    return tuple(f"ctx{at}" for at in range(size.bit_length() - 1))


norm_eps = 1e-06
masked_score = -1e30
highest = lax.Precision.HIGHEST
f32 = jnp.float32
bf16 = jnp.bfloat16
VMEM_LIMIT = 56 * 1024 * 1024
SPLIT = 3

AT_CONST = 16
AT_CVEC = 24
AT_ATTN = 32
AT_MOE = 33


def dot_nn(a, b):
    return lax.dot_general(a, b, (((1,), (0,)), ((), ())), preferred_element_type=f32)


def dot_nt(a, b):
    return lax.dot_general(a, b, (((1,), (1,)), ((), ())), preferred_element_type=f32)


def dot_tn(a, b):
    return lax.dot_general(a, b, (((0,), (0,)), ((), ())), preferred_element_type=f32)


def kernel_params(steps):
    return pltpu.CompilerParams(
        dimension_semantics=("arbitrary",) * steps, vmem_limit_bytes=VMEM_LIMIT
    )


def turn_lanes(x, cosine, sine):
    lane = lax.broadcasted_iota(jnp.int32, x.shape, 1)
    ahead = pltpu.roll(x, LANES - HEAD_DIM // 2, 1)
    behind = pltpu.roll(x, HEAD_DIM // 2, 1)
    partner = jnp.where(lane % HEAD_DIM < HEAD_DIM // 2, ahead, behind)
    return x * cosine + partner * sine


def once(shape, index):
    return pl.BlockSpec(shape, index, pipeline_mode=pl.Buffered(1))


def project_kernel(turned, count, fresh, *refs):
    w_ref, small_ref, cos_ref, sin_ref, out_ref = refs[count : count + 5]
    sources = [(ref, 0, ref.shape[0]) for ref in refs[:count]]
    if fresh:
        low_ref = refs[count + 5]

        @pl.when(pl.program_id(0) == 0)
        def _():
            line = line_of(small_ref, AT_ATTN)
            start = 0
            for ref, _, tall in sources:
                x = ref[...].astype(f32)
                low_ref[start : start + tall] = (x * root_scale(x) * line).astype(bf16)
                start += tall

        sources = [(low_ref, 0, low_ref.shape[0])]
    weights = w_ref[...]

    def walk(turn):
        start = 0
        for a_ref, _, whole in sources:
            for low in range(0, whole, 256):
                tall = min(256, whole - low)
                acc = dot_nn(a_ref[low : low + tall], weights)
                place = slice(start + low, start + low + tall)
                for at in range(0, acc.shape[1], LANES):
                    part = acc[:, at : at + LANES]
                    if turn:
                        part = turn_lanes(part, cos_ref[place], sin_ref[place])
                    out_ref[place, at : at + LANES] = part.astype(bf16)
            start += whole

    @pl.when(pl.program_id(0) < turned)
    def _():
        walk(True)

    @pl.when(pl.program_id(0) >= turned)
    def _():
        walk(False)


def project(blocks, packed, cosine, sine, fresh=False):
    width = blocks[0].shape[1]
    count = sum(block.shape[0] for block in blocks)
    tile = width // SPLIT
    table = once((count, LANES), lambda i: (0, 0))
    return pl.pallas_call(
        functools.partial(project_kernel, 2 * SPLIT, len(blocks), fresh),
        grid=(3 * SPLIT,),
        in_specs=[once(block.shape, lambda i: (0, 0)) for block in blocks]
        + [pl.BlockSpec((width, tile), lambda i: (0, i))]
        + [once((width, LANES), lambda i: (0, 4 * width // LANES)), table, table],
        out_specs=pl.BlockSpec((count, tile), lambda i: (0, i)),
        out_shape=jax.ShapeDtypeStruct((count, 3 * width), bf16),
        scratch_shapes=[pltpu.VMEM((count, width), bf16)] if fresh else [],
        compiler_params=kernel_params(1),
        cost_estimate=pl.CostEstimate(
            flops=6 * count * width * width,
            bytes_accessed=2 * width * (4 * count + 3 * width),
            transcendentals=0,
        ),
    )(*blocks, packed, packed, cosine, sine)


def split_heads(x):
    wide = x.astype(f32)
    left = lax.broadcasted_iota(jnp.int32, wide.shape, 1) < HEAD_DIM
    zero = jnp.zeros_like(wide)
    return jnp.concatenate(
        [jnp.where(left, wide, zero), jnp.where(left, zero, wide)], axis=0
    ).astype(bf16)


def join_heads(x, rows):
    left = lax.broadcasted_iota(jnp.int32, (rows, LANES), 1) < HEAD_DIM
    return jnp.where(left, x[:rows], x[rows:])


def attend_kernel(
    prompt, q_ref, k_ref, v_ref, at_ref, start_ref, key_ref, o_ref, total_ref, bias_ref
):
    pair = pl.program_id(0)
    rows = q_ref.shape[0]

    @pl.when(pair == 0)
    def _():
        places, keys = at_ref[...], key_ref[...]
        seen = (keys <= places) & ((keys < prompt) | (keys >= start_ref[...]))
        bias_ref[...] = jnp.where(seen, 0.0, masked_score)
        total_ref[...] = jnp.zeros_like(total_ref)

    queries = split_heads(q_ref[...] * HEAD_DIM ** (-0.5))
    keys, values = k_ref[...], v_ref[...]
    lane = lax.broadcasted_iota(jnp.int32, (rows, LANES), 1)
    outs = []
    totals = total_ref[...]
    for side in range(2):
        scores = dot_nt(queries[side * rows : (side + 1) * rows], keys) + bias_ref[...]
        top = jnp.max(scores, axis=1, keepdims=True)
        expo = jnp.exp(scores - top)
        total = jnp.sum(expo, axis=1, keepdims=True)
        outs.append(dot_nn(expo.astype(bf16), values) / total)
        totals = jnp.where(lane == 2 * pair + side, top + jnp.log(total), totals)
    o_ref[...] = jnp.where(lane < HEAD_DIM, outs[0], outs[1])
    total_ref[...] = totals


def attend(projected, places, starts, key_places, prompt):
    rows = places.shape[0]
    length, width = projected.shape[0], projected.shape[1] // 3
    own = pl.BlockSpec((rows, LANES), lambda j: (0, j))
    keys = pl.BlockSpec((length, LANES), lambda j: (0, PAIRS + j))
    values = pl.BlockSpec((length, LANES), lambda j: (0, 2 * PAIRS + j))
    column = pl.BlockSpec((rows, 1), lambda j: (0, 0))
    line = pl.BlockSpec((1, length), lambda j: (0, 0))
    return pl.pallas_call(
        functools.partial(attend_kernel, prompt),
        grid=(PAIRS,),
        in_specs=[own, keys, values, column, column, line],
        out_specs=[own, pl.BlockSpec((rows, LANES), lambda j: (0, 0))],
        out_shape=[
            jax.ShapeDtypeStruct((rows, width), f32),
            jax.ShapeDtypeStruct((rows, LANES), f32),
        ],
        scratch_shapes=[pltpu.VMEM((rows, length), f32)],
        compiler_params=kernel_params(1),
        cost_estimate=pl.CostEstimate(
            flops=8 * rows * length * width,
            bytes_accessed=4 * length * width,
            transcendentals=rows * length * HEADS,
        ),
    )(projected, projected, projected, places, starts, key_places)


def pick_column(table, at):
    lane = lax.broadcasted_iota(jnp.int32, table.shape, 1)
    return jnp.sum(jnp.where(lane == at, table, 0.0), axis=1, keepdims=True)


def query_kernel(
    prompt,
    start,
    q_ref,
    g_ref,
    k_ref,
    v_ref,
    total_ref,
    delta_ref,
    at_ref,
    start_ref,
    key_ref,
    cos_ref,
    sin_ref,
    out_ref,
    bias_ref,
):
    pair = pl.program_id(0) + start
    rows = q_ref.shape[0]

    @pl.when(pair == start)
    def _():
        places, keys = at_ref[...], key_ref[...]
        seen = (keys <= places) & ((keys < prompt) | (keys >= start_ref[...]))
        bias_ref[...] = jnp.where(seen, 0.0, masked_score)

    scale = HEAD_DIM ** (-0.5)
    queries = split_heads(q_ref[...] * scale)
    grads = split_heads(g_ref[...])
    keys, values = k_ref[...], v_ref[...]
    lane = lax.broadcasted_iota(jnp.int32, (rows, LANES), 1)
    outs = []
    for side in range(2):
        part = slice(side * rows, (side + 1) * rows)
        total = pick_column(total_ref[...], 2 * pair + side)
        delta = pick_column(delta_ref[...], 2 * pair + side)
        scores = dot_nt(queries[part], keys) + bias_ref[...]
        probs = jnp.exp(scores - total)
        prob_grad = dot_nt(grads[part], values)
        score_grad = (probs * (prob_grad - delta)).astype(bf16)
        outs.append(dot_nn(score_grad, keys))
    out = jnp.where(lane < HEAD_DIM, outs[0], outs[1]) * scale
    out_ref[...] = turn_lanes(out, cos_ref[...], -sin_ref[...]).astype(bf16)


def query_back(
    start, count, projected, grads, totals, delta, places, starts, key_places, cosine, sine, prompt
):
    rows = places.shape[0]
    length = projected.shape[0]
    own = pl.BlockSpec((rows, LANES), lambda j: (0, j + start))
    keys = pl.BlockSpec((length, LANES), lambda j: (0, PAIRS + j + start))
    values = pl.BlockSpec((length, LANES), lambda j: (0, 2 * PAIRS + j + start))
    same = pl.BlockSpec((rows, LANES), lambda j: (0, 0))
    column = pl.BlockSpec((rows, 1), lambda j: (0, 0))
    line = pl.BlockSpec((1, length), lambda j: (0, 0))
    width = count * LANES
    return pl.pallas_call(
        functools.partial(query_kernel, prompt, start),
        grid=(count,),
        in_specs=[own, own, keys, values, same, same, column, column, line, same, same],
        out_specs=pl.BlockSpec((rows, LANES), lambda j: (0, j)),
        out_shape=jax.ShapeDtypeStruct((rows, width), bf16),
        scratch_shapes=[pltpu.VMEM((rows, length), f32)],
        compiler_params=kernel_params(1),
        cost_estimate=pl.CostEstimate(
            flops=12 * rows * length * width,
            bytes_accessed=4 * length * width,
            transcendentals=rows * length * HEADS,
        ),
    )(
        projected,
        grads,
        projected,
        projected,
        totals,
        delta,
        places,
        starts,
        key_places,
        cosine,
        sine,
    )


def key_kernel(prompt, count, k_ref, v_ref, q_ref, *refs):
    grad_refs, stat_refs = refs[:count], refs[count : 2 * count]
    own_ref, at_ref, start_ref, cos_ref, sin_ref = refs[2 * count : 2 * count + 5]
    dk_ref, dv_ref, bias_ref, lines_ref = refs[2 * count + 5 :]
    pair = pl.program_id(0)
    rows = k_ref.shape[0]

    @pl.when(pair == 0)
    def _():
        keys, places = own_ref[...], at_ref[...]
        seen = (keys <= places) & ((keys < prompt) | (keys >= start_ref[...]))
        bias_ref[...] = jnp.where(seen, 0.0, masked_score)
        flat = stack_rows(stat_refs).astype(f32).T
        for head in range(HEADS):
            lines_ref[head] = flat[head : head + 1] + flat[16 + head : 17 + head]
            lines_ref[16 + head] = flat[32 + head : 33 + head] + flat[48 + head : 49 + head]

    scale = HEAD_DIM ** (-0.5)
    own_keys = split_heads(k_ref[...] * scale)
    own_values = split_heads(v_ref[...])
    queries, grads = q_ref[...], stack_rows(grad_refs)
    lane = lax.broadcasted_iota(jnp.int32, (rows, LANES), 1)
    key_outs, value_outs = [], []
    for side in range(2):
        part = slice(side * rows, (side + 1) * rows)
        total = lines_ref[2 * pair + side]
        delta = lines_ref[16 + 2 * pair + side]
        scores = dot_nt(own_keys[part], queries) + bias_ref[...]
        probs = jnp.exp(scores - total)
        value_outs.append(dot_nn(probs.astype(bf16), grads))
        prob_grad = dot_nt(own_values[part], grads)
        score_grad = (probs * (prob_grad - delta)).astype(bf16)
        key_outs.append(dot_nn(score_grad, queries))
    left = lane < HEAD_DIM
    dk = jnp.where(left, key_outs[0], key_outs[1]) * scale
    dk_ref[...] = turn_lanes(dk, cos_ref[...], -sin_ref[...]).astype(bf16)
    dv_ref[...] = jnp.where(left, value_outs[0], value_outs[1]).astype(bf16)


def key_back(projected, sent, own_places, places, starts, cosine, sine, prompt):
    rows = own_places.shape[0]
    length, width = projected.shape[0], projected.shape[1] // 3
    out = pl.BlockSpec((rows, LANES), lambda j: (0, j))
    keys = pl.BlockSpec((rows, LANES), lambda j: (0, PAIRS + j))
    values = pl.BlockSpec((rows, LANES), lambda j: (0, 2 * PAIRS + j))
    every = pl.BlockSpec((length, LANES), lambda j: (0, j))
    same = pl.BlockSpec((rows, LANES), lambda j: (0, 0))
    column = pl.BlockSpec((rows, 1), lambda j: (0, 0))
    line = pl.BlockSpec((1, length), lambda j: (0, 0))
    return pl.pallas_call(
        functools.partial(key_kernel, prompt, len(sent)),
        grid=(PAIRS,),
        in_specs=[keys, values, every]
        + [pl.BlockSpec((block.shape[0], LANES), lambda j: (0, j)) for block in sent]
        + [pl.BlockSpec((block.shape[0], LANES), lambda j: (0, PAIRS)) for block in sent]
        + [column, line, line, same, same],
        out_specs=[out, out],
        out_shape=[jax.ShapeDtypeStruct((rows, width), bf16)] * 2,
        scratch_shapes=[
            pltpu.VMEM((rows, length), f32),
            pltpu.VMEM((32, 1, length), f32),
        ],
        compiler_params=kernel_params(1),
        cost_estimate=pl.CostEstimate(
            flops=16 * rows * length * width,
            bytes_accessed=4 * length * width,
            transcendentals=rows * length * HEADS,
        ),
    )(projected, projected, projected, *sent, *sent, own_places, places, starts, cosine, sine)


def cross(x, flag_ref):
    tall = x.shape[0]
    far = jnp.full((tall, LANES), flag_ref[0, 0], jnp.int32) > 0
    near = jnp.full((tall, LANES), flag_ref[0, 1], jnp.int32) > 0
    left, right = x[:, :LANES], x[:, LANES:]
    left = jnp.where(near, pltpu.roll(left, HEAD_DIM, 1), left)
    right = jnp.where(near, pltpu.roll(right, HEAD_DIM, 1), right)
    return jnp.concatenate(
        [jnp.where(far, right, left), jnp.where(far, left, right)], axis=1
    )


def stack_rows(refs):
    return jnp.concatenate([ref[...] for ref in refs], axis=0)


def expert_kernel(flag_ref, x_ref, *refs):
    gates, ups, downs = refs[:4], refs[4:8], refs[8:12]
    gate_ref, up_ref, out_ref, acc_ref = refs[12:]
    step = pl.program_id(0)
    x = x_ref[...]
    gate = dot_nn(x, stack_rows(gates))
    up = dot_nn(x, stack_rows(ups))
    gate_ref[...] = gate
    up_ref[...] = up
    inner = cross(gate * jax.nn.sigmoid(gate) * up, flag_ref).astype(bf16)
    out = dot_nn(inner, stack_rows(downs))

    @pl.when(step == 0)
    def _():
        acc_ref[...] = out

    @pl.when(step > 0)
    def _():
        acc_ref[...] += out

    @pl.when(step == pl.num_programs(0) - 1)
    def _():
        out_ref[...] = acc_ref[...].astype(bf16)


def expert_specs(width, hidden):
    tile = hidden // EXPERTS
    tall = pl.BlockSpec((width // 4, tile), lambda j: (0, j))
    flat = pl.BlockSpec((tile // 4, width), lambda j: (j, 0))
    return tile, [tall] * 8 + [flat] * 4


def run_expert(flags, x, gates, ups, downs):
    rows, width = x.shape
    hidden = gates[0].shape[1]
    tile, specs = expert_specs(width, hidden)
    whole = pl.BlockSpec((rows, width), lambda j: (0, 0))
    column = pl.BlockSpec((rows, tile), lambda j: (0, j))
    return pl.pallas_call(
        expert_kernel,
        grid=(EXPERTS,),
        in_specs=[pl.BlockSpec(memory_space=pltpu.SMEM), whole] + specs,
        out_specs=[column, column, whole],
        out_shape=[
            jax.ShapeDtypeStruct((rows, hidden), f32),
            jax.ShapeDtypeStruct((rows, hidden), f32),
            jax.ShapeDtypeStruct((rows, width), bf16),
        ],
        scratch_shapes=[pltpu.VMEM((rows, width), f32)],
        compiler_params=kernel_params(1),
        cost_estimate=pl.CostEstimate(
            flops=6 * rows * width * hidden,
            bytes_accessed=6 * width * hidden + 8 * rows * hidden,
            transcendentals=rows * hidden,
        ),
    )(flags, x, *gates, *ups, *downs)


def expert_back_kernel(both, flag_ref, x_ref, grad_ref, order_ref, *refs):
    if not both:
        gate_ref, up_ref = refs[:2]
        refs = refs[2:]
    gates, ups, downs = refs[:4], refs[4:8], refs[8:12]
    outs, back_ref = refs[12:18], refs[18]
    acc_ref, turned_ref = refs[19:21]
    step = pl.program_id(0)
    last = step == pl.num_programs(0) - 1
    width = x_ref.shape[1]

    @pl.when(step == 0)
    def _():
        turned_ref[...] = x_ref[...].astype(f32).T.astype(bf16)

    grad = grad_ref[...]
    gate_w, up_w, down_w = stack_rows(gates), stack_rows(ups), stack_rows(downs)
    if both:
        x = x_ref[...]
        gate, up = dot_nn(x, gate_w), dot_nn(x, up_w)
    else:
        gate, up = gate_ref[...], up_ref[...]
    sigma = jax.nn.sigmoid(gate)
    gated = gate * sigma
    inner = cross(gated * up, flag_ref)
    inner_grad = cross(dot_nt(grad, down_w), flag_ref)
    up_low = (inner_grad * gated).astype(bf16)
    gate_low = (inner_grad * up * (sigma + gated * (1.0 - sigma))).astype(bf16)
    parts = [dot_nt(gate_low, gate_w) + dot_nt(up_low, up_w)]
    if both:
        parts.append(dot_nn(inner.astype(bf16), down_w))
    part = jnp.concatenate(parts, axis=1) if both else parts[0]

    @pl.when(step == 0)
    def _():
        acc_ref[...] = part

    @pl.when(step > 0)
    def _():
        acc_ref[...] += part

    @pl.when(last)
    def _():
        in_low = acc_ref[:, :width].astype(bf16)
        back_ref[:, :width] = dot_nt(in_low, order_ref[...]).astype(bf16)
        if both:
            back_ref[:, width:] = acc_ref[:, width:].astype(bf16)

    turned = turned_ref[...]
    members = (
        dot_nn(turned, gate_low).astype(bf16),
        dot_nn(turned, up_low).astype(bf16),
        dot_nn(inner.T.astype(bf16), grad).astype(bf16),
    )
    for at, member in enumerate(members):
        half = member.shape[0] // 2
        outs[2 * at][...] = member[:half]
        outs[2 * at + 1][...] = member[half:]


def run_expert_back(flags, received, order, gate, up, gates, ups, downs):
    both = gate is None
    if both:
        rows, width = received[0].shape[0], received[0].shape[1] // 2
    else:
        rows, width = received[0].shape
    hidden = gates[0].shape[1]
    tile, specs = expert_specs(width, hidden)
    first = pl.BlockSpec((rows, width), lambda j: (0, 0))
    beside = pl.BlockSpec((rows, width), lambda j: (0, 1)) if both else first
    table = pl.BlockSpec((width, width), lambda j: (0, 0))
    column = pl.BlockSpec((rows, tile), lambda j: (0, j))
    tall = pl.BlockSpec((width // 2, tile), lambda j: (0, j))
    flat = pl.BlockSpec((None, tile // 2, width), lambda j: (j, 0, 0))
    tall_shape = jax.ShapeDtypeStruct((width // 2, hidden), bf16)
    flat_shape = jax.ShapeDtypeStruct((EXPERTS, tile // 2, width), bf16)
    wide = 2 * width if both else width
    *halves, back = pl.pallas_call(
        functools.partial(expert_back_kernel, both),
        grid=(EXPERTS,),
        in_specs=[pl.BlockSpec(memory_space=pltpu.SMEM), first, beside, table]
        + ([] if both else [column, column])
        + specs,
        out_specs=[tall] * 4 + [flat] * 2 + [pl.BlockSpec((rows, wide), lambda j: (0, 0))],
        out_shape=[tall_shape] * 4
        + [flat_shape] * 2
        + [jax.ShapeDtypeStruct((rows, wide), bf16)],
        scratch_shapes=[pltpu.VMEM((rows, wide), f32), pltpu.VMEM((width, rows), bf16)],
        compiler_params=kernel_params(1),
        cost_estimate=pl.CostEstimate(
            flops=(18 if both else 12) * rows * width * hidden,
            bytes_accessed=12 * width * hidden + 8 * rows * hidden,
            transcendentals=rows * hidden,
        ),
    )(flags, *received, order, *([] if both else [gate, up]), *gates, *ups, *downs)
    return halves, back


def product_kernel(x_ref, g_ref, *refs):
    thin_ref = refs[0] if len(refs) == 3 else None
    kept_ref, given_ref = refs[-2:]
    turned = x_ref[...].astype(f32).T.astype(bf16)
    half = turned.shape[0] // 2
    wide = g_ref.shape[1]
    span = turned.shape[0]
    for at in range(0, wide, span):
        part = dot_nn(turned, g_ref[:, at : at + span]).astype(bf16)
        kept_ref[:, at : at + span] = part[:half]
        given_ref[:, at : at + span] = part[half:]
    if thin_ref is not None:
        kept_ref[:, wide:] = thin_ref[:half]
        given_ref[:, wide:] = thin_ref[half:]


def weight_product(x, grad, thin=None):
    rows, width = x.shape
    wide = grad.shape[1] + (0 if thin is None else thin.shape[1])
    shape = jax.ShapeDtypeStruct((width // 2, wide), bf16)
    vmem = pl.BlockSpec(memory_space=pltpu.VMEM)
    return pl.pallas_call(
        product_kernel,
        in_specs=[vmem] * (2 if thin is None else 3),
        out_specs=[vmem] * 2,
        out_shape=[shape] * 2,
        compiler_params=pltpu.CompilerParams(vmem_limit_bytes=VMEM_LIMIT),
        cost_estimate=pl.CostEstimate(
            flops=2 * rows * width * wide,
            bytes_accessed=2 * (width * wide + rows * (width + wide)),
            transcendentals=0,
        ),
    )(x, grad, *([] if thin is None else [thin]))


def lanes_of(rows):
    return lax.broadcasted_iota(jnp.int32, (rows, LANES), 1)


def two_part_nn(a, b):
    top = a.astype(bf16)
    return dot_nn(top, b) + dot_nn((a - top.astype(f32)).astype(bf16), b)


def two_part_nt(a, b):
    top = a.astype(bf16)
    return dot_nt(top, b) + dot_nt((a - top.astype(f32)).astype(bf16), b)


def root_scale(x):
    return lax.rsqrt(jnp.mean(x * x, axis=1, keepdims=True) + norm_eps)


def line_of(small_ref, at):
    return small_ref[...].astype(f32).T[at : at + 1]


def norm_kernel(*refs):
    small_ref, out_ref = refs[-2:]
    line = line_of(small_ref, AT_ATTN)
    start = 0
    for x_ref in refs[:-2]:
        tall = x_ref.shape[0]
        x = x_ref[...].astype(f32)
        out_ref[start : start + tall] = (x * root_scale(x) * line).astype(bf16)
        start += tall


def norm_rows(blocks, packed):
    width = blocks[0].shape[1]
    count = sum(block.shape[0] for block in blocks)
    return pl.pallas_call(
        norm_kernel,
        grid=(1,),
        in_specs=[once(block.shape, lambda i: (0, 0)) for block in blocks]
        + [pl.BlockSpec((width, LANES), lambda i: (0, 4 * width // LANES))],
        out_specs=once((count, width), lambda i: (0, 0)),
        out_shape=jax.ShapeDtypeStruct((count, width), bf16),
        compiler_params=kernel_params(1),
        cost_estimate=pl.CostEstimate(
            flops=8 * count * width, bytes_accessed=4 * count * width, transcendentals=0
        ),
    )(*blocks, packed)


def pair_partner(x):
    lane = lanes_of(x.shape[0])
    return jnp.where(lane % 2 == 0, pltpu.roll(x, LANES - 1, 1), pltpu.roll(x, 1, 1))


def side_weights(chances, mixes, chosen):
    weight = chances * chosen
    last = [pick_column(weight, 9 + at) for at in range(3)]
    mix = [pick_column(mixes, AT_CONST + at) for at in range(4)]
    alpha = last[0] + last[1] * mix[0] + last[2] * mix[2]
    return last, mix, alpha, (last[1] * mix[1], last[2] * mix[3])


def slots_of_grad(grad, chances, picks, slot_pairs):
    parts = [jnp.sum(chances * pick, axis=1, keepdims=True) * grad for pick in picks]
    return dot_nn(slot_pairs, jnp.concatenate(parts, axis=0).astype(bf16)).astype(bf16)


def to_expert_kernel(
    final,
    att_ref,
    hidden_ref,
    wout_ref,
    small_ref,
    previous_ref,
    slot_tokens_ref,
    order_ref,
    *refs,
):
    if final:
        grad_ref, first_ref, second_ref, slot_pairs_ref = refs[:4]
        refs = refs[4:]
    mid_ref, logit_ref, chance_ref, mix_ref, message_ref = refs
    mid = hidden_ref[...] + dot_nn(att_ref[...].astype(bf16), wout_ref[...])
    mid_ref[...] = mid
    low = (mid * root_scale(mid) * line_of(small_ref, AT_MOE)).astype(bf16)
    thin = dot_nn(low, small_ref[...])
    lane = lanes_of(mid.shape[0])
    logits = jnp.where(lane < ROUTED, thin + previous_ref[...], 0.0)
    logit_ref[...] = logits
    top = jnp.max(jnp.where(lane < ROUTED, logits, masked_score), axis=1, keepdims=True)
    expo = jnp.where(lane < ROUTED, jnp.exp(logits - top), 0.0)
    chances = expo / jnp.sum(expo, axis=1, keepdims=True)
    chance_ref[...] = chances
    inside = (lane >= AT_CONST) & (lane < AT_CONST + 4)
    apart = jnp.where(inside, thin - pair_partner(thin), 0.0)
    mix_ref[...] = jnp.where(inside, jax.nn.sigmoid(apart), 0.0)
    width = mid.shape[1]
    moved = dot_nn(low, order_ref[...]).astype(bf16)
    message_ref[:, :width] = dot_nn(slot_tokens_ref[...], moved).astype(bf16)
    if final:
        message_ref[:, width:] = slots_of_grad(
            grad_ref[...].astype(f32),
            chances,
            (first_ref[...], second_ref[...]),
            slot_pairs_ref[...],
        )


def from_expert_kernel(
    final, mid_ref, chance_ref, mix_ref, first_ref, second_ref, small_ref, pair_slots_ref, back_ref, *refs
):
    if final:
        (out_ref,) = refs
    else:
        next_ref, out_ref, normed_ref = refs
    mid = mid_ref[...]
    rows, width = mid.shape
    picks = (first_ref[...], second_ref[...])
    chances = chance_ref[...]
    _, _, alpha, betas = side_weights(chances, mix_ref[...], picks[0] + picks[1])
    lines = small_ref[...].astype(f32).T
    out = mid + alpha * (mid * root_scale(mid) * lines[AT_MOE : AT_MOE + 1])
    out += betas[0] * lines[AT_CVEC : AT_CVEC + 1] + betas[1] * lines[AT_CVEC + 1 : AT_CVEC + 2]
    pairs = dot_nn(pair_slots_ref[...], back_ref[...])
    for at in range(TOP):
        picked = jnp.sum(chances * picks[at], axis=1, keepdims=True)
        out += picked * pairs[at * rows : (at + 1) * rows]
    out_ref[...] = out.astype(out_ref.dtype)
    if not final:
        normed_ref[...] = (out * root_scale(out) * line_of(next_ref, AT_ATTN)).astype(bf16)


def rms_back_rows(values, gain, grad):
    scale = root_scale(values)
    inner = grad * gain
    along = jnp.mean(inner * values, axis=1, keepdims=True)
    gain_grad = jnp.sum(grad * values * scale, axis=0, keepdims=True)
    return scale * inner - values * (scale * scale * scale * along), gain_grad


def to_attention_kernel(
    grad_ref,
    mid_ref,
    chance_ref,
    mix_ref,
    first_ref,
    second_ref,
    small_ref,
    pair_slots_ref,
    token_slots_ref,
    back_ref,
    in_back_ref,
    next_ref,
    wout_ref,
    att_ref,
    total_ref,
    head_ref,
    mid_grad_ref,
    mid_low_ref,
    sent_ref,
    delta_ref,
    thin_grad_ref,
    thin_w_ref,
    line_grad_ref,
):
    grad, mid = grad_ref[...].astype(f32), mid_ref[...]
    rows, width = mid.shape
    picks = (first_ref[...], second_ref[...])
    chosen = picks[0] + picks[1]
    chances, mixes = chance_ref[...], mix_ref[...]
    last, mix, alpha, betas = side_weights(chances, mixes, chosen)
    lines = small_ref[...].astype(f32).T
    gain = lines[AT_MOE : AT_MOE + 1]
    cvecs = [lines[AT_CVEC + c : AT_CVEC + 1 + c] for c in range(2)]
    mixed = mid * root_scale(mid) * gain
    pairs = dot_nn(pair_slots_ref[...], back_ref[...])
    along = jnp.sum(grad * mixed, axis=1, keepdims=True)
    across = [jnp.sum(grad * cvecs[c], axis=1, keepdims=True) for c in range(2)]
    lane = lanes_of(rows)
    chance_grad = jnp.where(lane == 9, along, 0.0)
    for c in range(2):
        both = mix[2 * c] * along + mix[2 * c + 1] * across[c]
        chance_grad = jnp.where(lane == 10 + c, both, chance_grad)
    chance_grad *= chosen
    for at in range(TOP):
        part = jnp.sum(grad * pairs[at * rows : (at + 1) * rows], axis=1, keepdims=True)
        chance_grad += picks[at] * part
    logit_grad = chances * (
        chance_grad - jnp.sum(chances * chance_grad, axis=1, keepdims=True)
    ) + jnp.where(lane < ROUTED, next_ref[...], 0.0)
    mix_grad = jnp.zeros_like(mixes)
    for c in range(2):
        mix_grad = jnp.where(lane == AT_CONST + 2 * c, last[1 + c] * along, mix_grad)
        mix_grad = jnp.where(lane == AT_CONST + 2 * c + 1, last[1 + c] * across[c], mix_grad)
    product = mixes * mix_grad
    thin_grad = logit_grad + mixes * (mix_grad - (product + pair_partner(product)))
    thin_grad_ref[...] = thin_grad
    low_grad = (
        alpha * grad
        + two_part_nt(thin_grad, small_ref[...])
        + dot_nn(token_slots_ref[...], in_back_ref[...])
    )
    mid_part, gain_grad = rms_back_rows(mid, gain, low_grad)
    mid_grad = grad + mid_part
    mid_grad_ref[...] = mid_grad
    mid_low = mid_grad.astype(bf16)
    mid_low_ref[...] = mid_low
    att_grad = dot_nt(mid_low, wout_ref[...]).astype(bf16)
    delta = two_part_nn(att_grad.astype(f32) * att_ref[...], head_ref[...])
    delta_ref[...] = delta
    sent_ref[:, :width] = att_grad
    stats = jnp.zeros((rows, LANES), f32)
    for at, stat in enumerate((total_ref[...], delta)):
        top = stat.astype(bf16).astype(f32)
        for part, piece in enumerate((top, stat - top)):
            place = 32 * at + 16 * part
            stats += pltpu.roll(piece, place, 1) if place else piece
    sent_ref[:, width:] = stats.astype(bf16)
    turned = mixed.T.astype(bf16)
    thin_w_ref[...] = two_part_tn(turned, thin_grad)
    line_grad_ref[...] = jnp.concatenate(
        [gain_grad]
        + [jnp.sum(betas[c] * grad, axis=0, keepdims=True) for c in range(2)]
        + [jnp.zeros((5, width), f32)],
        axis=0,
    )


def two_part_tn(turned, x):
    top = x.astype(bf16)
    return dot_nn(turned, top) + dot_nn(turned, (x - top.astype(f32)).astype(bf16))


def from_attention_kernel(final, *refs):
    q_refs, (k_ref, v_ref, wq_ref, wk_ref, wv_ref) = refs[:3], refs[3:8]
    hidden_ref, small_ref, mid_grad_ref = refs[8:11]
    refs = refs[11:]
    if final:
        grad_ref, line_grad_ref = refs
    else:
        chance_ref, first_ref, second_ref, slot_pairs_ref, grad_ref, line_grad_ref, message_ref = refs
    queries = jnp.concatenate([ref[...] for ref in q_refs], axis=1)
    normed_grad = dot_nt(queries, wq_ref[...])
    normed_grad += dot_nt(k_ref[...], wk_ref[...])
    normed_grad += dot_nt(v_ref[...], wv_ref[...])
    part, gain_grad = rms_back_rows(
        hidden_ref[...], line_of(small_ref, AT_ATTN), normed_grad
    )
    grad = mid_grad_ref[...] + part
    grad_ref[...] = grad
    line_grad_ref[...] = jnp.concatenate(
        [gain_grad, jnp.zeros((7, gain_grad.shape[1]), f32)], axis=0
    )
    if not final:
        message_ref[...] = slots_of_grad(
            grad, chance_ref[...], (first_ref[...], second_ref[...]), slot_pairs_ref[...]
        )


class Block:
    def __init__(self, array, wide, at):
        self.array, self.wide, self.at = array, wide, at


def run_fused(kernel, args, outs, flops):
    arrays, specs = [], []
    for arg in args:
        if isinstance(arg, Block):
            arrays.append(arg.array)
            specs.append(
                pl.BlockSpec(
                    (arg.array.shape[0], arg.wide),
                    functools.partial(lambda at, i: (0, at), arg.at),
                )
            )
        else:
            arrays.append(arg)
            specs.append(pl.BlockSpec(arg.shape, lambda i: (0, 0)))
    return pl.pallas_call(
        kernel,
        grid=(1,),
        in_specs=specs,
        out_specs=[pl.BlockSpec(shape, lambda i: (0, 0)) for shape, _ in outs],
        out_shape=[jax.ShapeDtypeStruct(shape, dtype) for shape, dtype in outs],
        compiler_params=kernel_params(1),
        cost_estimate=pl.CostEstimate(flops=flops, bytes_accessed=1 << 22, transcendentals=0),
    )(*arrays)


def after(x, *things):
    return lax.optimization_barrier((x,) + things)[0]


TABLE = {
    "a_g0": ("", ""),
    "a_u0": ("", "packed0"),
    "a_d0": ("packed0", "proj0"),
    "x_g0": ("", "packed0"),
    "x_u0": ("packed0", "proj0"),
    "x_d0": ("proj0", "ein0"),
    "c_g0": ("packed0", ""),
    "c_u0": ("proj0", ""),
    "c_d0": ("", ""),
    "k_1": ("proj0", ""),
    "a_g1": ("proj0", "msg0"),
    "a_u1": ("ein0", "eout0"),
    "a_d1": ("ag1", "att1"),
    "x_g1": ("eout0", "ag1"),
    "x_u1": ("ag1", ""),
    "x_d1": ("att1", ""),
    "c_g1": ("msg1", ""),
    "c_u1": ("msg1", ""),
    "c_d1": ("msg1", ""),
    "cj_g1": ("", ""),
    "cj_u1": ("", ""),
    "cj_d1": ("", ""),
    "xj_g1": ("", "sall1"),
    "xj_u1": ("", ""),
    "xj_d1": ("", ""),
    "p_o1": ("slot0", ""),
    "xj_o1": ("", ""),
    "r_g1": ("sall1", "key1"),
    "p_q1": ("og0", ""),
    "xj_q1": ("", "key0"),
    "r_u1": ("og0", "ig0"),
    "r_d1": ("sall0", "cols0"),
    "cj_g0": ("", ""),
    "cj_u0": ("", ""),
    "cj_d0": ("", ""),
    "xj_g0": ("", ""),
    "xj_u0": ("", ""),
    "xj_d0": ("", ""),
    "p_o0": ("sall0", ""),
    "xj_o0": ("", ""),
    "rs": ("key0", ""),
    "r_u0": ("cols", "part0"),
    "r_d0": ("part", ""),
}


class Plan:
    def __init__(self, table):
        self.table, self.make, self.found, self.passed = table, {}, {}, {"": True}

    def add(self, name, build):
        self.make[name] = build
        if self.table[name][0] in self.passed:
            self.get(name)

    def get(self, name):
        if name not in self.found:
            self.found[name] = self.make[name](lambda x: x)
        return self.found[name]

    def point(self, at, value):
        done = []
        for name, (_, end) in self.table.items():
            if end == at and name in self.make:
                done += jax.tree.leaves(self.get(name))
        if done:
            value = after(value, *done)
        self.passed[at] = True
        for name, (start, _) in self.table.items():
            if start == at and name in self.make and name not in self.found:
                self.found[name] = self.make[name](lambda x: after(x, value))
        return value


def swap(x, axis):
    return lax.ppermute(x, axis, [(0, 1), (1, 0)])


def fold(x, axis, at):
    given = lax.dynamic_index_in_dim(x, 1 - at, 1, keepdims=False)
    kept = lax.dynamic_index_in_dim(x, at, 1, keepdims=False)
    return (kept.astype(f32) + swap(given, axis).astype(f32)).astype(bf16)


def gather_rows(x, axes, fillers=()):
    far, near, core = axes[:-2], axes[-2], axes[-1]
    count = 2 ** len(far)
    found = [x]
    for step in range(1, count):
        pairs = [(at, (at + step) % count) for at in range(count)]
        found.append(lax.ppermute(x, far, pairs))
    blocks, filled = [], []
    for step, block in enumerate(found):
        if 0 < step <= len(fillers):
            beside = [block] if step > 1 else [blocks[0]]
            filled.append(fillers[step - 1](*beside, *filled[-1:]))
            block = after(block, filled[-1])
        pair = jnp.concatenate([block, swap(block, near)], axis=0)
        blocks += [pair, swap(pair, core)]
    return (blocks, filled) if fillers else blocks


def gathered_order(axes):
    count = 2 ** (len(axes) - 2)
    me = lax.axis_index(axes)
    far, near, core = me // 4, me // 2 % 2, me % 2
    order = []
    for step in range(count):
        for other_core in range(2):
            for other_near in range(2):
                order.append(
                    (far - step) % count * 4 + (near ^ other_near) * 2 + (core ^ other_core)
                )
    return jnp.stack(order).astype(jnp.int32)


def shards(
    axes,
    tokens,
    prev_logits,
    routes,
    order,
    deal,
    w_qkv,
    w_out,
    w_gate,
    w_up,
    w_down,
    norm_attn,
    norm_moe,
    w_router,
    w_const,
    const_vec,
    grad_out,
):
    rows, width = tokens.shape[1], tokens.shape[2]
    ex_axes, sub_axes = axes[:3], axes[3:]
    every_axis = axes + (FS,)
    subs = 2 ** len(sub_axes)
    ctx_size = EXPERTS * subs
    length = rows * ctx_size
    prompt = length // 2
    cont_len = prompt // (ctx_size // 8)
    block_rows = rows // 2
    own_rows = w_qkv.shape[1]
    fs_at = lax.axis_index(FS)
    sub_at = lax.axis_index(sub_axes)


    def deal_out(x):
        return lax.all_to_all(x, ex_axes, 0, 0, tiled=True)

    def dispatch(x):
        return deal_out(x.reshape(EXPERTS, SLOTS, -1)).reshape(x.shape)

    def blank(count):
        return jnp.zeros((own_rows, count), bf16)

    def fetch_packed(layer, tie):
        mine = jnp.concatenate(
            [
                w_qkv[layer],
                w_out[layer],
                w_router[layer],
                blank(AT_CONST - ROUTED),
                w_const[layer],
                blank(AT_CVEC - AT_CONST - 4),
                const_vec[layer],
                blank(AT_ATTN - AT_CVEC - 2),
                norm_attn[layer][:, None],
                norm_moe[layer][:, None],
                blank(LANES - AT_MOE - 1),
            ],
            axis=1,
        )
        return lax.all_gather(tie(mine), every_axis, axis=0, tiled=True)

    by_chunks = subs == 2
    flags = jnp.stack([sub_at, fs_at]).astype(jnp.int32)[None, :]

    plan = Plan(TABLE)

    def add_weight(name, member):
        plan.add(
            "a_" + name,
            lambda tie: deal_out(tie(member)).reshape(-1, member.shape[-1]),
        )
        plan.add("x_" + name, lambda tie: swap(tie(plan.get("a_" + name)), FS))
        plan.add(
            "c_" + name,
            lambda tie: (
                swap(tie(plan.get("a_" + name)), sub_axes[0]),
                swap(plan.get("x_" + name), sub_axes[0]),
            ),
        )

    def weights_of(layer):
        found = []
        for name, member in zip("gud", (w_gate, w_up, w_down)):
            if by_chunks:
                parts = [plan.get(part + name + str(layer)) for part in ("a_", "x_", "c_")]
                found.append((parts[0], parts[1]) + parts[2])
            else:
                moved = deal_out(member[layer])
                whole = lax.all_gather(moved, sub_axes + (FS,), axis=1, tiled=True)
                found.append(whole.reshape(-1, whole.shape[2]))
        return found

    if not by_chunks:
        to_chunks = jnp.eye(width, dtype=bf16)
    else:
        place = jnp.arange(width, dtype=jnp.int32)
        chunk, inside = place // (width // 4), place % (width // 4)
        source = (
            inside // own_rows * 4 + (chunk ^ (sub_at * 2 + fs_at)).astype(jnp.int32)
        ) * own_rows + inside % own_rows
        to_chunks = (place[:, None] == source[None, :]).astype(bf16)

    tokens_all = gather_rows(tokens[0], axes)
    all_packed = [fetch_packed(0, lambda x: x)]
    block_order = gathered_order(axes)
    deal_pairs = deal.reshape(ctx_size, 2)
    own_blocks = jnp.sum(
        jnp.where(
            (block_order[:, None] == jnp.arange(ctx_size, dtype=jnp.int32)[None, :])[:, :, None],
            deal_pairs[None],
            0,
        ),
        axis=1,
    ).reshape(2 * ctx_size)
    all_places = (
        own_blocks[:, None] * block_rows + jnp.arange(block_rows, dtype=jnp.int32)[None, :]
    ).reshape(length)
    within = jnp.where(all_places < prompt, all_places, prompt + (all_places - prompt) % cont_len)
    all_starts = jnp.where(all_places < prompt, 0, all_places - (all_places - prompt) % cont_len)
    lane = jnp.arange(LANES, dtype=jnp.int32)
    half = HEAD_DIM // 2
    frequency = 10000.0 ** (-(lane % half).astype(f32) / half)
    angles = within.astype(f32)[:, None] * frequency[None, :]
    cosine = jnp.cos(angles)
    sine = jnp.sin(angles) * jnp.where(lane % HEAD_DIM < half, -1.0, 1.0)[None, :]
    own_cos, own_sin = cosine, sine
    own_places, own_starts = all_places[:rows, None], all_starts[:rows, None]
    place_line, start_line = all_places[None, :], all_starts[None, :]

    if by_chunks:
        for layer in range(LAYERS):
            for name, member in zip("gud", (w_gate, w_up, w_down)):
                member = member[layer]
                if (name, layer) == ("u", 0):
                    member = after(member, cosine, sine)
                add_weight(name + str(layer), member)
    first_things = [*tokens_all, cosine, sine]

    route_rows = routes[0]
    flat_routes = jnp.concatenate([route_rows[:, k] for k in range(TOP)])
    flat_order = jnp.concatenate([order[0].reshape(rows, TOP)[:, k] for k in range(TOP)])
    earlier = (flat_routes[None, :] == flat_routes[:, None]) & (
        flat_order[None, :] < flat_order[:, None]
    )
    slot = jnp.sum(earlier.astype(jnp.int32), axis=1)
    in_slot = (flat_routes < EXPERTS) & (slot < CAP)
    target = jnp.where(in_slot, flat_routes * SLOTS + slot, -1)
    slot_ids = jnp.arange(EXPERTS * SLOTS, dtype=jnp.int32)
    pair_slots = (target[:, None] == slot_ids[None, :]).astype(bf16)
    slot_pairs = (slot_ids[:, None] == target[None, :]).astype(bf16)
    slot_tokens = slot_pairs[:, :rows] + slot_pairs[:, rows:]
    token_slots = pair_slots[:rows] + pair_slots[rows:]
    picks = [(route_rows[:, k : k + 1] == lane[None, :]).astype(f32) for k in range(TOP)]
    head_of = (jnp.arange(width, dtype=jnp.int32)[:, None] // HEAD_DIM == lane[None, :]).astype(
        bf16
    )

    table = (rows, LANES)
    full = (rows, width)
    core_axis = sub_axes[0]

    def join_cores(kept, given, *wait):
        part = kept.astype(f32) + swap(after(given, *wait), core_axis).astype(f32)
        if part.ndim == 3:
            half = part.shape[1] // 2
            return part[:, :half].astype(bf16), part[:, half:].astype(bf16)
        half = part.shape[0] // 2
        return part[:half].astype(bf16), part[half:].astype(bf16)

    def join_groups(pieces, *wait):
        kept, given = pieces
        part = (kept.astype(f32) + swap(after(given, *wait), FS).astype(f32)).astype(bf16)
        return part.reshape(EXPERTS, -1, part.shape[-1])

    def reduce_rows(part):
        part = part.reshape(-1, part.shape[2])
        return lax.psum_scatter(part, ex_axes, scatter_dimension=0, tiled=True)

    def add_grads(layer, halves):
        for at, name in enumerate("gud"):
            name += str(layer)
            kept, given = halves[2 * at], halves[2 * at + 1]
            plan.add(
                "cj_" + name,
                lambda tie, kept=kept, given=given: join_cores(kept, tie(given)),
            )
            plan.add(
                "xj_" + name,
                lambda tie, name=name: join_groups(
                    (plan.get("cj_" + name)[0], tie(plan.get("cj_" + name)[1]))
                ),
            )
            if name == "u0":
                plan.add(
                    "r_u0",
                    lambda tie: deal_out(
                        tie(jnp.concatenate([plan.get("xj_g0"), plan.get("xj_u0")], axis=2))
                    ),
                )
            if name not in ("g0", "u0", "d0"):
                plan.add(
                    "r_" + name, lambda tie, name=name: deal_out(tie(plan.get("xj_" + name)))
                )

    def add_out(layer, attended, mid_low):
        name = "o" + str(layer)

        def product(tie):
            att_rel = dot_nn(attended.astype(bf16), to_chunks).astype(bf16)
            return join_cores(*weight_product(att_rel, tie(mid_low)))

        plan.add("p_" + name, product)
        plan.add(
            "xj_" + name,
            lambda tie: join_groups((plan.get("p_" + name)[0], tie(plan.get("p_" + name)[1]))),
        )
        if layer == 0:
            plan.add(
                "r_d0",
                lambda tie: deal_out(
                    tie(jnp.concatenate([plan.get("xj_d0"), plan.get("xj_o0")], axis=1))
                ),
            )

    def add_qkv(thin_part, normed, proj_grad):
        def product(tie):
            thin_low = dot_tn(to_chunks, thin_part.astype(bf16)).astype(bf16)
            normed_rel = dot_nn(normed, to_chunks).astype(bf16)
            return join_cores(*weight_product(normed_rel, tie(proj_grad), thin_low))

        plan.add("p_q1", product)
        plan.add(
            "xj_q1",
            lambda tie: join_groups((plan.get("p_q1")[0], tie(plan.get("p_q1")[1]))),
        )
        plan.add(
            "rs",
            lambda tie: reduce_rows(
                jnp.concatenate([plan.get("xj_o1"), tie(plan.get("xj_q1"))], axis=2)
            ),
        )

    def scatter_whole(member):
        cut = member.astype(bf16).reshape(EXPERTS, subs * 2, -1, member.shape[1])
        part = lax.psum_scatter(cut, sub_axes + (FS,), scatter_dimension=1, tiled=True)
        return part.reshape((EXPERTS,) + part.shape[2:])

    def expert_plain_back(x, out_grad, gate_act, upward, weights):
        wgate, wup, wdown = weights
        sigma = jax.nn.sigmoid(gate_act)
        gated = gate_act * sigma
        inner = (gated * upward).astype(bf16)
        inner_grad = dot_nt(out_grad, wdown)
        up_grad = (inner_grad * gated).astype(bf16)
        gate_grad = (inner_grad * upward * (sigma + gated * (1.0 - sigma))).astype(bf16)
        in_grad = (dot_nt(gate_grad, wgate) + dot_nt(up_grad, wup)).astype(bf16)
        products = (dot_tn(x, gate_grad), dot_tn(x, up_grad), dot_tn(inner, out_grad))
        return [scatter_whole(member) for member in products], in_grad

    def expert_plain(x, weights):
        wgate, wup, wdown = weights
        gate_act, upward = dot_nn(x, wgate), dot_nn(x, wup)
        inner = (jax.nn.silu(gate_act) * upward).astype(bf16)
        return gate_act, upward, dot_nn(inner, wdown).astype(bf16)

    hidden = tokens[0].astype(f32)
    previous = jnp.pad(prev_logits[0], ((0, 0), (0, LANES - ROUTED)))
    grad = grad_out[0]
    all_packed[0] = after(all_packed[0], *first_things, slot_tokens, previous)
    all_packed[0] = plan.point("packed0", all_packed[0])
    plan.add("k_1", lambda tie: fetch_packed(1, tie))
    saved_all = []
    for layer in range(LAYERS):
        final = layer == LAYERS - 1
        packed = all_packed[layer]
        if layer == 0:
            blocks = tokens_all
            normed_all = norm_rows(tokens_all, packed)
        else:
            normed = plan.point("norm1", normed)
            blocks = gather_rows(normed, axes)
            blocks[-1] = plan.point("ag1", blocks[-1])
            normed_all = None if by_chunks else jnp.concatenate(blocks, axis=0)
        projected = project(blocks, packed, cosine, sine, layer == 0)
        projected = plan.point("proj" + str(layer), projected)
        attended, totals = attend(projected, own_places, own_starts, place_line, prompt)
        attended = plan.point("att" + str(layer), attended)
        if layer == 0:
            all_packed.append(plan.get("k_1"))
        small = Block(packed, LANES, 4 * width // LANES)
        wout = Block(packed, width, 3)
        midway, logits, chances, mixing, slot_in = run_fused(
            functools.partial(to_expert_kernel, final),
            [attended, hidden, wout, small, previous, slot_tokens, to_chunks]
            + ([grad, picks[0], picks[1], slot_pairs] if final else []),
            [
                (full, f32),
                (table, f32),
                (table, f32),
                (table, f32),
                ((EXPERTS * SLOTS, (2 if final else 1) * width), bf16),
            ],
            6 * rows * width * width,
        )
        slot_in = plan.point("msg" + str(layer), slot_in)
        expert_in = dispatch(slot_in)
        expert_in = plan.point("ein" + str(layer), expert_in)
        weights = weights_of(layer)
        gate_act = upward = halves = None
        if by_chunks and final:
            halves, expert_out = run_expert_back(
                flags, (expert_in, expert_in), to_chunks, None, None, *weights
            )
        elif by_chunks:
            gate_act, upward, expert_out = run_expert(flags, expert_in, *weights)
        elif final:
            half_in, half_grad = expert_in[:, :width], expert_in[:, width:]
            gate_act, upward, expert_out = expert_plain(half_in, weights)
            halves, in_grad = expert_plain_back(half_in, half_grad, gate_act, upward, weights)
            expert_out = jnp.concatenate([in_grad, expert_out], axis=1)
        else:
            gate_act, upward, expert_out = expert_plain(expert_in, weights)
        if by_chunks and final:
            add_grads(1, halves)
        expert_out = plan.point("eout" + str(layer), expert_out)
        back = dispatch(expert_out)
        in_back = None
        if final:
            in_back, back = back[:, :width], back[:, width:]
        if not final:
            all_packed[1] = after(all_packed[1], expert_out)
            output, normed = run_fused(
                functools.partial(from_expert_kernel, False),
                [midway, chances, mixing, picks[0], picks[1], small, pair_slots, back]
                + [Block(all_packed[layer + 1], LANES, 4 * width // LANES)],
                [(full, f32), (full, bf16)],
                2 * rows * width * EXPERTS * SLOTS,
            )
        normed_own = None if layer == 0 else blocks[0][:rows]
        saved_all.append(
            (
                hidden,
                normed_own,
                normed_all,
                projected,
                attended,
                totals,
                midway,
                chances,
                mixing,
                expert_in,
                gate_act,
                upward,
                halves,
                in_back,
                weights,
                back,
            )
        )
        if not final:
            hidden = output
        previous = logits

    logit_next = jnp.zeros(table, f32)
    results = [None] * LAYERS
    moved_grads = [[None] * 3 for _ in range(LAYERS)]
    out_folded = [None] * LAYERS
    for layer in reversed(range(LAYERS)):
        final = layer == LAYERS - 1
        (
            hidden,
            normed,
            normed_all,
            projected,
            attended,
            totals,
            midway,
            chances,
            mixing,
            expert_in,
            gate_act,
            upward,
            halves,
            in_back,
            weights,
            back,
        ) = saved_all[layer]
        packed = all_packed[layer]
        small = Block(packed, LANES, 4 * width // LANES)
        wout = Block(packed, width, 3)
        if not final:
            slot_grad = plan.point("slot0", slot_grad)
            out_grad = dispatch(slot_grad)
            out_grad = plan.point("og0", out_grad)
            if by_chunks:
                halves, in_grad = run_expert_back(
                    flags, (expert_in, out_grad), to_chunks, gate_act, upward, *weights
                )
            else:
                halves, in_grad = expert_plain_back(
                    expert_in, out_grad, gate_act, upward, weights
                )
            if by_chunks:
                add_grads(0, halves)
            in_grad = plan.point("ig0", in_grad)
            in_back = dispatch(in_grad)
            in_back = plan.point("ib0", in_back)

        mid_grad, mid_low, sent, delta, logit_next, thin_w, line_grads = run_fused(
            to_attention_kernel,
            [grad, midway, chances, mixing, picks[0], picks[1], small, pair_slots]
            + [token_slots, back, in_back, logit_next, wout, attended, totals, head_of],
            [
                (full, f32),
                (full, bf16),
                ((rows, width + LANES), bf16),
                (table, f32),
                (table, f32),
                ((width, LANES), f32),
                ((8, width), f32),
            ],
            6 * rows * width * width,
        )
        def some_queries(start, *things):
            return query_back(
                start,
                2,
                after(projected, *things),
                sent,
                totals,
                delta,
                own_places,
                own_starts,
                place_line,
                own_cos,
                own_sin,
                prompt,
            )

        sent = plan.point("sent" + str(layer), sent)
        if final:
            (output_rows,) = run_fused(
                functools.partial(from_expert_kernel, True),
                [midway, chances, mixing, picks[0], picks[1], small, pair_slots]
                + [after(back, sent)],
                [(full, bf16)],
                2 * rows * width * EXPERTS * SLOTS,
            )
        sent_all, query_grads = gather_rows(
            sent, axes, [functools.partial(some_queries, start) for start in range(0, PAIRS, 2)]
        )
        if by_chunks:
            add_out(layer, attended, mid_low)
        else:
            out_w_grad = dot_tn(attended.astype(bf16), mid_low).astype(bf16)
        sent_all[-1] = plan.point("sall" + str(layer), sent_all[-1])
        key_grad, value_grad = key_back(
            projected,
            sent_all,
            own_places,
            place_line,
            start_line,
            own_cos,
            own_sin,
            prompt,
        )
        key_grad = plan.point("key" + str(layer), key_grad)
        proj_grad = jnp.concatenate([*query_grads, key_grad, value_grad], axis=1)
        before = []
        if layer > 0:
            before = [saved_all[layer - 1][7], picks[0], picks[1], slot_pairs]
        grad, gain_grads, *slot_grad = run_fused(
            functools.partial(from_attention_kernel, layer == 0),
            [*query_grads, key_grad, value_grad]
            + [Block(packed, width, at) for at in range(3)]
            + [hidden, small, mid_grad]
            + before,
            [(full, f32), ((8, width), f32)]
            + ([((EXPERTS * SLOTS, width), bf16)] if layer > 0 else []),
            6 * rows * width * width,
        )
        slot_grad = slot_grad[0] if slot_grad else None
        some = jnp.concatenate([gain_grads[:1], line_grads[:3]], axis=0)
        wanted = jnp.array([AT_ATTN, AT_MOE, AT_CVEC, AT_CVEC + 1], dtype=jnp.int32)
        spread_out = (wanted[:, None] == lane[None, :]).astype(f32)
        thin_part = thin_w + jnp.dot(some.T, spread_out, precision=highest)
        if by_chunks and final:
            add_qkv(thin_part, normed, proj_grad)
            continue
        share_of = 3 * width // ctx_size
        columns = proj_grad.reshape(rows, ctx_size, share_of).transpose(1, 0, 2)
        columns = plan.point("cols0", columns)
        columns = lax.all_to_all(columns, axes, 0, 0, tiled=True)
        columns = plan.point("cols", columns)
        columns = jnp.take(columns, block_order, axis=0).reshape(length, share_of)
        part = jnp.concatenate([dot_tn(columns, normed_all).T, thin_part], axis=1).astype(bf16)
        part = fold(part.reshape(ctx_size, 2, own_rows, share_of + LANES), FS, fs_at)
        part = plan.point("part0", part)
        part = lax.all_to_all(part, axes, 0, 0, tiled=True)
        part = plan.point("part", part)
        if by_chunks:
            last = plan.get("r_d0")
            tall = plan.get("xj_d0").shape[1]
            both = plan.get("r_u0")
            wide = both.shape[2] // 2
            moved_grads[0] = [both[:, :, :wide], both[:, :, wide:], last[:, :tall]]
            moved_grads[1] = [plan.get("r_" + name + "1") for name in "gud"]
            last_out = last[:, tall:]
        part = part.astype(f32)
        qkv_owned = part[:, :, :share_of].transpose(1, 0, 2).reshape(own_rows, 3 * width)
        thin_owned = jnp.sum(part[:, :, share_of:], axis=0)
        if by_chunks:
            out_owned = jnp.sum(last_out.astype(f32), axis=0)
        else:
            moved_grads[layer] = [deal_out(part) for part in halves]
            out_owned = lax.psum_scatter(
                out_w_grad, every_axis, scatter_dimension=0, tiled=True
            ).astype(f32)
        results[layer] = (qkv_owned, out_owned, thin_owned)
    if by_chunks:
        owned = after(plan.get("rs"), last).astype(f32)
        results[1] = (owned[:, width : 4 * width], owned[:, :width], owned[:, 4 * width :])

    def stack(parts):
        return jnp.stack(parts)

    thin_all = [results[layer][2] for layer in range(LAYERS)]
    return (
        output_rows[None],
        grad[None],
        stack([results[layer][0] for layer in range(LAYERS)]),
        stack([results[layer][1] for layer in range(LAYERS)]),
        stack([moved_grads[layer][0].astype(f32) for layer in range(LAYERS)]),
        stack([moved_grads[layer][1].astype(f32) for layer in range(LAYERS)]),
        stack([moved_grads[layer][2].astype(f32) for layer in range(LAYERS)]),
        stack([thin[:, AT_ATTN] for thin in thin_all]),
        stack([thin[:, AT_MOE] for thin in thin_all]),
        stack([thin[:, :ROUTED] for thin in thin_all]),
        stack([thin[:, AT_CONST : AT_CONST + 4] for thin in thin_all]),
        stack([thin[:, AT_CVEC : AT_CVEC + 2] for thin in thin_all]),
    )


def solution(mesh):
    devices = mesh.devices
    axes = ctx_axes(devices.shape[0])
    every_axis = axes + (FS,)
    finer = Mesh(devices.reshape((2,) * len(axes) + (devices.shape[1],)), every_axis)
    token_spec = P(FS, axes, None)
    row_spec = P(None, every_axis, None)
    expert_spec = P(None, None, every_axis, None)
    gain_spec = P(None, every_axis)
    return jax.shard_map(
        functools.partial(shards, axes),
        mesh=finer,
        in_specs=(
            token_spec,
            token_spec,
            token_spec,
            P(FS, axes),
            P(),
            row_spec,
            row_spec,
            expert_spec,
            expert_spec,
            expert_spec,
            gain_spec,
            gain_spec,
            row_spec,
            row_spec,
            row_spec,
            token_spec,
        ),
        out_specs=(
            token_spec,
            token_spec,
            row_spec,
            row_spec,
            expert_spec,
            expert_spec,
            expert_spec,
            gain_spec,
            gain_spec,
            row_spec,
            row_spec,
            row_spec,
        ),
        check_vma=False,
    )
```

```python
import functools

import jax
import jax.numpy as jnp
from jax import lax
from jax.experimental import pallas as pl
from jax.experimental.pallas import tpu as pltpu
from jax.sharding import Mesh
from jax.sharding import PartitionSpec as P

HEADS = 12
HEAD_DIM = 64
EXPERTS = 8
TOP = 2
LAYERS = 2
ROUTED = 12
CAP = 26
SLOTS = 32
LANES = 128
PAIRS = HEADS // 2

FS = "fsdp"


def ctx_axes(size):
    return tuple(f"ctx{at}" for at in range(size.bit_length() - 1))


norm_eps = 1e-06
masked_score = -1e30
highest = lax.Precision.HIGHEST
f32 = jnp.float32
bf16 = jnp.bfloat16
VMEM_LIMIT = 56 * 1024 * 1024
SPLIT = 3

AT_CONST = 16
AT_CVEC = 24
AT_ATTN = 32
AT_MOE = 33


def dot_nn(a, b):
    return lax.dot_general(a, b, (((1,), (0,)), ((), ())), preferred_element_type=f32)


def dot_nt(a, b):
    return lax.dot_general(a, b, (((1,), (1,)), ((), ())), preferred_element_type=f32)


def dot_tn(a, b):
    return lax.dot_general(a, b, (((0,), (0,)), ((), ())), preferred_element_type=f32)


def kernel_params(steps):
    return pltpu.CompilerParams(
        dimension_semantics=("arbitrary",) * steps, vmem_limit_bytes=VMEM_LIMIT
    )


def turn_lanes(x, cosine, sine):
    lane = lax.broadcasted_iota(jnp.int32, x.shape, 1)
    ahead = pltpu.roll(x, LANES - HEAD_DIM // 2, 1)
    behind = pltpu.roll(x, HEAD_DIM // 2, 1)
    partner = jnp.where(lane % HEAD_DIM < HEAD_DIM // 2, ahead, behind)
    return x * cosine + partner * sine


def once(shape, index):
    return pl.BlockSpec(shape, index, pipeline_mode=pl.Buffered(1))


def project_kernel(turned, count, fresh, *refs):
    w_ref, small_ref, cos_ref, sin_ref, out_ref = refs[count : count + 5]
    sources = [(ref, 0, ref.shape[0]) for ref in refs[:count]]
    if fresh:
        low_ref = refs[count + 5]

        @pl.when(pl.program_id(0) == 0)
        def _():
            line = line_of(small_ref, AT_ATTN)
            start = 0
            for ref, _, tall in sources:
                x = ref[...].astype(f32)
                low_ref[start : start + tall] = (x * root_scale(x) * line).astype(bf16)
                start += tall

        sources = [(low_ref, 0, low_ref.shape[0])]
    weights = w_ref[...]

    def walk(turn):
        start = 0
        for a_ref, _, whole in sources:
            for low in range(0, whole, 256):
                tall = min(256, whole - low)
                acc = dot_nn(a_ref[low : low + tall], weights)
                place = slice(start + low, start + low + tall)
                for at in range(0, acc.shape[1], LANES):
                    part = acc[:, at : at + LANES]
                    if turn:
                        part = turn_lanes(part, cos_ref[place], sin_ref[place])
                    out_ref[place, at : at + LANES] = part.astype(bf16)
            start += whole

    @pl.when(pl.program_id(0) < turned)
    def _():
        walk(True)

    @pl.when(pl.program_id(0) >= turned)
    def _():
        walk(False)


def project(blocks, packed, cosine, sine, fresh=False):
    width = blocks[0].shape[1]
    count = sum(block.shape[0] for block in blocks)
    tile = width // SPLIT
    table = once((count, LANES), lambda i: (0, 0))
    return pl.pallas_call(
        functools.partial(project_kernel, 2 * SPLIT, len(blocks), fresh),
        grid=(3 * SPLIT,),
        in_specs=[once(block.shape, lambda i: (0, 0)) for block in blocks]
        + [pl.BlockSpec((width, tile), lambda i: (0, i))]
        + [once((width, LANES), lambda i: (0, 4 * width // LANES)), table, table],
        out_specs=pl.BlockSpec((count, tile), lambda i: (0, i)),
        out_shape=jax.ShapeDtypeStruct((count, 3 * width), bf16),
        scratch_shapes=[pltpu.VMEM((count, width), bf16)] if fresh else [],
        compiler_params=kernel_params(1),
        cost_estimate=pl.CostEstimate(
            flops=6 * count * width * width,
            bytes_accessed=2 * width * (4 * count + 3 * width),
            transcendentals=0,
        ),
    )(*blocks, packed, packed, cosine, sine)


def split_heads(x):
    wide = x.astype(f32)
    left = lax.broadcasted_iota(jnp.int32, wide.shape, 1) < HEAD_DIM
    zero = jnp.zeros_like(wide)
    return jnp.concatenate(
        [jnp.where(left, wide, zero), jnp.where(left, zero, wide)], axis=0
    ).astype(bf16)


def join_heads(x, rows):
    left = lax.broadcasted_iota(jnp.int32, (rows, LANES), 1) < HEAD_DIM
    return jnp.where(left, x[:rows], x[rows:])


def attend_kernel(
    prompt, q_ref, k_ref, v_ref, at_ref, start_ref, key_ref, o_ref, total_ref, bias_ref
):
    pair = pl.program_id(0)
    rows = q_ref.shape[0]

    @pl.when(pair == 0)
    def _():
        places, keys = at_ref[...], key_ref[...]
        seen = (keys <= places) & ((keys < prompt) | (keys >= start_ref[...]))
        bias_ref[...] = jnp.where(seen, 0.0, masked_score)
        total_ref[...] = jnp.zeros_like(total_ref)

    queries = split_heads(q_ref[...] * HEAD_DIM ** (-0.5))
    keys, values = k_ref[...], v_ref[...]
    lane = lax.broadcasted_iota(jnp.int32, (rows, LANES), 1)
    outs = []
    totals = total_ref[...]
    for side in range(2):
        scores = dot_nt(queries[side * rows : (side + 1) * rows], keys) + bias_ref[...]
        top = jnp.max(scores, axis=1, keepdims=True)
        expo = jnp.exp(scores - top)
        total = jnp.sum(expo, axis=1, keepdims=True)
        outs.append(dot_nn(expo.astype(bf16), values) / total)
        totals = jnp.where(lane == 2 * pair + side, top + jnp.log(total), totals)
    o_ref[...] = jnp.where(lane < HEAD_DIM, outs[0], outs[1])
    total_ref[...] = totals


def attend(projected, places, starts, key_places, prompt):
    rows = places.shape[0]
    length, width = projected.shape[0], projected.shape[1] // 3
    own = pl.BlockSpec((rows, LANES), lambda j: (0, j))
    keys = pl.BlockSpec((length, LANES), lambda j: (0, PAIRS + j))
    values = pl.BlockSpec((length, LANES), lambda j: (0, 2 * PAIRS + j))
    column = pl.BlockSpec((rows, 1), lambda j: (0, 0))
    line = pl.BlockSpec((1, length), lambda j: (0, 0))
    return pl.pallas_call(
        functools.partial(attend_kernel, prompt),
        grid=(PAIRS,),
        in_specs=[own, keys, values, column, column, line],
        out_specs=[own, pl.BlockSpec((rows, LANES), lambda j: (0, 0))],
        out_shape=[
            jax.ShapeDtypeStruct((rows, width), f32),
            jax.ShapeDtypeStruct((rows, LANES), f32),
        ],
        scratch_shapes=[pltpu.VMEM((rows, length), f32)],
        compiler_params=kernel_params(1),
        cost_estimate=pl.CostEstimate(
            flops=8 * rows * length * width,
            bytes_accessed=4 * length * width,
            transcendentals=rows * length * HEADS,
        ),
    )(projected, projected, projected, places, starts, key_places)


def pick_column(table, at):
    lane = lax.broadcasted_iota(jnp.int32, table.shape, 1)
    return jnp.sum(jnp.where(lane == at, table, 0.0), axis=1, keepdims=True)


def query_kernel(
    prompt,
    start,
    q_ref,
    g_ref,
    k_ref,
    v_ref,
    total_ref,
    delta_ref,
    at_ref,
    start_ref,
    key_ref,
    cos_ref,
    sin_ref,
    out_ref,
    bias_ref,
):
    pair = pl.program_id(0) + start
    rows = q_ref.shape[0]

    @pl.when(pair == start)
    def _():
        places, keys = at_ref[...], key_ref[...]
        seen = (keys <= places) & ((keys < prompt) | (keys >= start_ref[...]))
        bias_ref[...] = jnp.where(seen, 0.0, masked_score)

    scale = HEAD_DIM ** (-0.5)
    queries = split_heads(q_ref[...] * scale)
    grads = split_heads(g_ref[...])
    keys, values = k_ref[...], v_ref[...]
    lane = lax.broadcasted_iota(jnp.int32, (rows, LANES), 1)
    outs = []
    for side in range(2):
        part = slice(side * rows, (side + 1) * rows)
        total = pick_column(total_ref[...], 2 * pair + side)
        delta = pick_column(delta_ref[...], 2 * pair + side)
        scores = dot_nt(queries[part], keys) + bias_ref[...]
        probs = jnp.exp(scores - total)
        prob_grad = dot_nt(grads[part], values)
        score_grad = (probs * (prob_grad - delta)).astype(bf16)
        outs.append(dot_nn(score_grad, keys))
    out = jnp.where(lane < HEAD_DIM, outs[0], outs[1]) * scale
    out_ref[...] = turn_lanes(out, cos_ref[...], -sin_ref[...]).astype(bf16)


def query_back(
    start, count, projected, grads, totals, delta, places, starts, key_places, cosine, sine, prompt
):
    rows = places.shape[0]
    length = projected.shape[0]
    own = pl.BlockSpec((rows, LANES), lambda j: (0, j + start))
    keys = pl.BlockSpec((length, LANES), lambda j: (0, PAIRS + j + start))
    values = pl.BlockSpec((length, LANES), lambda j: (0, 2 * PAIRS + j + start))
    same = pl.BlockSpec((rows, LANES), lambda j: (0, 0))
    column = pl.BlockSpec((rows, 1), lambda j: (0, 0))
    line = pl.BlockSpec((1, length), lambda j: (0, 0))
    width = count * LANES
    return pl.pallas_call(
        functools.partial(query_kernel, prompt, start),
        grid=(count,),
        in_specs=[own, own, keys, values, same, same, column, column, line, same, same],
        out_specs=pl.BlockSpec((rows, LANES), lambda j: (0, j)),
        out_shape=jax.ShapeDtypeStruct((rows, width), bf16),
        scratch_shapes=[pltpu.VMEM((rows, length), f32)],
        compiler_params=kernel_params(1),
        cost_estimate=pl.CostEstimate(
            flops=12 * rows * length * width,
            bytes_accessed=4 * length * width,
            transcendentals=rows * length * HEADS,
        ),
    )(
        projected,
        grads,
        projected,
        projected,
        totals,
        delta,
        places,
        starts,
        key_places,
        cosine,
        sine,
    )


def key_kernel(prompt, count, k_ref, v_ref, q_ref, *refs):
    grad_refs, stat_refs = refs[:count], refs[count : 2 * count]
    own_ref, at_ref, start_ref, cos_ref, sin_ref = refs[2 * count : 2 * count + 5]
    dk_ref, dv_ref, bias_ref, lines_ref = refs[2 * count + 5 :]
    pair = pl.program_id(0)
    rows = k_ref.shape[0]

    @pl.when(pair == 0)
    def _():
        keys, places = own_ref[...], at_ref[...]
        seen = (keys <= places) & ((keys < prompt) | (keys >= start_ref[...]))
        bias_ref[...] = jnp.where(seen, 0.0, masked_score)
        flat = stack_rows(stat_refs).astype(f32).T
        for head in range(HEADS):
            lines_ref[head] = flat[head : head + 1] + flat[16 + head : 17 + head]
            lines_ref[16 + head] = flat[32 + head : 33 + head] + flat[48 + head : 49 + head]

    scale = HEAD_DIM ** (-0.5)
    own_keys = split_heads(k_ref[...] * scale)
    own_values = split_heads(v_ref[...])
    queries, grads = q_ref[...], stack_rows(grad_refs)
    lane = lax.broadcasted_iota(jnp.int32, (rows, LANES), 1)
    key_outs, value_outs = [], []
    for side in range(2):
        part = slice(side * rows, (side + 1) * rows)
        total = lines_ref[2 * pair + side]
        delta = lines_ref[16 + 2 * pair + side]
        scores = dot_nt(own_keys[part], queries) + bias_ref[...]
        probs = jnp.exp(scores - total)
        value_outs.append(dot_nn(probs.astype(bf16), grads))
        prob_grad = dot_nt(own_values[part], grads)
        score_grad = (probs * (prob_grad - delta)).astype(bf16)
        key_outs.append(dot_nn(score_grad, queries))
    left = lane < HEAD_DIM
    dk = jnp.where(left, key_outs[0], key_outs[1]) * scale
    dk_ref[...] = turn_lanes(dk, cos_ref[...], -sin_ref[...]).astype(bf16)
    dv_ref[...] = jnp.where(left, value_outs[0], value_outs[1]).astype(bf16)


def key_back(projected, sent, own_places, places, starts, cosine, sine, prompt):
    rows = own_places.shape[0]
    length, width = projected.shape[0], projected.shape[1] // 3
    out = pl.BlockSpec((rows, LANES), lambda j: (0, j))
    keys = pl.BlockSpec((rows, LANES), lambda j: (0, PAIRS + j))
    values = pl.BlockSpec((rows, LANES), lambda j: (0, 2 * PAIRS + j))
    every = pl.BlockSpec((length, LANES), lambda j: (0, j))
    same = pl.BlockSpec((rows, LANES), lambda j: (0, 0))
    column = pl.BlockSpec((rows, 1), lambda j: (0, 0))
    line = pl.BlockSpec((1, length), lambda j: (0, 0))
    return pl.pallas_call(
        functools.partial(key_kernel, prompt, len(sent)),
        grid=(PAIRS,),
        in_specs=[keys, values, every]
        + [pl.BlockSpec((block.shape[0], LANES), lambda j: (0, j)) for block in sent]
        + [pl.BlockSpec((block.shape[0], LANES), lambda j: (0, PAIRS)) for block in sent]
        + [column, line, line, same, same],
        out_specs=[out, out],
        out_shape=[jax.ShapeDtypeStruct((rows, width), bf16)] * 2,
        scratch_shapes=[
            pltpu.VMEM((rows, length), f32),
            pltpu.VMEM((32, 1, length), f32),
        ],
        compiler_params=kernel_params(1),
        cost_estimate=pl.CostEstimate(
            flops=16 * rows * length * width,
            bytes_accessed=4 * length * width,
            transcendentals=rows * length * HEADS,
        ),
    )(projected, projected, projected, *sent, *sent, own_places, places, starts, cosine, sine)


def cross(x, flag_ref):
    tall = x.shape[0]
    far = jnp.full((tall, LANES), flag_ref[0, 0], jnp.int32) > 0
    near = jnp.full((tall, LANES), flag_ref[0, 1], jnp.int32) > 0
    left, right = x[:, :LANES], x[:, LANES:]
    left = jnp.where(near, pltpu.roll(left, HEAD_DIM, 1), left)
    right = jnp.where(near, pltpu.roll(right, HEAD_DIM, 1), right)
    return jnp.concatenate(
        [jnp.where(far, right, left), jnp.where(far, left, right)], axis=1
    )


def stack_rows(refs):
    return jnp.concatenate([ref[...] for ref in refs], axis=0)


def expert_kernel(flag_ref, x_ref, *refs):
    gates, ups, downs = refs[:4], refs[4:8], refs[8:12]
    gate_ref, up_ref, out_ref, acc_ref = refs[12:]
    step = pl.program_id(0)
    x = x_ref[...]
    gate = dot_nn(x, stack_rows(gates))
    up = dot_nn(x, stack_rows(ups))
    gate_ref[...] = gate
    up_ref[...] = up
    inner = cross(gate * jax.nn.sigmoid(gate) * up, flag_ref).astype(bf16)
    out = dot_nn(inner, stack_rows(downs))

    @pl.when(step == 0)
    def _():
        acc_ref[...] = out

    @pl.when(step > 0)
    def _():
        acc_ref[...] += out

    @pl.when(step == pl.num_programs(0) - 1)
    def _():
        out_ref[...] = acc_ref[...].astype(bf16)


def expert_specs(width, hidden):
    tile = hidden // EXPERTS
    tall = pl.BlockSpec((width // 4, tile), lambda j: (0, j))
    flat = pl.BlockSpec((tile // 4, width), lambda j: (j, 0))
    return tile, [tall] * 8 + [flat] * 4


def run_expert(flags, x, gates, ups, downs):
    rows, width = x.shape
    hidden = gates[0].shape[1]
    tile, specs = expert_specs(width, hidden)
    whole = pl.BlockSpec((rows, width), lambda j: (0, 0))
    column = pl.BlockSpec((rows, tile), lambda j: (0, j))
    return pl.pallas_call(
        expert_kernel,
        grid=(EXPERTS,),
        in_specs=[pl.BlockSpec(memory_space=pltpu.SMEM), whole] + specs,
        out_specs=[column, column, whole],
        out_shape=[
            jax.ShapeDtypeStruct((rows, hidden), f32),
            jax.ShapeDtypeStruct((rows, hidden), f32),
            jax.ShapeDtypeStruct((rows, width), bf16),
        ],
        scratch_shapes=[pltpu.VMEM((rows, width), f32)],
        compiler_params=kernel_params(1),
        cost_estimate=pl.CostEstimate(
            flops=6 * rows * width * hidden,
            bytes_accessed=6 * width * hidden + 8 * rows * hidden,
            transcendentals=rows * hidden,
        ),
    )(flags, x, *gates, *ups, *downs)


def expert_back_kernel(both, flag_ref, x_ref, grad_ref, order_ref, *refs):
    if not both:
        gate_ref, up_ref = refs[:2]
        refs = refs[2:]
    gates, ups, downs = refs[:4], refs[4:8], refs[8:12]
    outs, back_ref = refs[12:18], refs[18]
    acc_ref, turned_ref = refs[19:21]
    step = pl.program_id(0)
    last = step == pl.num_programs(0) - 1
    width = x_ref.shape[1]

    @pl.when(step == 0)
    def _():
        turned_ref[...] = x_ref[...].astype(f32).T.astype(bf16)

    grad = grad_ref[...]
    gate_w, up_w, down_w = stack_rows(gates), stack_rows(ups), stack_rows(downs)
    if both:
        x = x_ref[...]
        gate, up = dot_nn(x, gate_w), dot_nn(x, up_w)
    else:
        gate, up = gate_ref[...], up_ref[...]
    sigma = jax.nn.sigmoid(gate)
    gated = gate * sigma
    inner = cross(gated * up, flag_ref)
    inner_grad = cross(dot_nt(grad, down_w), flag_ref)
    up_low = (inner_grad * gated).astype(bf16)
    gate_low = (inner_grad * up * (sigma + gated * (1.0 - sigma))).astype(bf16)
    parts = [dot_nt(gate_low, gate_w) + dot_nt(up_low, up_w)]
    if both:
        parts.append(dot_nn(inner.astype(bf16), down_w))
    part = jnp.concatenate(parts, axis=1) if both else parts[0]

    @pl.when(step == 0)
    def _():
        acc_ref[...] = part

    @pl.when(step > 0)
    def _():
        acc_ref[...] += part

    @pl.when(last)
    def _():
        in_low = acc_ref[:, :width].astype(bf16)
        back_ref[:, :width] = dot_nt(in_low, order_ref[...]).astype(bf16)
        if both:
            back_ref[:, width:] = acc_ref[:, width:].astype(bf16)

    turned = turned_ref[...]
    members = (
        dot_nn(turned, gate_low).astype(bf16),
        dot_nn(turned, up_low).astype(bf16),
        dot_nn(inner.T.astype(bf16), grad).astype(bf16),
    )
    for at, member in enumerate(members):
        half = member.shape[0] // 2
        outs[2 * at][...] = member[:half]
        outs[2 * at + 1][...] = member[half:]


def run_expert_back(flags, received, order, gate, up, gates, ups, downs):
    both = gate is None
    if both:
        rows, width = received[0].shape[0], received[0].shape[1] // 2
    else:
        rows, width = received[0].shape
    hidden = gates[0].shape[1]
    tile, specs = expert_specs(width, hidden)
    first = pl.BlockSpec((rows, width), lambda j: (0, 0))
    beside = pl.BlockSpec((rows, width), lambda j: (0, 1)) if both else first
    table = pl.BlockSpec((width, width), lambda j: (0, 0))
    column = pl.BlockSpec((rows, tile), lambda j: (0, j))
    tall = pl.BlockSpec((width // 2, tile), lambda j: (0, j))
    flat = pl.BlockSpec((None, tile // 2, width), lambda j: (j, 0, 0))
    tall_shape = jax.ShapeDtypeStruct((width // 2, hidden), bf16)
    flat_shape = jax.ShapeDtypeStruct((EXPERTS, tile // 2, width), bf16)
    wide = 2 * width if both else width
    *halves, back = pl.pallas_call(
        functools.partial(expert_back_kernel, both),
        grid=(EXPERTS,),
        in_specs=[pl.BlockSpec(memory_space=pltpu.SMEM), first, beside, table]
        + ([] if both else [column, column])
        + specs,
        out_specs=[tall] * 4 + [flat] * 2 + [pl.BlockSpec((rows, wide), lambda j: (0, 0))],
        out_shape=[tall_shape] * 4
        + [flat_shape] * 2
        + [jax.ShapeDtypeStruct((rows, wide), bf16)],
        scratch_shapes=[pltpu.VMEM((rows, wide), f32), pltpu.VMEM((width, rows), bf16)],
        compiler_params=kernel_params(1),
        cost_estimate=pl.CostEstimate(
            flops=(18 if both else 12) * rows * width * hidden,
            bytes_accessed=12 * width * hidden + 8 * rows * hidden,
            transcendentals=rows * hidden,
        ),
    )(flags, *received, order, *([] if both else [gate, up]), *gates, *ups, *downs)
    return halves, back


def product_kernel(x_ref, g_ref, *refs):
    thin_ref = refs[0] if len(refs) == 3 else None
    kept_ref, given_ref = refs[-2:]
    turned = x_ref[...].astype(f32).T.astype(bf16)
    half = turned.shape[0] // 2
    wide = g_ref.shape[1]
    span = turned.shape[0]
    for at in range(0, wide, span):
        part = dot_nn(turned, g_ref[:, at : at + span]).astype(bf16)
        kept_ref[:, at : at + span] = part[:half]
        given_ref[:, at : at + span] = part[half:]
    if thin_ref is not None:
        kept_ref[:, wide:] = thin_ref[:half]
        given_ref[:, wide:] = thin_ref[half:]


def weight_product(x, grad, thin=None):
    rows, width = x.shape
    wide = grad.shape[1] + (0 if thin is None else thin.shape[1])
    shape = jax.ShapeDtypeStruct((width // 2, wide), bf16)
    vmem = pl.BlockSpec(memory_space=pltpu.VMEM)
    return pl.pallas_call(
        product_kernel,
        in_specs=[vmem] * (2 if thin is None else 3),
        out_specs=[vmem] * 2,
        out_shape=[shape] * 2,
        compiler_params=pltpu.CompilerParams(vmem_limit_bytes=VMEM_LIMIT),
        cost_estimate=pl.CostEstimate(
            flops=2 * rows * width * wide,
            bytes_accessed=2 * (width * wide + rows * (width + wide)),
            transcendentals=0,
        ),
    )(x, grad, *([] if thin is None else [thin]))


def lanes_of(rows):
    return lax.broadcasted_iota(jnp.int32, (rows, LANES), 1)


def two_part_nn(a, b):
    top = a.astype(bf16)
    return dot_nn(top, b) + dot_nn((a - top.astype(f32)).astype(bf16), b)


def two_part_nt(a, b):
    top = a.astype(bf16)
    return dot_nt(top, b) + dot_nt((a - top.astype(f32)).astype(bf16), b)


def root_scale(x):
    return lax.rsqrt(jnp.mean(x * x, axis=1, keepdims=True) + norm_eps)


def line_of(small_ref, at):
    return small_ref[...].astype(f32).T[at : at + 1]


def norm_kernel(*refs):
    small_ref, out_ref = refs[-2:]
    line = line_of(small_ref, AT_ATTN)
    start = 0
    for x_ref in refs[:-2]:
        tall = x_ref.shape[0]
        x = x_ref[...].astype(f32)
        out_ref[start : start + tall] = (x * root_scale(x) * line).astype(bf16)
        start += tall


def norm_rows(blocks, packed):
    width = blocks[0].shape[1]
    count = sum(block.shape[0] for block in blocks)
    return pl.pallas_call(
        norm_kernel,
        grid=(1,),
        in_specs=[once(block.shape, lambda i: (0, 0)) for block in blocks]
        + [pl.BlockSpec((width, LANES), lambda i: (0, 4 * width // LANES))],
        out_specs=once((count, width), lambda i: (0, 0)),
        out_shape=jax.ShapeDtypeStruct((count, width), bf16),
        compiler_params=kernel_params(1),
        cost_estimate=pl.CostEstimate(
            flops=8 * count * width, bytes_accessed=4 * count * width, transcendentals=0
        ),
    )(*blocks, packed)


def pair_partner(x):
    lane = lanes_of(x.shape[0])
    return jnp.where(lane % 2 == 0, pltpu.roll(x, LANES - 1, 1), pltpu.roll(x, 1, 1))


def side_weights(chances, mixes, chosen):
    weight = chances * chosen
    last = [pick_column(weight, 9 + at) for at in range(3)]
    mix = [pick_column(mixes, AT_CONST + at) for at in range(4)]
    alpha = last[0] + last[1] * mix[0] + last[2] * mix[2]
    return last, mix, alpha, (last[1] * mix[1], last[2] * mix[3])


def slots_of_grad(grad, chances, picks, slot_pairs):
    parts = [jnp.sum(chances * pick, axis=1, keepdims=True) * grad for pick in picks]
    return dot_nn(slot_pairs, jnp.concatenate(parts, axis=0).astype(bf16)).astype(bf16)


def to_expert_kernel(
    final,
    att_ref,
    hidden_ref,
    wout_ref,
    small_ref,
    previous_ref,
    slot_tokens_ref,
    order_ref,
    *refs,
):
    if final:
        grad_ref, first_ref, second_ref, slot_pairs_ref = refs[:4]
        refs = refs[4:]
    mid_ref, logit_ref, chance_ref, mix_ref, message_ref = refs
    mid = hidden_ref[...] + dot_nn(att_ref[...].astype(bf16), wout_ref[...])
    mid_ref[...] = mid
    low = (mid * root_scale(mid) * line_of(small_ref, AT_MOE)).astype(bf16)
    thin = dot_nn(low, small_ref[...])
    lane = lanes_of(mid.shape[0])
    logits = jnp.where(lane < ROUTED, thin + previous_ref[...], 0.0)
    logit_ref[...] = logits
    top = jnp.max(jnp.where(lane < ROUTED, logits, masked_score), axis=1, keepdims=True)
    expo = jnp.where(lane < ROUTED, jnp.exp(logits - top), 0.0)
    chances = expo / jnp.sum(expo, axis=1, keepdims=True)
    chance_ref[...] = chances
    inside = (lane >= AT_CONST) & (lane < AT_CONST + 4)
    apart = jnp.where(inside, thin - pair_partner(thin), 0.0)
    mix_ref[...] = jnp.where(inside, jax.nn.sigmoid(apart), 0.0)
    width = mid.shape[1]
    moved = dot_nn(low, order_ref[...]).astype(bf16)
    message_ref[:, :width] = dot_nn(slot_tokens_ref[...], moved).astype(bf16)
    if final:
        message_ref[:, width:] = slots_of_grad(
            grad_ref[...].astype(f32),
            chances,
            (first_ref[...], second_ref[...]),
            slot_pairs_ref[...],
        )


def from_expert_kernel(
    final, mid_ref, chance_ref, mix_ref, first_ref, second_ref, small_ref, pair_slots_ref, back_ref, *refs
):
    if final:
        (out_ref,) = refs
    else:
        next_ref, out_ref, normed_ref = refs
    mid = mid_ref[...]
    rows, width = mid.shape
    picks = (first_ref[...], second_ref[...])
    chances = chance_ref[...]
    _, _, alpha, betas = side_weights(chances, mix_ref[...], picks[0] + picks[1])
    lines = small_ref[...].astype(f32).T
    out = mid + alpha * (mid * root_scale(mid) * lines[AT_MOE : AT_MOE + 1])
    out += betas[0] * lines[AT_CVEC : AT_CVEC + 1] + betas[1] * lines[AT_CVEC + 1 : AT_CVEC + 2]
    pairs = dot_nn(pair_slots_ref[...], back_ref[...])
    for at in range(TOP):
        picked = jnp.sum(chances * picks[at], axis=1, keepdims=True)
        out += picked * pairs[at * rows : (at + 1) * rows]
    out_ref[...] = out.astype(out_ref.dtype)
    if not final:
        normed_ref[...] = (out * root_scale(out) * line_of(next_ref, AT_ATTN)).astype(bf16)


def rms_back_rows(values, gain, grad):
    scale = root_scale(values)
    inner = grad * gain
    along = jnp.mean(inner * values, axis=1, keepdims=True)
    gain_grad = jnp.sum(grad * values * scale, axis=0, keepdims=True)
    return scale * inner - values * (scale * scale * scale * along), gain_grad


def to_attention_kernel(
    grad_ref,
    mid_ref,
    chance_ref,
    mix_ref,
    first_ref,
    second_ref,
    small_ref,
    pair_slots_ref,
    token_slots_ref,
    back_ref,
    in_back_ref,
    next_ref,
    wout_ref,
    att_ref,
    total_ref,
    head_ref,
    mid_grad_ref,
    mid_low_ref,
    sent_ref,
    delta_ref,
    thin_grad_ref,
    thin_w_ref,
    line_grad_ref,
):
    grad, mid = grad_ref[...].astype(f32), mid_ref[...]
    rows, width = mid.shape
    picks = (first_ref[...], second_ref[...])
    chosen = picks[0] + picks[1]
    chances, mixes = chance_ref[...], mix_ref[...]
    last, mix, alpha, betas = side_weights(chances, mixes, chosen)
    lines = small_ref[...].astype(f32).T
    gain = lines[AT_MOE : AT_MOE + 1]
    cvecs = [lines[AT_CVEC + c : AT_CVEC + 1 + c] for c in range(2)]
    mixed = mid * root_scale(mid) * gain
    pairs = dot_nn(pair_slots_ref[...], back_ref[...])
    along = jnp.sum(grad * mixed, axis=1, keepdims=True)
    across = [jnp.sum(grad * cvecs[c], axis=1, keepdims=True) for c in range(2)]
    lane = lanes_of(rows)
    chance_grad = jnp.where(lane == 9, along, 0.0)
    for c in range(2):
        both = mix[2 * c] * along + mix[2 * c + 1] * across[c]
        chance_grad = jnp.where(lane == 10 + c, both, chance_grad)
    chance_grad *= chosen
    for at in range(TOP):
        part = jnp.sum(grad * pairs[at * rows : (at + 1) * rows], axis=1, keepdims=True)
        chance_grad += picks[at] * part
    logit_grad = chances * (
        chance_grad - jnp.sum(chances * chance_grad, axis=1, keepdims=True)
    ) + jnp.where(lane < ROUTED, next_ref[...], 0.0)
    mix_grad = jnp.zeros_like(mixes)
    for c in range(2):
        mix_grad = jnp.where(lane == AT_CONST + 2 * c, last[1 + c] * along, mix_grad)
        mix_grad = jnp.where(lane == AT_CONST + 2 * c + 1, last[1 + c] * across[c], mix_grad)
    product = mixes * mix_grad
    thin_grad = logit_grad + mixes * (mix_grad - (product + pair_partner(product)))
    thin_grad_ref[...] = thin_grad
    low_grad = (
        alpha * grad
        + two_part_nt(thin_grad, small_ref[...])
        + dot_nn(token_slots_ref[...], in_back_ref[...])
    )
    mid_part, gain_grad = rms_back_rows(mid, gain, low_grad)
    mid_grad = grad + mid_part
    mid_grad_ref[...] = mid_grad
    mid_low = mid_grad.astype(bf16)
    mid_low_ref[...] = mid_low
    att_grad = dot_nt(mid_low, wout_ref[...]).astype(bf16)
    delta = two_part_nn(att_grad.astype(f32) * att_ref[...], head_ref[...])
    delta_ref[...] = delta
    sent_ref[:, :width] = att_grad
    stats = jnp.zeros((rows, LANES), f32)
    for at, stat in enumerate((total_ref[...], delta)):
        top = stat.astype(bf16).astype(f32)
        for part, piece in enumerate((top, stat - top)):
            place = 32 * at + 16 * part
            stats += pltpu.roll(piece, place, 1) if place else piece
    sent_ref[:, width:] = stats.astype(bf16)
    turned = mixed.T.astype(bf16)
    thin_w_ref[...] = two_part_tn(turned, thin_grad)
    line_grad_ref[...] = jnp.concatenate(
        [gain_grad]
        + [jnp.sum(betas[c] * grad, axis=0, keepdims=True) for c in range(2)]
        + [jnp.zeros((5, width), f32)],
        axis=0,
    )


def two_part_tn(turned, x):
    top = x.astype(bf16)
    return dot_nn(turned, top) + dot_nn(turned, (x - top.astype(f32)).astype(bf16))


def from_attention_kernel(final, *refs):
    q_refs, (k_ref, v_ref, wq_ref, wk_ref, wv_ref) = refs[:3], refs[3:8]
    hidden_ref, small_ref, mid_grad_ref = refs[8:11]
    refs = refs[11:]
    if final:
        grad_ref, line_grad_ref = refs
    else:
        chance_ref, first_ref, second_ref, slot_pairs_ref, grad_ref, line_grad_ref, message_ref = refs
    queries = jnp.concatenate([ref[...] for ref in q_refs], axis=1)
    normed_grad = dot_nt(queries, wq_ref[...])
    normed_grad += dot_nt(k_ref[...], wk_ref[...])
    normed_grad += dot_nt(v_ref[...], wv_ref[...])
    part, gain_grad = rms_back_rows(
        hidden_ref[...], line_of(small_ref, AT_ATTN), normed_grad
    )
    grad = mid_grad_ref[...] + part
    grad_ref[...] = grad
    line_grad_ref[...] = jnp.concatenate(
        [gain_grad, jnp.zeros((7, gain_grad.shape[1]), f32)], axis=0
    )
    if not final:
        message_ref[...] = slots_of_grad(
            grad, chance_ref[...], (first_ref[...], second_ref[...]), slot_pairs_ref[...]
        )


class Block:
    def __init__(self, array, wide, at):
        self.array, self.wide, self.at = array, wide, at


def run_fused(kernel, args, outs, flops):
    arrays, specs = [], []
    for arg in args:
        if isinstance(arg, Block):
            arrays.append(arg.array)
            specs.append(
                pl.BlockSpec(
                    (arg.array.shape[0], arg.wide),
                    functools.partial(lambda at, i: (0, at), arg.at),
                )
            )
        else:
            arrays.append(arg)
            specs.append(pl.BlockSpec(arg.shape, lambda i: (0, 0)))
    return pl.pallas_call(
        kernel,
        grid=(1,),
        in_specs=specs,
        out_specs=[pl.BlockSpec(shape, lambda i: (0, 0)) for shape, _ in outs],
        out_shape=[jax.ShapeDtypeStruct(shape, dtype) for shape, dtype in outs],
        compiler_params=kernel_params(1),
        cost_estimate=pl.CostEstimate(flops=flops, bytes_accessed=1 << 22, transcendentals=0),
    )(*arrays)


def after(x, *things):
    return lax.optimization_barrier((x,) + things)[0]


TABLE = {
    "a_g0": ("", ""),
    "a_u0": ("", "packed0"),
    "a_d0": ("packed0", "proj0"),
    "x_g0": ("", "packed0"),
    "x_u0": ("packed0", "proj0"),
    "x_d0": ("proj0", "ein0"),
    "c_g0": ("packed0", ""),
    "c_u0": ("proj0", ""),
    "c_d0": ("", ""),
    "k_1": ("proj0", ""),
    "a_g1": ("proj0", "msg0"),
    "a_u1": ("ein0", "eout0"),
    "a_d1": ("ag1", "att1"),
    "x_g1": ("eout0", "ag1"),
    "x_u1": ("ag1", ""),
    "x_d1": ("att1", ""),
    "c_g1": ("msg1", ""),
    "c_u1": ("msg1", ""),
    "c_d1": ("msg1", ""),
    "cj_g1": ("", ""),
    "cj_u1": ("", ""),
    "cj_d1": ("", ""),
    "xj_g1": ("", ""),
    "xj_u1": ("", ""),
    "xj_d1": ("", ""),
    "p_o1": ("slot0", ""),
    "xj_o1": ("", ""),
    "r_g1": ("sall1", "key1"),
    "p_q1": ("og0", ""),
    "xj_q1": ("", "key0"),
    "r_u1": ("og0", "ig0"),
    "r_d1": ("sall0", "cols0"),
    "cj_g0": ("", ""),
    "cj_u0": ("", ""),
    "cj_d0": ("", ""),
    "xj_g0": ("", ""),
    "xj_u0": ("", ""),
    "xj_d0": ("", ""),
    "p_o0": ("sall0", ""),
    "xj_o0": ("", ""),
    "rs": ("key0", ""),
    "r_u0": ("cols", "part0"),
    "r_d0": ("part", ""),
}


class Plan:
    def __init__(self, table):
        self.table, self.make, self.found, self.passed = table, {}, {}, {"": True}

    def add(self, name, build):
        self.make[name] = build
        if self.table[name][0] in self.passed:
            self.get(name)

    def get(self, name):
        if name not in self.found:
            self.found[name] = self.make[name](lambda x: x)
        return self.found[name]

    def point(self, at, value):
        done = []
        for name, (_, end) in self.table.items():
            if end == at and name in self.make:
                done += jax.tree.leaves(self.get(name))
        if done:
            value = after(value, *done)
        self.passed[at] = True
        for name, (start, _) in self.table.items():
            if start == at and name in self.make and name not in self.found:
                self.found[name] = self.make[name](lambda x: after(x, value))
        return value


def swap(x, axis):
    return lax.ppermute(x, axis, [(0, 1), (1, 0)])


def fold(x, axis, at):
    given = lax.dynamic_index_in_dim(x, 1 - at, 1, keepdims=False)
    kept = lax.dynamic_index_in_dim(x, at, 1, keepdims=False)
    return (kept.astype(f32) + swap(given, axis).astype(f32)).astype(bf16)


def gather_rows(x, axes, fillers=()):
    far, near, core = axes[:-2], axes[-2], axes[-1]
    count = 2 ** len(far)
    found = [x]
    for step in range(1, count):
        pairs = [(at, (at + step) % count) for at in range(count)]
        found.append(lax.ppermute(x, far, pairs))
    blocks, filled = [], []
    for step, block in enumerate(found):
        if 0 < step <= len(fillers):
            beside = [block] if step > 1 else [blocks[0]]
            filled.append(fillers[step - 1](*beside, *filled[-1:]))
            block = after(block, filled[-1])
        pair = jnp.concatenate([block, swap(block, near)], axis=0)
        blocks += [pair, swap(pair, core)]
    return (blocks, filled) if fillers else blocks


def gathered_order(axes):
    count = 2 ** (len(axes) - 2)
    me = lax.axis_index(axes)
    far, near, core = me // 4, me // 2 % 2, me % 2
    order = []
    for step in range(count):
        for other_core in range(2):
            for other_near in range(2):
                order.append(
                    (far - step) % count * 4 + (near ^ other_near) * 2 + (core ^ other_core)
                )
    return jnp.stack(order).astype(jnp.int32)


def shards(
    axes,
    tokens,
    prev_logits,
    routes,
    order,
    deal,
    w_qkv,
    w_out,
    w_gate,
    w_up,
    w_down,
    norm_attn,
    norm_moe,
    w_router,
    w_const,
    const_vec,
    grad_out,
):
    rows, width = tokens.shape[1], tokens.shape[2]
    ex_axes, sub_axes = axes[:3], axes[3:]
    every_axis = axes + (FS,)
    subs = 2 ** len(sub_axes)
    ctx_size = EXPERTS * subs
    length = rows * ctx_size
    prompt = length // 2
    cont_len = prompt // (ctx_size // 8)
    block_rows = rows // 2
    own_rows = w_qkv.shape[1]
    fs_at = lax.axis_index(FS)
    sub_at = lax.axis_index(sub_axes)


    def deal_out(x):
        return lax.all_to_all(x, ex_axes, 0, 0, tiled=True)

    def dispatch(x):
        return deal_out(x.reshape(EXPERTS, SLOTS, -1)).reshape(x.shape)

    def blank(count):
        return jnp.zeros((own_rows, count), bf16)

    def fetch_packed(layer, tie):
        mine = jnp.concatenate(
            [
                w_qkv[layer],
                w_out[layer],
                w_router[layer],
                blank(AT_CONST - ROUTED),
                w_const[layer],
                blank(AT_CVEC - AT_CONST - 4),
                const_vec[layer],
                blank(AT_ATTN - AT_CVEC - 2),
                norm_attn[layer][:, None],
                norm_moe[layer][:, None],
                blank(LANES - AT_MOE - 1),
            ],
            axis=1,
        )
        return lax.all_gather(tie(mine), every_axis, axis=0, tiled=True)

    by_chunks = subs == 2
    flags = jnp.stack([sub_at, fs_at]).astype(jnp.int32)[None, :]

    plan = Plan(TABLE)

    def add_weight(name, member):
        plan.add(
            "a_" + name,
            lambda tie: deal_out(tie(member)).reshape(-1, member.shape[-1]),
        )
        plan.add("x_" + name, lambda tie: swap(tie(plan.get("a_" + name)), FS))
        plan.add(
            "c_" + name,
            lambda tie: (
                swap(tie(plan.get("a_" + name)), sub_axes[0]),
                swap(plan.get("x_" + name), sub_axes[0]),
            ),
        )

    def weights_of(layer):
        found = []
        for name, member in zip("gud", (w_gate, w_up, w_down)):
            if by_chunks:
                parts = [plan.get(part + name + str(layer)) for part in ("a_", "x_", "c_")]
                found.append((parts[0], parts[1]) + parts[2])
            else:
                moved = deal_out(member[layer])
                whole = lax.all_gather(moved, sub_axes + (FS,), axis=1, tiled=True)
                found.append(whole.reshape(-1, whole.shape[2]))
        return found

    if not by_chunks:
        to_chunks = jnp.eye(width, dtype=bf16)
    else:
        place = jnp.arange(width, dtype=jnp.int32)
        chunk, inside = place // (width // 4), place % (width // 4)
        source = (
            inside // own_rows * 4 + (chunk ^ (sub_at * 2 + fs_at)).astype(jnp.int32)
        ) * own_rows + inside % own_rows
        to_chunks = (place[:, None] == source[None, :]).astype(bf16)

    tokens_all = gather_rows(tokens[0], axes)
    all_packed = [fetch_packed(0, lambda x: x)]
    block_order = gathered_order(axes)
    deal_pairs = deal.reshape(ctx_size, 2)
    own_blocks = jnp.sum(
        jnp.where(
            (block_order[:, None] == jnp.arange(ctx_size, dtype=jnp.int32)[None, :])[:, :, None],
            deal_pairs[None],
            0,
        ),
        axis=1,
    ).reshape(2 * ctx_size)
    all_places = (
        own_blocks[:, None] * block_rows + jnp.arange(block_rows, dtype=jnp.int32)[None, :]
    ).reshape(length)
    within = jnp.where(all_places < prompt, all_places, prompt + (all_places - prompt) % cont_len)
    all_starts = jnp.where(all_places < prompt, 0, all_places - (all_places - prompt) % cont_len)
    lane = jnp.arange(LANES, dtype=jnp.int32)
    half = HEAD_DIM // 2
    frequency = 10000.0 ** (-(lane % half).astype(f32) / half)
    angles = within.astype(f32)[:, None] * frequency[None, :]
    cosine = jnp.cos(angles)
    sine = jnp.sin(angles) * jnp.where(lane % HEAD_DIM < half, -1.0, 1.0)[None, :]
    own_cos, own_sin = cosine, sine
    own_places, own_starts = all_places[:rows, None], all_starts[:rows, None]
    place_line, start_line = all_places[None, :], all_starts[None, :]

    if by_chunks:
        for layer in range(LAYERS):
            for name, member in zip("gud", (w_gate, w_up, w_down)):
                member = member[layer]
                if (name, layer) == ("u", 0):
                    member = after(member, cosine, sine)
                add_weight(name + str(layer), member)
    first_things = [*tokens_all, cosine, sine]

    route_rows = routes[0]
    flat_routes = jnp.concatenate([route_rows[:, k] for k in range(TOP)])
    flat_order = jnp.concatenate([order[0].reshape(rows, TOP)[:, k] for k in range(TOP)])
    earlier = (flat_routes[None, :] == flat_routes[:, None]) & (
        flat_order[None, :] < flat_order[:, None]
    )
    slot = jnp.sum(earlier.astype(jnp.int32), axis=1)
    in_slot = (flat_routes < EXPERTS) & (slot < CAP)
    target = jnp.where(in_slot, flat_routes * SLOTS + slot, -1)
    slot_ids = jnp.arange(EXPERTS * SLOTS, dtype=jnp.int32)
    pair_slots = (target[:, None] == slot_ids[None, :]).astype(bf16)
    slot_pairs = (slot_ids[:, None] == target[None, :]).astype(bf16)
    slot_tokens = slot_pairs[:, :rows] + slot_pairs[:, rows:]
    token_slots = pair_slots[:rows] + pair_slots[rows:]
    picks = [(route_rows[:, k : k + 1] == lane[None, :]).astype(f32) for k in range(TOP)]
    head_of = (jnp.arange(width, dtype=jnp.int32)[:, None] // HEAD_DIM == lane[None, :]).astype(
        bf16
    )

    table = (rows, LANES)
    full = (rows, width)
    core_axis = sub_axes[0]

    def join_cores(kept, given, *wait):
        part = kept.astype(f32) + swap(after(given, *wait), core_axis).astype(f32)
        if part.ndim == 3:
            half = part.shape[1] // 2
            return part[:, :half].astype(bf16), part[:, half:].astype(bf16)
        half = part.shape[0] // 2
        return part[:half].astype(bf16), part[half:].astype(bf16)

    def join_groups(pieces, *wait):
        kept, given = pieces
        part = (kept.astype(f32) + swap(after(given, *wait), FS).astype(f32)).astype(bf16)
        return part.reshape(EXPERTS, -1, part.shape[-1])

    def reduce_rows(part):
        part = part.reshape(-1, part.shape[2])
        return lax.psum_scatter(part, ex_axes, scatter_dimension=0, tiled=True)

    def add_grads(layer, halves):
        for at, name in enumerate("gud"):
            name += str(layer)
            kept, given = halves[2 * at], halves[2 * at + 1]
            plan.add(
                "cj_" + name,
                lambda tie, kept=kept, given=given: join_cores(kept, tie(given)),
            )
            plan.add(
                "xj_" + name,
                lambda tie, name=name: join_groups(
                    (plan.get("cj_" + name)[0], tie(plan.get("cj_" + name)[1]))
                ),
            )
            if name == "u0":
                plan.add(
                    "r_u0",
                    lambda tie: deal_out(
                        tie(jnp.concatenate([plan.get("xj_g0"), plan.get("xj_u0")], axis=2))
                    ),
                )
            if name not in ("g0", "u0", "d0"):
                plan.add(
                    "r_" + name, lambda tie, name=name: deal_out(tie(plan.get("xj_" + name)))
                )

    def add_out(layer, attended, mid_low):
        name = "o" + str(layer)

        def product(tie):
            att_rel = dot_nn(attended.astype(bf16), to_chunks).astype(bf16)
            return join_cores(*weight_product(att_rel, tie(mid_low)))

        plan.add("p_" + name, product)
        plan.add(
            "xj_" + name,
            lambda tie: join_groups((plan.get("p_" + name)[0], tie(plan.get("p_" + name)[1]))),
        )
        if layer == 0:
            plan.add(
                "r_d0",
                lambda tie: deal_out(
                    tie(jnp.concatenate([plan.get("xj_d0"), plan.get("xj_o0")], axis=1))
                ),
            )

    def add_qkv(thin_part, normed, proj_grad):
        def product(tie):
            thin_low = dot_tn(to_chunks, thin_part.astype(bf16)).astype(bf16)
            normed_rel = dot_nn(normed, to_chunks).astype(bf16)
            return join_cores(*weight_product(normed_rel, tie(proj_grad), thin_low))

        plan.add("p_q1", product)
        plan.add(
            "xj_q1",
            lambda tie: join_groups((plan.get("p_q1")[0], tie(plan.get("p_q1")[1]))),
        )
        plan.add(
            "rs",
            lambda tie: reduce_rows(
                jnp.concatenate([plan.get("xj_o1"), tie(plan.get("xj_q1"))], axis=2)
            ),
        )

    def scatter_whole(member):
        cut = member.astype(bf16).reshape(EXPERTS, subs * 2, -1, member.shape[1])
        part = lax.psum_scatter(cut, sub_axes + (FS,), scatter_dimension=1, tiled=True)
        return part.reshape((EXPERTS,) + part.shape[2:])

    def expert_plain_back(x, out_grad, gate_act, upward, weights):
        wgate, wup, wdown = weights
        sigma = jax.nn.sigmoid(gate_act)
        gated = gate_act * sigma
        inner = (gated * upward).astype(bf16)
        inner_grad = dot_nt(out_grad, wdown)
        up_grad = (inner_grad * gated).astype(bf16)
        gate_grad = (inner_grad * upward * (sigma + gated * (1.0 - sigma))).astype(bf16)
        in_grad = (dot_nt(gate_grad, wgate) + dot_nt(up_grad, wup)).astype(bf16)
        products = (dot_tn(x, gate_grad), dot_tn(x, up_grad), dot_tn(inner, out_grad))
        return [scatter_whole(member) for member in products], in_grad

    def expert_plain(x, weights):
        wgate, wup, wdown = weights
        gate_act, upward = dot_nn(x, wgate), dot_nn(x, wup)
        inner = (jax.nn.silu(gate_act) * upward).astype(bf16)
        return gate_act, upward, dot_nn(inner, wdown).astype(bf16)

    hidden = tokens[0].astype(f32)
    previous = jnp.pad(prev_logits[0], ((0, 0), (0, LANES - ROUTED)))
    grad = grad_out[0]
    all_packed[0] = after(all_packed[0], *first_things, slot_tokens, previous)
    all_packed[0] = plan.point("packed0", all_packed[0])
    plan.add("k_1", lambda tie: fetch_packed(1, tie))
    saved_all = []
    for layer in range(LAYERS):
        final = layer == LAYERS - 1
        packed = all_packed[layer]
        if layer == 0:
            blocks = tokens_all
            normed_all = norm_rows(tokens_all, packed)
        else:
            normed = plan.point("norm1", normed)
            blocks = gather_rows(normed, axes)
            blocks[-1] = plan.point("ag1", blocks[-1])
            normed_all = None if by_chunks else jnp.concatenate(blocks, axis=0)
        projected = project(blocks, packed, cosine, sine, layer == 0)
        projected = plan.point("proj" + str(layer), projected)
        attended, totals = attend(projected, own_places, own_starts, place_line, prompt)
        attended = plan.point("att" + str(layer), attended)
        if layer == 0:
            all_packed.append(plan.get("k_1"))
        small = Block(packed, LANES, 4 * width // LANES)
        wout = Block(packed, width, 3)
        midway, logits, chances, mixing, slot_in = run_fused(
            functools.partial(to_expert_kernel, final),
            [attended, hidden, wout, small, previous, slot_tokens, to_chunks]
            + ([grad, picks[0], picks[1], slot_pairs] if final else []),
            [
                (full, f32),
                (table, f32),
                (table, f32),
                (table, f32),
                ((EXPERTS * SLOTS, (2 if final else 1) * width), bf16),
            ],
            6 * rows * width * width,
        )
        slot_in = plan.point("msg" + str(layer), slot_in)
        expert_in = dispatch(slot_in)
        expert_in = plan.point("ein" + str(layer), expert_in)
        weights = weights_of(layer)
        gate_act = upward = halves = None
        if by_chunks and final:
            halves, expert_out = run_expert_back(
                flags, (expert_in, expert_in), to_chunks, None, None, *weights
            )
        elif by_chunks:
            gate_act, upward, expert_out = run_expert(flags, expert_in, *weights)
        elif final:
            half_in, half_grad = expert_in[:, :width], expert_in[:, width:]
            gate_act, upward, expert_out = expert_plain(half_in, weights)
            halves, in_grad = expert_plain_back(half_in, half_grad, gate_act, upward, weights)
            expert_out = jnp.concatenate([in_grad, expert_out], axis=1)
        else:
            gate_act, upward, expert_out = expert_plain(expert_in, weights)
        if by_chunks and final:
            add_grads(1, halves)
        expert_out = plan.point("eout" + str(layer), expert_out)
        back = dispatch(expert_out)
        in_back = None
        if final:
            in_back, back = back[:, :width], back[:, width:]
        if not final:
            all_packed[1] = after(all_packed[1], expert_out)
            output, normed = run_fused(
                functools.partial(from_expert_kernel, False),
                [midway, chances, mixing, picks[0], picks[1], small, pair_slots, back]
                + [Block(all_packed[layer + 1], LANES, 4 * width // LANES)],
                [(full, f32), (full, bf16)],
                2 * rows * width * EXPERTS * SLOTS,
            )
        normed_own = None if layer == 0 else blocks[0][:rows]
        saved_all.append(
            (
                hidden,
                normed_own,
                normed_all,
                projected,
                attended,
                totals,
                midway,
                chances,
                mixing,
                expert_in,
                gate_act,
                upward,
                halves,
                in_back,
                weights,
                back,
            )
        )
        if not final:
            hidden = output
        previous = logits

    logit_next = jnp.zeros(table, f32)
    results = [None] * LAYERS
    moved_grads = [[None] * 3 for _ in range(LAYERS)]
    out_folded = [None] * LAYERS
    for layer in reversed(range(LAYERS)):
        final = layer == LAYERS - 1
        (
            hidden,
            normed,
            normed_all,
            projected,
            attended,
            totals,
            midway,
            chances,
            mixing,
            expert_in,
            gate_act,
            upward,
            halves,
            in_back,
            weights,
            back,
        ) = saved_all[layer]
        packed = all_packed[layer]
        small = Block(packed, LANES, 4 * width // LANES)
        wout = Block(packed, width, 3)
        if not final:
            slot_grad = plan.point("slot0", slot_grad)
            out_grad = dispatch(slot_grad)
            out_grad = plan.point("og0", out_grad)
            if by_chunks:
                halves, in_grad = run_expert_back(
                    flags, (expert_in, out_grad), to_chunks, gate_act, upward, *weights
                )
            else:
                halves, in_grad = expert_plain_back(
                    expert_in, out_grad, gate_act, upward, weights
                )
            if by_chunks:
                add_grads(0, halves)
            in_grad = plan.point("ig0", in_grad)
            in_back = dispatch(in_grad)
            in_back = plan.point("ib0", in_back)

        mid_grad, mid_low, sent, delta, logit_next, thin_w, line_grads = run_fused(
            to_attention_kernel,
            [grad, midway, chances, mixing, picks[0], picks[1], small, pair_slots]
            + [token_slots, back, in_back, logit_next, wout, attended, totals, head_of],
            [
                (full, f32),
                (full, bf16),
                ((rows, width + LANES), bf16),
                (table, f32),
                (table, f32),
                ((width, LANES), f32),
                ((8, width), f32),
            ],
            6 * rows * width * width,
        )
        def some_queries(start, *things):
            return query_back(
                start,
                2,
                after(projected, *things),
                sent,
                totals,
                delta,
                own_places,
                own_starts,
                place_line,
                own_cos,
                own_sin,
                prompt,
            )

        sent = plan.point("sent" + str(layer), sent)
        if final:
            (output_rows,) = run_fused(
                functools.partial(from_expert_kernel, True),
                [midway, chances, mixing, picks[0], picks[1], small, pair_slots]
                + [after(back, sent)],
                [(full, bf16)],
                2 * rows * width * EXPERTS * SLOTS,
            )
        sent_all, query_grads = gather_rows(
            sent, axes, [functools.partial(some_queries, start) for start in range(0, PAIRS, 2)]
        )
        if by_chunks:
            add_out(layer, attended, mid_low)
        else:
            out_w_grad = dot_tn(attended.astype(bf16), mid_low).astype(bf16)
        sent_all[-1] = plan.point("sall" + str(layer), sent_all[-1])
        key_grad, value_grad = key_back(
            projected,
            sent_all,
            own_places,
            place_line,
            start_line,
            own_cos,
            own_sin,
            prompt,
        )
        key_grad = plan.point("key" + str(layer), key_grad)
        proj_grad = jnp.concatenate([*query_grads, key_grad, value_grad], axis=1)
        before = []
        if layer > 0:
            before = [saved_all[layer - 1][7], picks[0], picks[1], slot_pairs]
        grad, gain_grads, *slot_grad = run_fused(
            functools.partial(from_attention_kernel, layer == 0),
            [*query_grads, key_grad, value_grad]
            + [Block(packed, width, at) for at in range(3)]
            + [hidden, small, mid_grad]
            + before,
            [(full, f32), ((8, width), f32)]
            + ([((EXPERTS * SLOTS, width), bf16)] if layer > 0 else []),
            6 * rows * width * width,
        )
        slot_grad = slot_grad[0] if slot_grad else None
        some = jnp.concatenate([gain_grads[:1], line_grads[:3]], axis=0)
        wanted = jnp.array([AT_ATTN, AT_MOE, AT_CVEC, AT_CVEC + 1], dtype=jnp.int32)
        spread_out = (wanted[:, None] == lane[None, :]).astype(f32)
        thin_part = thin_w + jnp.dot(some.T, spread_out, precision=highest)
        if by_chunks and final:
            add_qkv(thin_part, normed, proj_grad)
            continue
        share_of = 3 * width // ctx_size
        columns = proj_grad.reshape(rows, ctx_size, share_of).transpose(1, 0, 2)
        columns = plan.point("cols0", columns)
        columns = lax.all_to_all(columns, axes, 0, 0, tiled=True)
        columns = plan.point("cols", columns)
        columns = jnp.take(columns, block_order, axis=0).reshape(length, share_of)
        part = jnp.concatenate([dot_tn(columns, normed_all).T, thin_part], axis=1).astype(bf16)
        part = fold(part.reshape(ctx_size, 2, own_rows, share_of + LANES), FS, fs_at)
        part = plan.point("part0", part)
        part = lax.all_to_all(part, axes, 0, 0, tiled=True)
        part = plan.point("part", part)
        if by_chunks:
            last = plan.get("r_d0")
            tall = plan.get("xj_d0").shape[1]
            both = plan.get("r_u0")
            wide = both.shape[2] // 2
            moved_grads[0] = [both[:, :, :wide], both[:, :, wide:], last[:, :tall]]
            moved_grads[1] = [plan.get("r_" + name + "1") for name in "gud"]
            last_out = last[:, tall:]
        part = part.astype(f32)
        qkv_owned = part[:, :, :share_of].transpose(1, 0, 2).reshape(own_rows, 3 * width)
        thin_owned = jnp.sum(part[:, :, share_of:], axis=0)
        if by_chunks:
            out_owned = jnp.sum(last_out.astype(f32), axis=0)
        else:
            moved_grads[layer] = [deal_out(part) for part in halves]
            out_owned = lax.psum_scatter(
                out_w_grad, every_axis, scatter_dimension=0, tiled=True
            ).astype(f32)
        results[layer] = (qkv_owned, out_owned, thin_owned)
    if by_chunks:
        owned = after(plan.get("rs"), last).astype(f32)
        results[1] = (owned[:, width : 4 * width], owned[:, :width], owned[:, 4 * width :])

    def stack(parts):
        return jnp.stack(parts)

    thin_all = [results[layer][2] for layer in range(LAYERS)]
    return (
        output_rows[None],
        grad[None],
        stack([results[layer][0] for layer in range(LAYERS)]),
        stack([results[layer][1] for layer in range(LAYERS)]),
        stack([moved_grads[layer][0].astype(f32) for layer in range(LAYERS)]),
        stack([moved_grads[layer][1].astype(f32) for layer in range(LAYERS)]),
        stack([moved_grads[layer][2].astype(f32) for layer in range(LAYERS)]),
        stack([thin[:, AT_ATTN] for thin in thin_all]),
        stack([thin[:, AT_MOE] for thin in thin_all]),
        stack([thin[:, :ROUTED] for thin in thin_all]),
        stack([thin[:, AT_CONST : AT_CONST + 4] for thin in thin_all]),
        stack([thin[:, AT_CVEC : AT_CVEC + 2] for thin in thin_all]),
    )


def solution(mesh):
    devices = mesh.devices
    axes = ctx_axes(devices.shape[0])
    every_axis = axes + (FS,)
    finer = Mesh(devices.reshape((2,) * len(axes) + (devices.shape[1],)), every_axis)
    token_spec = P(FS, axes, None)
    row_spec = P(None, every_axis, None)
    expert_spec = P(None, None, every_axis, None)
    gain_spec = P(None, every_axis)
    return jax.shard_map(
        functools.partial(shards, axes),
        mesh=finer,
        in_specs=(
            token_spec,
            token_spec,
            token_spec,
            P(FS, axes),
            P(),
            row_spec,
            row_spec,
            expert_spec,
            expert_spec,
            expert_spec,
            gain_spec,
            gain_spec,
            row_spec,
            row_spec,
            row_spec,
            token_spec,
        ),
        out_specs=(
            token_spec,
            token_spec,
            row_spec,
            row_spec,
            expert_spec,
            expert_spec,
            expert_spec,
            gain_spec,
            gain_spec,
            row_spec,
            row_spec,
            row_spec,
        ),
        check_vma=False,
    )
```
